128 devices in a mesh: section: 2 (over core), shard: 8 (over y_lo, x), context: 4 (over z), tensor: 2 (over y_hi).
Axes of the slice: x: 4, y: 4 (y_hi: 2, y_lo: 2; y = y_hi * 2 + y_lo), z: 4, core: 2. Of those that a mesh axis runs over, the one named last changes fastest.
Arguments:
- block_input: bfloat16 [2, 8, 1024, 768], P(None, 'shard', ('context', 'tensor')), may hold values from -36 to 36
- cotangent: bfloat16 [2, 8, 1024, 768], P(None, 'shard', ('context', 'tensor')), may hold values from -6 to 6
- segment_ids: int32 [2, 8, 1024], P(None, 'shard'), may hold values from 0 to 7, as said below
- w_qkv: bfloat16 [2, 768, 2304], P('section', 'shard'), may hold values from -0.21875 to 0.21875
- w_out: bfloat16 [2, 768, 768], P('section', 'shard'), may hold values from -1.75 to 1.75
- w_fc: bfloat16 [2, 768, 3072], P('section', 'shard', 'tensor'), may hold values from -0.21875 to 0.21875
- w_proj: bfloat16 [2, 3072, 768], P('section', 'tensor', 'shard'), may hold values from -0.109375 to 0.109375
- norm_gains: bfloat16 [2, 2, 768], P('section', None, 'shard'), may hold values from 0.25 to 1.75
- norm_biases: bfloat16 [2, 2, 768], P('section', None, 'shard'), may hold values from -3 to 3
Outputs:
- block_outputs: bfloat16 [2, 2, 8, 1024, 768], P('section', None, 'shard', ('context', 'tensor'))
- input_grads: bfloat16 [2, 2, 8, 1024, 768], P('section', None, 'shard', ('context', 'tensor'))
- grad_qkv: float32 [2, 768, 2304], P('section', 'shard')
- grad_out: float32 [2, 768, 768], P('section', 'shard')
- grad_fc: float32 [2, 768, 3072], P('section', 'shard', 'tensor')
- grad_proj: float32 [2, 3072, 768], P('section', 'tensor', 'shard')
- grad_gains: float32 [2, 2, 768], P('section', None, 'shard')
- grad_bias_attention: float32 [2, 768], P('section', 'shard')
- grad_bias_feedforward: float32 [2, 768], P('section', 'shard')
The draws below stay inside these ranges and needn't reach their ends.
Inputs may be any that keep to these rules, and one draw needn't show every extreme that they name: `segment_ids`: along each sequence the ids start at 0 and never fall; in each group of 2 sequences of one index of the second dimension, one sequence drawn from the seed is a single document.
All inputs are finite; a program needn't handle non-finite values.
Results may differ from the reference program's by a relative error of at most 0.03.
Values may be sent and summed in bfloat16 or wider, within the bound.
A program may use at most 192 MiB of HBM per device.

```python
import math
import jax
import jax.numpy as jnp
from jax import lax

HEAD_DIM = 64
D = 768
FF = 3072
LENGTH = 1024
MICRO = 2
SEQS = 8


def draw_block_input(key, part):
    key = jax.random.fold_in(key, 11)
    key_base, key_rows, key_cols = jax.random.split(key, 3)
    shape = (MICRO, SEQS, LENGTH, D)
    base = jnp.clip(jax.random.normal(key_base, shape, jnp.float32), -4.0, 4.0)
    row_scale = jnp.exp(jax.random.uniform(key_rows, (MICRO, SEQS, LENGTH, 1), jnp.float32, math.log(0.3), math.log(3.0)))
    col_scale = jnp.exp(jax.random.uniform(key_cols, (D,), jnp.float32, math.log(0.3), math.log(3.0)))
    return (base * row_scale * col_scale).astype(jnp.bfloat16)


def draw_segment_ids(key, part):
    key = jax.random.fold_in(key, 23)
    key_marks, key_keep, key_whole = jax.random.split(key, 3)
    spacing = LENGTH // 8
    jitter = max(1, LENGTH // 32)
    marks = jnp.arange(1, 8, dtype=jnp.int32) * spacing + jax.random.randint(key_marks, (MICRO, SEQS, 7), -jitter, jitter + 1)
    keep_mark = jax.random.randint(key_keep, (MICRO, SEQS, 7), 0, 2)
    whole_one = jax.random.randint(key_whole, (1, SEQS, 1), 0, MICRO)
    full_one = (whole_one + 1) % MICRO
    micro_idx = jnp.arange(MICRO, dtype=jnp.int32)[:, None, None]
    keep_mark = jnp.where(micro_idx == full_one, 1, keep_mark)
    keep_mark = jnp.where(micro_idx == whole_one, 0, keep_mark)
    positions = jnp.arange(LENGTH, dtype=jnp.int32)
    passed = (positions[None, None, :, None] >= marks[:, :, None, :]).astype(jnp.int32)
    return jnp.sum(passed * keep_mark[:, :, None, :], -1).astype(jnp.int32)


def level_of(rng, shape, pieces, least, top_value):
    gain = 1.0
    for axis_at, blocks in pieces:
        draws = jax.random.uniform(jax.random.fold_in(jax.random.fold_in(rng, 6), axis_at), (blocks,), jnp.float32, least / len(pieces), top_value / len(pieces))
        gain = gain * jnp.repeat(jnp.exp(draws), shape[axis_at] // blocks).reshape((-1,) + (1,) * (len(shape) - 1 - axis_at))
    return gain


def gaussian(stream_key, dims, width, bound, pieces=(), kind=jnp.bfloat16):
    gain = level_of(stream_key, dims, pieces, -0.22, 0.18) if pieces else 1.0
    drawn = jax.random.normal(stream_key, dims, jnp.float32) * width * gain
    return jnp.minimum(jnp.maximum(drawn, -bound), bound).astype(kind)


def setup_inputs(seed: int = 0) -> dict:
    key_of = jax.random.split(jax.random.key(seed), 10)
    block_input = draw_block_input(jax.random.fold_in(key_of[9], 71), 0)
    cotangent = gaussian(key_of[1], (MICRO, SEQS, LENGTH, D), 1.0, 6.0, ((1, 8), (2, 8)))
    segment_ids = draw_segment_ids(jax.random.fold_in(key_of[9], 71), 0)
    w_qkv = gaussian(key_of[3], (2, D, 3 * D), D ** -0.5, 0.21875, ((0, 2), (1, 8)))
    w_out = gaussian(key_of[4], (2, D, D), (max(1, D // 64)) ** -0.5, 1.75, ((0, 2), (1, 8)))
    w_fc = gaussian(key_of[5], (2, D, FF), D ** -0.5, 0.21875, ((0, 2), (1, 8), (2, 2)))
    w_proj = gaussian(key_of[6], (2, FF, D), FF ** -0.5, 0.109375, ((0, 2), (1, 2), (2, 8)))
    norm_gains = jnp.clip(1.0 + 0.15 * jax.random.normal(key_of[7], (2, 2, D), jnp.float32), 0.25, 1.75).astype(jnp.bfloat16)
    norm_biases = gaussian(key_of[8], (2, 2, D), 0.5, 3.0, ((0, 2), (2, 8)))
    return {"block_input": block_input, "cotangent": cotangent, "segment_ids": segment_ids, "w_qkv": w_qkv, "w_out": w_out, "w_fc": w_fc, "w_proj": w_proj, "norm_gains": norm_gains, "norm_biases": norm_biases}


@jax.custom_vjp
def low(v):
    return lax.optimization_barrier(v.astype(jnp.bfloat16)).astype(jnp.float32)

@jax.custom_vjp
def low_back(v):
    return v

def low_keep(v):
    return (low(v), None)

def low_pass(kept, grad):
    return (grad,)

def back_keep(v):
    return (v, None)

def back_low(kept, grad):
    return (low(grad),)
low.defvjp(low_keep, low_pass)
low_back.defvjp(back_keep, back_low)
EPSILON = 1e-05
MASKED = -1000000000.0
HIGHEST = lax.Precision.HIGHEST

def layer_norm(values, gain_vec, bias_vec):
    row_mean = lax.optimization_barrier(jnp.mean(values, -1, keepdims=True))
    centred = values - row_mean
    variance = lax.optimization_barrier(jnp.mean(centred * centred, -1, keepdims=True))
    return centred * lax.rsqrt(variance + EPSILON) * gain_vec + bias_vec

def sequence_block(inputs, seg_row, qkv_full, out_full, fc_full, proj_full, gain_full, bias_full):
    seq_length, feat_width = inputs.shape
    head_count = feat_width // HEAD_DIM
    score_scale = 1.0 / math.sqrt(HEAD_DIM)
    normed = low(layer_norm(inputs, gain_full[0], bias_full[0]))
    projected = low_back(low(jnp.dot(normed, qkv_full, precision=HIGHEST)))
    shaped = projected.reshape(seq_length, 3, head_count, HEAD_DIM)
    query = shaped[:, 0]
    keys = shaped[:, 1]
    values = shaped[:, 2]
    scores = low_back(jnp.einsum('qhd,khd->hqk', query, keys, precision=HIGHEST) * score_scale)
    positions = jnp.arange(seq_length)
    allowed = (positions[None, :] <= positions[:, None]) & (seg_row[None, :] == seg_row[:, None])
    masked = jnp.where(allowed[None], scores, MASKED)
    totals = jax.nn.logsumexp(masked, axis=-1, keepdims=True)
    probs = low(jnp.exp(masked - totals))
    mixed = jnp.einsum('hqk,khd->qhd', probs, values, precision=HIGHEST).reshape(seq_length, feat_width)
    mixed = low_back(low(mixed))
    resid = inputs + low_back(jnp.dot(mixed, out_full, precision=HIGHEST))
    inner = low(layer_norm(resid, gain_full[1], bias_full[1]))
    upward = low_back(jnp.dot(inner, fc_full, precision=HIGHEST))
    active = low(jax.nn.gelu(upward, approximate=True))
    return resid + low_back(jnp.dot(active, proj_full, precision=HIGHEST))

def reference(block_input, cotangent, segment_ids, w_qkv, w_out, w_fc, w_proj, norm_gains, norm_biases):
    seq_count = MICRO * SEQS
    inputs = block_input.astype(jnp.float32).reshape(seq_count, LENGTH, D)
    upstream = cotangent.astype(jnp.float32).reshape(seq_count, LENGTH, D)
    seg_rows = segment_ids.reshape(seq_count, LENGTH)

    def run_block(entry, *weights):

        def one_sequence(paired):
            return jax.checkpoint(sequence_block)(paired[0], paired[1], *weights)
        return lax.map(one_sequence, (entry, seg_rows))

    def weights_of(index):
        return tuple((member[index].astype(jnp.float32) for member in (w_qkv, w_out, w_fc, w_proj, norm_gains, norm_biases)))
    first, pull_first = jax.vjp(run_block, inputs, *weights_of(0))
    middle = low(first)
    last, pull_last = jax.vjp(run_block, middle, *weights_of(1))
    grads_last = pull_last(upstream)
    middle_grad = low(grads_last[0])
    grads_first = pull_first(middle_grad)
    full_shape = (2, MICRO, SEQS, LENGTH, D)
    block_outputs = jnp.stack([first, last]).astype(jnp.bfloat16).reshape(full_shape)
    input_grads = jnp.stack([grads_first[0], middle_grad]).astype(jnp.bfloat16).reshape(full_shape)
    stacked = [jnp.stack([grads_first[position], grads_last[position]]) for position in range(1, 7)]
    bias_stack = stacked[5]
    return (block_outputs, input_grads, stacked[0], stacked[1], stacked[2], stacked[3], stacked[4], bias_stack[:, 0], bias_stack[:, 1])
```

```python
import functools
import math

import jax
import jax.numpy as jnp
from jax import lax
from jax.experimental import pallas as pl
from jax.experimental.pallas import tpu as pltpu
from jax.sharding import PartitionSpec as P

HEAD_DIM = 64
EPSILON = 1e-05
MASKED = -1000000000.0
MESH = pl.DeviceIdType.MESH
BF16 = jnp.bfloat16
F32 = jnp.float32
ANY = pl.BlockSpec(memory_space=pl.ANY)
VMEM = pl.BlockSpec(memory_space=pltpu.VMEM)


class Copies:
    def __init__(self, send_sems, recv_sems):
        self.send_sems, self.recv_sems, self.made = send_sems, recv_sems, []

    def push(self, src, dst, device_id):
        index = len(self.made)
        copy = pltpu.make_async_remote_copy(
            src_ref=src,
            dst_ref=dst,
            send_sem=self.send_sems.at[index],
            recv_sem=self.recv_sems.at[index],
            device_id=device_id,
            device_id_type=MESH,
        )
        copy.start()
        self.made.append(copy)
        return copy

    def finish(self):
        for copy in self.made:
            copy.wait_send()


def greet(peers):
    barrier = pltpu.get_barrier_semaphore()
    for peer in peers:
        pl.semaphore_signal(barrier, inc=1, device_id=peer, device_id_type=MESH)
    pl.semaphore_wait(barrier, len(peers))


def call_remote(body, out_shape, copies, collective_id, args, scratch=(), locals_=1, specs=None, vmem=None):
    in_specs, out_specs = specs if specs else ([ANY] * len(args), jax.tree.map(lambda _: ANY, out_shape))
    return pl.pallas_call(
        body,
        out_shape=out_shape,
        in_specs=in_specs,
        out_specs=out_specs,
        scratch_shapes=[
            *scratch,
            pltpu.SemaphoreType.DMA((copies,)),
            pltpu.SemaphoreType.DMA((copies,)),
            pltpu.SemaphoreType.DMA((locals_,)),
        ],
        compiler_params=pltpu.CompilerParams(
            collective_id=collective_id, has_side_effects=True, vmem_limit_bytes=vmem
        ),
    )(*args)


def place():
    shard = lax.axis_index("shard")
    return lax.axis_index("section"), shard // 4, lax.rem(shard, 4)


AG_COPIES = 64


def weights_body(split, own_ref, all_ref, send_sems, recv_sems, local_sems):
    section, row, col = place()
    columns = own_ref.shape[1]
    right, left, far = lax.rem(col + 1, 4), lax.rem(col + 3, 4), lax.rem(col + 2, 4)
    to_right = {"shard": row * 4 + right}
    to_left = {"shard": row * 4 + left}
    other = 1 - row
    to_row = {"shard": other * 4 + col}
    to_core = {"section": 1 - section}
    greet([to_right, to_left, to_row, to_core])
    copies = Copies(send_sems, recv_sems)
    parts = (pl.ds(0, split), pl.ds(split, columns - split))
    half = own_ref.shape[0] // 2
    rows = (pl.ds(0, half), pl.ds(half, half))

    def slot(a_row, a_col, part, which=None):
        shard = a_row * 4 + a_col
        if which is None:
            return all_ref.at[section, shard, :, parts[part]]
        return all_ref.at[section, shard, rows[which], parts[part]]

    own_a, own_b = own_ref.at[:, parts[0]], own_ref.at[:, parts[1]]
    b_row = copies.push(own_b, slot(row, col, 1), to_row)
    a_right = copies.push(own_a, slot(row, col, 0), to_right)
    a_left = copies.push(own_a, slot(row, col, 0), to_left)
    a_row = copies.push(own_a, slot(row, col, 0), to_row)
    b_right = copies.push(own_b, slot(row, col, 1), to_right)
    b_left = copies.push(own_b, slot(row, col, 1), to_left)
    c_own = copies.push(own_ref, all_ref.at[section, row * 4 + col], to_core)
    mine = pltpu.make_async_copy(own_ref, all_ref.at[section, row * 4 + col], local_sems.at[0])
    mine.start()
    cores = [c_own]

    def share(ref):
        cores.append(copies.push(ref, ref, to_core))

    a_right.wait_recv()
    ref = slot(row, left, 0)
    a_far_right = copies.push(slot(row, left, 0, 0), slot(row, left, 0, 0), to_right)
    a_row_left = copies.push(ref, ref, to_row)
    a_left.wait_recv()
    ref2 = slot(row, right, 0)
    a_far_left = copies.push(slot(row, right, 0, 1), slot(row, right, 0, 1), to_left)
    a_row_right = copies.push(ref2, ref2, to_row)
    b_row.wait_recv()
    ref3 = slot(other, col, 1)
    b_or = copies.push(ref3, ref3, to_right)
    b_ol = copies.push(ref3, ref3, to_left)
    share(ref)
    share(ref2)
    share(ref3)
    a_far_right.wait_recv()
    a_far_left.wait_recv()
    ref = slot(row, far, 0)
    a_row_far = copies.push(ref, ref, to_row)
    share(ref)
    b_right.wait_recv()
    b_far_right = copies.push(slot(row, left, 1, 0), slot(row, left, 1, 0), to_right)
    share(slot(row, left, 1))
    b_left.wait_recv()
    b_far_left = copies.push(slot(row, right, 1, 1), slot(row, right, 1, 1), to_left)
    share(slot(row, right, 1))
    a_row.wait_recv()
    share(slot(other, col, 0))
    b_or.wait_recv()
    bo_far_right = copies.push(slot(other, left, 1, 0), slot(other, left, 1, 0), to_right)
    share(slot(other, left, 1))
    b_ol.wait_recv()
    bo_far_left = copies.push(slot(other, right, 1, 1), slot(other, right, 1, 1), to_left)
    share(slot(other, right, 1))
    a_row_left.wait_recv()
    share(slot(other, left, 0))
    a_row_right.wait_recv()
    share(slot(other, right, 0))
    b_far_right.wait_recv()
    b_far_left.wait_recv()
    share(slot(row, far, 1))
    a_row_far.wait_recv()
    share(slot(other, far, 0))
    bo_far_right.wait_recv()
    bo_far_left.wait_recv()
    share(slot(other, far, 1))
    for copy in cores:
        copy.wait_recv()
    copies.finish()
    mine.wait()


def gather_weights(own):
    depth, columns = own.shape
    return call_remote(
        functools.partial(weights_body, 2688),
        jax.ShapeDtypeStruct((2, 8, depth, columns), own.dtype),
        AG_COPIES,
        0,
        (own,),
    )


def span_peers():
    context, tensor = lax.axis_index("context"), lax.axis_index("tensor")
    span = context * 2 + tensor
    peers = []
    for step in range(1, 8):
        peer = lax.rem(span + step, 8)
        peers.append((peer, peer // 2, lax.rem(peer, 2)))
    return context, tensor, span, peers


def heads_body(by_span, q_ref, kv_ref, q_out, kv_out, send_sems, recv_sems, local_sems):
    context, tensor, span, peers = span_peers()
    greet([{"context": c, "tensor": t} for _, c, t in peers])
    copies = Copies(send_sems, recv_sems)
    for peer, c, t in peers:
        copies.push(
            kv_ref.at[peer if by_span else c], kv_out.at[span], {"context": c, "tensor": t}
        )
    for step in range(1, 4):
        c = lax.rem(context + step, 4)
        copies.push(q_ref.at[c], q_out.at[context], {"context": c})
    own = [
        pltpu.make_async_copy(q_ref.at[context], q_out.at[context], local_sems.at[0]),
        pltpu.make_async_copy(
            kv_ref.at[span if by_span else context], kv_out.at[span], local_sems.at[1]
        ),
    ]
    for copy in own:
        copy.start()
    for copy in copies.made:
        copy.wait_recv()
    copies.finish()
    for copy in own:
        copy.wait()


def exchange_heads(q_parts, kv_parts, by_span):
    return call_remote(
        functools.partial(heads_body, by_span),
        (
            jax.ShapeDtypeStruct(q_parts.shape, q_parts.dtype),
            jax.ShapeDtypeStruct((8, *kv_parts.shape[1:]), kv_parts.dtype),
        ),
        10,
        1 if by_span else 2,
        (q_parts, kv_parts),
        locals_=2,
    )


def context_body(in_ref, out_ref, send_sems, recv_sems, local_sems):
    context = lax.axis_index("context")
    peers = [lax.rem(context + step, 4) for step in range(1, 4)]
    greet([{"context": c} for c in peers])
    copies = Copies(send_sems, recv_sems)
    for c in peers:
        copies.push(in_ref.at[c], out_ref.at[context], {"context": c})
    own = pltpu.make_async_copy(in_ref.at[context], out_ref.at[context], local_sems.at[0])
    own.start()
    for copy in copies.made:
        copy.wait_recv()
    copies.finish()
    own.wait()


def exchange_context(parts):
    return call_remote(
        context_body, jax.ShapeDtypeStruct(parts.shape, parts.dtype), 3, 3, (parts,)
    )


def pair_body(in_ref, out_ref, send_sems, recv_sems, local_sems):
    peer = {"tensor": 1 - lax.axis_index("tensor")}
    greet([peer])
    copies = Copies(send_sems, recv_sems)
    copies.push(in_ref, out_ref, peer)
    copies.made[0].wait_recv()
    copies.finish()


def exchange_pair(rows):
    return call_remote(pair_body, jax.ShapeDtypeStruct(rows.shape, rows.dtype), 1, 4, (rows,))


BLOCK = 16


def add_rows(dst, terms, rows, cast=BF16):
    def step(index, _):
        at = pl.ds(pl.multiple_of(index * BLOCK, BLOCK), BLOCK)
        total = terms[0][at, :].astype(F32)
        for term in terms[1:]:
            total = total + term[at, :].astype(F32)
        dst[at, :] = total.astype(cast)
        return 0

    lax.fori_loop(0, rows // BLOCK, step, 0)


def grads_body(
    ga, gb, gn, out_a, out_b, out_n, a1, a2, a3, b1, b2, b3, n1, n2, za, zb, fa, fb,
    send_sems, recv_sems, local_sems,
):
    _, row, col = place()
    other = 1 - row
    right, left, far = lax.rem(col + 1, 4), lax.rem(col + 3, 4), lax.rem(col + 2, 4)
    to_right = {"shard": row * 4 + right}
    to_left = {"shard": row * 4 + left}
    to_row = {"shard": other * 4 + col}
    shard = row * 4 + col
    context, tensor, span, spans = span_peers()
    shard_peers = [lax.rem(shard + step, 8) for step in range(1, 8)]
    greet(
        [{"shard": peer} for peer in shard_peers]
        + [{"context": c, "tensor": t} for _, c, t in spans]
    )
    copies = Copies(send_sems, recv_sems)
    depth, width = ga.shape[1], ga.shape[2]
    half = depth // 2
    lower, upper = pl.ds(0, half), pl.ds(half, half)

    a_far_r = copies.push(ga.at[far], a1.at[0], to_right)
    a_far_l = copies.push(ga.at[4 + far], a1.at[1], to_left)
    b_far = copies.push(gb.at[other * 4 + far], b1.at[0], to_row)
    b_right = copies.push(gb.at[other * 4 + right], b1.at[1], to_row)
    b_left = copies.push(gb.at[other * 4 + left], b1.at[2], to_row)
    b_own = copies.push(gb.at[other * 4 + col], b1.at[3], to_row)
    a_plain_r = copies.push(ga.at[4 + right], a2.at[1], to_right)
    a_plain_l = copies.push(ga.at[left], a3.at[0], to_left)
    norms = [copies.push(gn.at[peer], n1.at[shard], {"shard": peer}) for peer in shard_peers]

    a_far_r.wait_recv()
    add_rows(a1.at[0], [a1.at[0], ga.at[right]], depth)
    a_sum_r = copies.push(a1.at[0], a2.at[0], to_right)
    a_far_l.wait_recv()
    add_rows(a1.at[1], [a1.at[1], ga.at[4 + left]], depth)
    a_sum_l = copies.push(a1.at[1], a3.at[1], to_left)

    b_far.wait_recv()
    add_rows(b1.at[0], [b1.at[0], gb.at[row * 4 + far]], depth)
    b_far_r = copies.push(b1.at[0, lower], b2.at[0], to_right)
    b_far_l = copies.push(b1.at[0, upper], b2.at[1], to_left)
    b_right.wait_recv()
    add_rows(b1.at[1], [b1.at[1], gb.at[row * 4 + right]], depth)
    b_left.wait_recv()
    add_rows(b1.at[2], [b1.at[2], gb.at[row * 4 + left]], depth)

    a_plain_r.wait_recv()
    a_plain_l.wait_recv()
    a_sum_r.wait_recv()
    a_sum_l.wait_recv()
    add_rows(a2.at[other], [a2.at[other], a3.at[other], ga.at[other * 4 + col]], depth)
    a_row = copies.push(a2.at[other], a2.at[2], to_row)
    add_rows(a2.at[row], [a2.at[row], a3.at[row], ga.at[row * 4 + col]], depth)

    b_far_r.wait_recv()
    add_rows(b1.at[1, lower], [b1.at[1, lower], b2.at[0]], half)
    b_sum_r = copies.push(b1.at[1], b3.at[0], to_right)
    b_far_l.wait_recv()
    add_rows(b1.at[2, upper], [b1.at[2, upper], b2.at[1]], half)
    b_sum_l = copies.push(b1.at[2], b3.at[1], to_left)

    n1[shard] = gn[shard]
    for copy in norms:
        copy.wait_recv()
    n2[span] = jnp.sum(n1[...], axis=0)
    norms2 = [
        copies.push(n2.at[span], n2.at[span], {"context": c, "tensor": t}) for _, c, t in spans
    ]

    a_row.wait_recv()
    wide = width // 8
    a_own = a2.at[row]
    add_rows(a_own, [a_own, a2.at[2]], depth)
    a_piece = [
        copies.push(
            a_own.at[:, pl.ds(pl.multiple_of(peer * wide, 128), wide)],
            za.at[span],
            {"context": c, "tensor": t},
        )
        for peer, c, t in spans
    ]
    b_own.wait_recv()
    b_sum_r.wait_recv()
    b_sum_l.wait_recv()
    add_rows(
        b1.at[3], [b1.at[3], gb.at[row * 4 + col], b3.at[0], b3.at[1]], depth
    )
    wide_b = width // 4
    contexts = [lax.rem(context + step, 4) for step in range(1, 4)]
    b_piece = [
        copies.push(
            b1.at[3, :, pl.ds(pl.multiple_of(c * wide_b, 128), wide_b)],
            zb.at[context],
            {"context": c},
        )
        for c in contexts
    ]
    za[span] = a_own[:, pl.ds(pl.multiple_of(span * wide, 128), wide)]
    zb[context] = b1[3, :, pl.ds(pl.multiple_of(context * wide_b, 128), wide_b)]
    for copy in a_piece:
        copy.wait_recv()
    add_rows(fa.at[span], [za.at[index] for index in range(8)], depth)
    a_back = [
        copies.push(fa.at[span], fa.at[span], {"context": c, "tensor": t}) for _, c, t in spans
    ]
    for copy in b_piece:
        copy.wait_recv()
    add_rows(fb.at[context], [zb.at[index] for index in range(4)], depth)
    b_back = [copies.push(fb.at[context], fb.at[context], {"context": c}) for c in contexts]
    for copy in norms2:
        copy.wait_recv()
    out_n[...] = jnp.sum(n2[...], axis=0)
    for copy in a_back:
        copy.wait_recv()
    for index in range(8):
        out_a[:, index * wide : (index + 1) * wide] = fa[index].astype(F32)
    for copy in b_back:
        copy.wait_recv()
    for index in range(4):
        out_b[:, index * wide_b : (index + 1) * wide_b] = fb[index].astype(F32)
    copies.finish()


def reduce_grads(ga, gb, gn):
    _, depth, width = ga.shape
    half = depth // 2
    return call_remote(
        grads_body,
        (
            jax.ShapeDtypeStruct((depth, width), F32),
            jax.ShapeDtypeStruct((depth, width), F32),
            jax.ShapeDtypeStruct(gn.shape[1:], F32),
        ),
        64,
        5,
        (ga, gb, gn),
        scratch=[
            pltpu.VMEM((2, depth, width), BF16),
            pltpu.VMEM((3, depth, width), BF16),
            pltpu.VMEM((2, depth, width), BF16),
            pltpu.VMEM((4, depth, width), BF16),
            pltpu.VMEM((2, half, width), BF16),
            pltpu.VMEM((2, depth, width), BF16),
            pltpu.VMEM(gn.shape, F32),
            pltpu.VMEM(gn.shape, F32),
            pltpu.VMEM((8, depth, width // 8), BF16),
            pltpu.VMEM((4, depth, width // 4), BF16),
            pltpu.VMEM((8, depth, width // 8), BF16),
            pltpu.VMEM((4, depth, width // 4), BF16),
        ],
        specs=([VMEM] * 3, (VMEM, VMEM, VMEM)),
        vmem=48 * 1024 * 1024,
    )


def layer_norm(values, gain_vec, bias_vec):
    row_mean = jnp.mean(values, -1, keepdims=True)
    centred = values - row_mean
    variance = jnp.mean(centred * centred, -1, keepdims=True)
    return centred * lax.rsqrt(variance + EPSILON) * gain_vec + bias_vec


def smooth_unit(values):
    return jax.nn.gelu(values, approximate=True)


def dot(first, second):
    return jnp.dot(first, second, preferred_element_type=F32)


def dot_tn(first, second):
    return lax.dot_general(first, second, (((0,), (0,)), ((), ())), preferred_element_type=F32)


def dot_nt(first, second):
    return lax.dot_general(first, second, (((1,), (1,)), ((), ())), preferred_element_type=F32)


def to_groups(rows):
    return rows.reshape(rows.shape[0], 4, -1).transpose(1, 0, 2)


def from_groups(groups):
    return groups.transpose(1, 0, 2).reshape(groups.shape[1], -1)


def heads_of(rows):
    return rows.reshape(rows.shape[0], -1, HEAD_DIM)


def per_device(
    block_input, cotangent, segment_ids, w_qkv, w_out, w_fc, w_proj, norm_gains, norm_biases
):
    section = lax.axis_index("section")
    tensor = lax.axis_index("tensor")
    tokens, width = block_input.shape[2:]
    units = w_fc.shape[2]
    depth = w_qkv.shape[1]
    group = width // 4
    scale = 1.0 / math.sqrt(HEAD_DIM)

    vectors = jnp.concatenate([norm_gains[0], norm_biases[0]], 0)
    vectors = jnp.pad(vectors.T, ((0, 0), (0, 124)))
    own = jnp.concatenate([w_qkv[0], w_out[0], w_fc[0], w_proj[0].T, vectors], 1)
    full = gather_weights(own).reshape(2, width, -1)

    def weights(block):
        edges = [0, 3 * width, 4 * width, 4 * width + units, 4 * width + 2 * units]
        pieces = [full[block, :, edges[k] : edges[k + 1]] for k in range(4)]
        norms = full[block, :, edges[4] : edges[4] + 4].T.astype(F32)
        return (*pieces, norms)

    def mine(stacked):
        return lax.dynamic_index_in_dim(stacked, section, 0, keepdims=False)

    seg_keys = mine(segment_ids)[0]
    seg_queries = lax.dynamic_index_in_dim(
        seg_keys.reshape(4, 2, tokens), tensor, 1, keepdims=False
    ).reshape(-1)
    key_pos = jnp.arange(8 * tokens)
    query_pos = lax.dynamic_index_in_dim(
        key_pos.reshape(4, 2, tokens), tensor, 1, keepdims=False
    ).reshape(-1)
    allowed = (key_pos[None, :] <= query_pos[:, None]) & (
        seg_keys[None, :] == seg_queries[:, None]
    )

    def masked_scores(query, keys):
        raw = jnp.einsum("qhd,khd->hqk", query, keys, preferred_element_type=F32)
        return jnp.where(allowed[None], raw * scale, MASKED)

    def forward(block, entry):
        qkv, out, fc, proj, norms = weights(block)
        inputs = entry.astype(F32)
        normed = layer_norm(inputs, norms[0], norms[2]).astype(BF16)
        projected = dot(normed, qkv).astype(BF16)
        q_parts = to_groups(projected[:, :width])
        kv_parts = jnp.concatenate(
            [to_groups(projected[:, width : 2 * width]), to_groups(projected[:, 2 * width :])], 2
        )
        q_all, kv_all = exchange_heads(q_parts, kv_parts, False)
        query = heads_of(q_all.reshape(-1, group))
        kv_all = kv_all.reshape(-1, 2 * group)
        keys, values = heads_of(kv_all[:, :group]), heads_of(kv_all[:, group:])
        masked = masked_scores(query, keys)
        totals = jax.nn.logsumexp(masked, axis=-1)
        probs_low = jnp.exp(masked - totals[..., None]).astype(BF16)
        mixed = jnp.einsum("hqk,khd->qhd", probs_low, values, preferred_element_type=F32)
        mixed = mixed.reshape(4, tokens, group).astype(BF16)
        mixed = from_groups(exchange_context(mixed))
        resid = inputs + dot(mixed, out)
        inner = layer_norm(resid, norms[1], norms[3]).astype(BF16)
        inner_all = jnp.concatenate([inner, exchange_pair(inner)], 0)
        upward = dot(inner_all, fc)
        active = smooth_unit(upward).astype(BF16)
        down = dot_nt(active, proj)
        down = down[:tokens] + exchange_pair(down[tokens:].astype(BF16)).astype(F32)
        sent = (resid + down).astype(BF16)
        return sent, (entry, normed, query, keys, values, totals, mixed, resid, inner_all, upward, active)

    def backward(block, incoming, kept):
        qkv, out, fc, proj, norms = weights(block)
        entry, normed, query, keys, values, totals, mixed, resid, inner_all, upward, active = kept
        incoming_all = jnp.concatenate([incoming, exchange_pair(incoming)], 0)
        active_grad = dot(incoming_all, proj)
        _, unit_pull = jax.vjp(smooth_unit, upward)
        upward_grad = unit_pull(active_grad)[0].astype(BF16)
        inner_grad = dot_nt(upward_grad, fc)
        inner_grad = inner_grad[:tokens] + exchange_pair(inner_grad[tokens:].astype(BF16)).astype(F32)
        _, late_pull = jax.vjp(layer_norm, resid, norms[1], norms[3])
        resid_part, gain_late, bias_late = late_pull(inner_grad)
        resid_grad = incoming.astype(F32) + resid_part
        resid_low = resid_grad.astype(BF16)
        mixed_grad = dot_nt(resid_low, out).astype(BF16)
        mixed_heads = heads_of(exchange_context(to_groups(mixed_grad)).reshape(-1, group))
        probs = jnp.exp(masked_scores(query, keys) - totals[..., None])
        probs_low = probs.astype(BF16)
        prob_grad = jnp.einsum("qhd,khd->hqk", mixed_heads, values, preferred_element_type=F32)
        centre = jnp.sum(probs * prob_grad, -1, keepdims=True)
        score_grad = (probs * (prob_grad - centre)).astype(BF16)
        q_grad = jnp.einsum("hqk,khd->qhd", score_grad, keys, preferred_element_type=F32) * scale
        k_grad = jnp.einsum("hqk,qhd->khd", score_grad, query, preferred_element_type=F32) * scale
        v_grad = jnp.einsum("hqk,qhd->khd", probs_low, mixed_heads, preferred_element_type=F32)
        kv_grad = jnp.concatenate(
            [k_grad.reshape(8, tokens, group), v_grad.reshape(8, tokens, group)], 2
        )
        q_back, kv_back = exchange_heads(
            q_grad.reshape(4, tokens, group).astype(BF16), kv_grad.astype(BF16), True
        )
        kv_back = jnp.sum(kv_back.reshape(4, 2, tokens, 2 * group).astype(F32), 1).astype(BF16)
        projected_grad = jnp.concatenate(
            [
                from_groups(q_back),
                from_groups(kv_back[:, :, :group]),
                from_groups(kv_back[:, :, group:]),
            ],
            1,
        )
        normed_grad = dot_nt(projected_grad, qkv)
        _, early_pull = jax.vjp(layer_norm, entry.astype(F32), norms[0], norms[2])
        input_part, gain_early, bias_early = early_pull(normed_grad)
        sent_grad = (resid_grad + input_part).astype(BF16)
        vector_grads = jnp.stack([gain_early, gain_late, bias_early, bias_late])
        operands = (
            normed, projected_grad, mixed, resid_low, inner_all, upward_grad, incoming_all, active,
            vector_grads,
        )
        return sent_grad, operands

    first, kept_first = forward(0, mine(block_input)[0])
    second, kept_second = forward(1, first)
    grad_second, operands_second = backward(1, mine(cotangent)[0], kept_second)
    grad_first, operands_first = backward(0, grad_second, kept_first)

    def swap(of_first, of_second):
        keep = jnp.where(section == 0, of_first, of_second)
        send = jnp.where(section == 0, of_second, of_first)
        return keep, lax.ppermute(send, "section", [(0, 1), (1, 0)])

    def both(of_first, of_second):
        keep, got = swap(of_first, of_second)
        return jnp.concatenate([keep, got], 0)

    def in_order(of_first, of_second):
        keep, got = swap(of_first, of_second)
        return jnp.where(section == 0, jnp.stack([keep, got]), jnp.stack([got, keep]))

    normed, projected_grad, mixed, resid_low, inner_all, upward_grad, incoming_all, active = (
        both(one, two) for one, two in zip(operands_first[:-1], operands_second[:-1])
    )
    keep, got = swap(operands_first[-1], operands_second[-1])
    vector_grads = keep + got
    block_outputs = in_order(first, second)
    input_grads = in_order(grad_first, grad_second)

    ga = jnp.concatenate([dot_tn(normed, projected_grad), dot_tn(mixed, resid_low)], 1)
    gb = jnp.concatenate([dot_tn(inner_all, upward_grad), dot_tn(incoming_all, active)], 1)
    gn = vector_grads.reshape(4, 8, depth).transpose(1, 0, 2)
    gn = jnp.pad(gn, ((0, 0), (0, 4), (0, 128 - depth)))
    out_a, out_b, out_n = reduce_grads(
        ga.astype(BF16).reshape(8, depth, -1), gb.astype(BF16).reshape(8, depth, -1), gn
    )
    out_n = out_n[:4, :depth]
    return (
        block_outputs[None, :, None],
        input_grads[None, :, None],
        out_a[None, :, : 3 * width],
        out_a[None, :, 3 * width :],
        out_b[None, :, :units],
        out_b[:, units:].T[None],
        out_n[None, :2],
        out_n[None, 2],
        out_n[None, 3],
    )


def solution(mesh):
    in_specs = (
        P(None, "shard", ("context", "tensor"), None),
        P(None, "shard", ("context", "tensor"), None),
        P(None, "shard", None),
        P("section", "shard", None),
        P("section", "shard", None),
        P("section", "shard", "tensor"),
        P("section", "tensor", "shard"),
        P("section", None, "shard"),
        P("section", None, "shard"),
    )
    out_specs = (
        P("section", None, "shard", ("context", "tensor"), None),
        P("section", None, "shard", ("context", "tensor"), None),
        P("section", "shard", None),
        P("section", "shard", None),
        P("section", "shard", "tensor"),
        P("section", "tensor", "shard"),
        P("section", None, "shard"),
        P("section", "shard"),
        P("section", "shard"),
    )
    return jax.shard_map(
        per_device, mesh=mesh, in_specs=in_specs, out_specs=out_specs, check_vma=False
    )
```

```python
import functools
import math

import jax
import jax.numpy as jnp
from jax import lax
from jax.experimental import pallas as pl
from jax.experimental.pallas import tpu as pltpu
from jax.sharding import PartitionSpec as P

HEAD_DIM = 64
EPSILON = 1e-05
MASKED = -1000000000.0
MESH = pl.DeviceIdType.MESH
BF16 = jnp.bfloat16
F32 = jnp.float32
ANY = pl.BlockSpec(memory_space=pl.ANY)
VMEM = pl.BlockSpec(memory_space=pltpu.VMEM)


class Copies:
    def __init__(self, send_sems, recv_sems):
        self.send_sems, self.recv_sems, self.made = send_sems, recv_sems, []

    def push(self, src, dst, device_id):
        index = len(self.made)
        copy = pltpu.make_async_remote_copy(
            src_ref=src,
            dst_ref=dst,
            send_sem=self.send_sems.at[index],
            recv_sem=self.recv_sems.at[index],
            device_id=device_id,
            device_id_type=MESH,
        )
        copy.start()
        self.made.append(copy)
        return copy

    def finish(self):
        for copy in self.made:
            copy.wait_send()


def greet(peers):
    barrier = pltpu.get_barrier_semaphore()
    for peer in peers:
        pl.semaphore_signal(barrier, inc=1, device_id=peer, device_id_type=MESH)
    pl.semaphore_wait(barrier, len(peers))


def call_remote(body, out_shape, copies, collective_id, args, scratch=(), locals_=1, specs=None, vmem=None):
    in_specs, out_specs = specs if specs else ([ANY] * len(args), jax.tree.map(lambda _: ANY, out_shape))
    return pl.pallas_call(
        body,
        out_shape=out_shape,
        in_specs=in_specs,
        out_specs=out_specs,
        scratch_shapes=[
            *scratch,
            pltpu.SemaphoreType.DMA((copies,)),
            pltpu.SemaphoreType.DMA((copies,)),
            pltpu.SemaphoreType.DMA((locals_,)),
        ],
        compiler_params=pltpu.CompilerParams(
            collective_id=collective_id, has_side_effects=True, vmem_limit_bytes=vmem
        ),
    )(*args)


def place():
    shard = lax.axis_index("shard")
    return lax.axis_index("section"), shard // 4, lax.rem(shard, 4)


AG_COPIES = 64


def weights_body(split, own_ref, all_ref, send_sems, recv_sems, local_sems):
    section, row, col = place()
    columns = own_ref.shape[1]
    right, left, far = lax.rem(col + 1, 4), lax.rem(col + 3, 4), lax.rem(col + 2, 4)
    to_right = {"shard": row * 4 + right}
    to_left = {"shard": row * 4 + left}
    other = 1 - row
    to_row = {"shard": other * 4 + col}
    to_core = {"section": 1 - section}
    greet([to_right, to_left, to_row, to_core])
    copies = Copies(send_sems, recv_sems)
    parts = (pl.ds(0, split), pl.ds(split, columns - split))
    half = own_ref.shape[0] // 2
    rows = (pl.ds(0, half), pl.ds(half, half))

    def slot(a_row, a_col, part, which=None):
        shard = a_row * 4 + a_col
        if which is None:
            return all_ref.at[section, shard, :, parts[part]]
        return all_ref.at[section, shard, rows[which], parts[part]]

    own_a, own_b = own_ref.at[:, parts[0]], own_ref.at[:, parts[1]]
    b_row = copies.push(own_b, slot(row, col, 1), to_row)
    a_right = copies.push(own_a, slot(row, col, 0), to_right)
    a_left = copies.push(own_a, slot(row, col, 0), to_left)
    a_row = copies.push(own_a, slot(row, col, 0), to_row)
    b_right = copies.push(own_b, slot(row, col, 1), to_right)
    b_left = copies.push(own_b, slot(row, col, 1), to_left)
    c_own = copies.push(own_ref, all_ref.at[section, row * 4 + col], to_core)
    mine = pltpu.make_async_copy(own_ref, all_ref.at[section, row * 4 + col], local_sems.at[0])
    mine.start()
    cores = [c_own]

    def share(ref):
        cores.append(copies.push(ref, ref, to_core))

    a_right.wait_recv()
    ref = slot(row, left, 0)
    a_far_right = copies.push(slot(row, left, 0, 0), slot(row, left, 0, 0), to_right)
    a_row_left = copies.push(ref, ref, to_row)
    a_left.wait_recv()
    ref2 = slot(row, right, 0)
    a_far_left = copies.push(slot(row, right, 0, 1), slot(row, right, 0, 1), to_left)
    a_row_right = copies.push(ref2, ref2, to_row)
    b_row.wait_recv()
    ref3 = slot(other, col, 1)
    b_or = copies.push(ref3, ref3, to_right)
    b_ol = copies.push(ref3, ref3, to_left)
    share(ref)
    share(ref2)
    share(ref3)
    a_far_right.wait_recv()
    a_far_left.wait_recv()
    ref = slot(row, far, 0)
    a_row_far = copies.push(ref, ref, to_row)
    share(ref)
    b_right.wait_recv()
    b_far_right = copies.push(slot(row, left, 1, 0), slot(row, left, 1, 0), to_right)
    share(slot(row, left, 1))
    b_left.wait_recv()
    b_far_left = copies.push(slot(row, right, 1, 1), slot(row, right, 1, 1), to_left)
    share(slot(row, right, 1))
    a_row.wait_recv()
    share(slot(other, col, 0))
    b_or.wait_recv()
    bo_far_right = copies.push(slot(other, left, 1, 0), slot(other, left, 1, 0), to_right)
    share(slot(other, left, 1))
    b_ol.wait_recv()
    bo_far_left = copies.push(slot(other, right, 1, 1), slot(other, right, 1, 1), to_left)
    share(slot(other, right, 1))
    a_row_left.wait_recv()
    share(slot(other, left, 0))
    a_row_right.wait_recv()
    share(slot(other, right, 0))
    b_far_right.wait_recv()
    b_far_left.wait_recv()
    share(slot(row, far, 1))
    a_row_far.wait_recv()
    share(slot(other, far, 0))
    bo_far_right.wait_recv()
    bo_far_left.wait_recv()
    share(slot(other, far, 1))
    for copy in cores:
        copy.wait_recv()
    copies.finish()
    mine.wait()


def gather_weights(own):
    depth, columns = own.shape
    return call_remote(
        functools.partial(weights_body, 2688),
        jax.ShapeDtypeStruct((2, 8, depth, columns), own.dtype),
        AG_COPIES,
        0,
        (own,),
    )


def span_peers():
    context, tensor = lax.axis_index("context"), lax.axis_index("tensor")
    span = context * 2 + tensor
    peers = []
    for step in range(1, 8):
        peer = lax.rem(span + step, 8)
        peers.append((peer, peer // 2, lax.rem(peer, 2)))
    return context, tensor, span, peers


BLOCK = 16


def add_rows(dst, terms, rows, cast=BF16):
    def step(index, _):
        at = pl.ds(pl.multiple_of(index * BLOCK, BLOCK), BLOCK)
        total = terms[0][at, :].astype(F32)
        for term in terms[1:]:
            total = total + term[at, :].astype(F32)
        dst[at, :] = total.astype(cast)
        return 0

    lax.fori_loop(0, rows // BLOCK, step, 0)


def grads_body(
    ga, gb, gn, out_a, out_b, out_n, a1, a2, a3, b1, b2, b3, n1, n2, za, zb, fa, fb,
    send_sems, recv_sems, local_sems,
):
    _, row, col = place()
    other = 1 - row
    right, left, far = lax.rem(col + 1, 4), lax.rem(col + 3, 4), lax.rem(col + 2, 4)
    to_right = {"shard": row * 4 + right}
    to_left = {"shard": row * 4 + left}
    to_row = {"shard": other * 4 + col}
    shard = row * 4 + col
    context, tensor, span, spans = span_peers()
    shard_peers = [lax.rem(shard + step, 8) for step in range(1, 8)]
    greet(
        [{"shard": peer} for peer in shard_peers]
        + [{"context": c, "tensor": t} for _, c, t in spans]
    )
    copies = Copies(send_sems, recv_sems)
    depth, width = ga.shape[1], ga.shape[2]
    half = depth // 2
    lower, upper = pl.ds(0, half), pl.ds(half, half)

    a_far_r = copies.push(ga.at[far], a1.at[0], to_right)
    a_far_l = copies.push(ga.at[4 + far], a1.at[1], to_left)
    b_far = copies.push(gb.at[other * 4 + far], b1.at[0], to_row)
    b_right = copies.push(gb.at[other * 4 + right], b1.at[1], to_row)
    b_left = copies.push(gb.at[other * 4 + left], b1.at[2], to_row)
    b_own = copies.push(gb.at[other * 4 + col], b1.at[3], to_row)
    a_plain_r = copies.push(ga.at[4 + right], a2.at[1], to_right)
    a_plain_l = copies.push(ga.at[left], a3.at[0], to_left)
    norms = [copies.push(gn.at[peer], n1.at[shard], {"shard": peer}) for peer in shard_peers]

    a_far_r.wait_recv()
    add_rows(a1.at[0], [a1.at[0], ga.at[right]], depth)
    a_sum_r = copies.push(a1.at[0], a2.at[0], to_right)
    a_far_l.wait_recv()
    add_rows(a1.at[1], [a1.at[1], ga.at[4 + left]], depth)
    a_sum_l = copies.push(a1.at[1], a3.at[1], to_left)

    b_far.wait_recv()
    add_rows(b1.at[0], [b1.at[0], gb.at[row * 4 + far]], depth)
    b_far_r = copies.push(b1.at[0, lower], b2.at[0], to_right)
    b_far_l = copies.push(b1.at[0, upper], b2.at[1], to_left)
    b_right.wait_recv()
    add_rows(b1.at[1], [b1.at[1], gb.at[row * 4 + right]], depth)
    b_left.wait_recv()
    add_rows(b1.at[2], [b1.at[2], gb.at[row * 4 + left]], depth)

    a_plain_r.wait_recv()
    a_plain_l.wait_recv()
    a_sum_r.wait_recv()
    a_sum_l.wait_recv()
    add_rows(a2.at[other], [a2.at[other], a3.at[other], ga.at[other * 4 + col]], depth)
    a_row = copies.push(a2.at[other], a2.at[2], to_row)
    add_rows(a2.at[row], [a2.at[row], a3.at[row], ga.at[row * 4 + col]], depth)

    b_far_r.wait_recv()
    add_rows(b1.at[1, lower], [b1.at[1, lower], b2.at[0]], half)
    b_sum_r = copies.push(b1.at[1], b3.at[0], to_right)
    b_far_l.wait_recv()
    add_rows(b1.at[2, upper], [b1.at[2, upper], b2.at[1]], half)
    b_sum_l = copies.push(b1.at[2], b3.at[1], to_left)

    n1[shard] = gn[shard]
    for copy in norms:
        copy.wait_recv()
    n2[span] = jnp.sum(n1[...], axis=0)
    norms2 = [
        copies.push(n2.at[span], n2.at[span], {"context": c, "tensor": t}) for _, c, t in spans
    ]

    a_row.wait_recv()
    wide = width // 8
    a_own = a2.at[row]
    add_rows(a_own, [a_own, a2.at[2]], depth)
    a_piece = [
        copies.push(
            a_own.at[:, pl.ds(pl.multiple_of(peer * wide, 128), wide)],
            za.at[span],
            {"context": c, "tensor": t},
        )
        for peer, c, t in spans
    ]
    b_own.wait_recv()
    b_sum_r.wait_recv()
    b_sum_l.wait_recv()
    add_rows(
        b1.at[3], [b1.at[3], gb.at[row * 4 + col], b3.at[0], b3.at[1]], depth
    )
    wide_b = width // 4
    contexts = [lax.rem(context + step, 4) for step in range(1, 4)]
    b_piece = [
        copies.push(
            b1.at[3, :, pl.ds(pl.multiple_of(c * wide_b, 128), wide_b)],
            zb.at[context],
            {"context": c},
        )
        for c in contexts
    ]
    za[span] = a_own[:, pl.ds(pl.multiple_of(span * wide, 128), wide)]
    zb[context] = b1[3, :, pl.ds(pl.multiple_of(context * wide_b, 128), wide_b)]
    for copy in a_piece:
        copy.wait_recv()
    add_rows(fa.at[span], [za.at[index] for index in range(8)], depth)
    a_back = [
        copies.push(fa.at[span], fa.at[span], {"context": c, "tensor": t}) for _, c, t in spans
    ]
    for copy in b_piece:
        copy.wait_recv()
    add_rows(fb.at[context], [zb.at[index] for index in range(4)], depth)
    b_back = [copies.push(fb.at[context], fb.at[context], {"context": c}) for c in contexts]
    for copy in norms2:
        copy.wait_recv()
    out_n[...] = jnp.sum(n2[...], axis=0)
    for copy in a_back:
        copy.wait_recv()
    for index in range(8):
        out_a[:, index * wide : (index + 1) * wide] = fa[index].astype(F32)
    for copy in b_back:
        copy.wait_recv()
    for index in range(4):
        out_b[:, index * wide_b : (index + 1) * wide_b] = fb[index].astype(F32)
    copies.finish()


def reduce_grads(ga, gb, gn):
    _, depth, width = ga.shape
    half = depth // 2
    return call_remote(
        grads_body,
        (
            jax.ShapeDtypeStruct((depth, width), F32),
            jax.ShapeDtypeStruct((depth, width), F32),
            jax.ShapeDtypeStruct(gn.shape[1:], F32),
        ),
        64,
        5,
        (ga, gb, gn),
        scratch=[
            pltpu.VMEM((2, depth, width), BF16),
            pltpu.VMEM((3, depth, width), BF16),
            pltpu.VMEM((2, depth, width), BF16),
            pltpu.VMEM((4, depth, width), BF16),
            pltpu.VMEM((2, half, width), BF16),
            pltpu.VMEM((2, depth, width), BF16),
            pltpu.VMEM(gn.shape, F32),
            pltpu.VMEM(gn.shape, F32),
            pltpu.VMEM((8, depth, width // 8), BF16),
            pltpu.VMEM((4, depth, width // 4), BF16),
            pltpu.VMEM((8, depth, width // 8), BF16),
            pltpu.VMEM((4, depth, width // 4), BF16),
        ],
        specs=([VMEM] * 3, (VMEM, VMEM, VMEM)),
        vmem=48 * 1024 * 1024,
    )


TOKENS = 128
SPANS = 8
GROUPS = 4
GROUP_HEADS = 3
WIDTH = 768
PAIR = 2 * HEAD_DIM
KV_GROUP = GROUP_HEADS * PAIR
SCALE = 1.0 / math.sqrt(HEAD_DIM)
GELU_A = math.sqrt(2.0 / math.pi)
GELU_B = 0.044715


def dot(first, second):
    return jnp.dot(first, second, preferred_element_type=F32)


def dot_tn(first, second):
    return lax.dot_general(first, second, (((0,), (0,)), ((), ())), preferred_element_type=F32)


def dot_nt(first, second):
    return lax.dot_general(first, second, (((1,), (1,)), ((), ())), preferred_element_type=F32)


def normalised(values):
    centred = values - jnp.mean(values, -1, keepdims=True)
    inverse = lax.rsqrt(jnp.mean(centred * centred, -1, keepdims=True) + EPSILON)
    return centred * inverse, inverse


def norm_pull(values, gain, grad):
    unit, inverse = normalised(values)
    scaled = grad * gain
    along = jnp.mean(scaled * unit, -1, keepdims=True)
    pulled = inverse * (scaled - jnp.mean(scaled, -1, keepdims=True) - unit * along)
    return pulled, jnp.sum(grad * unit, 0, keepdims=True), jnp.sum(grad, 0, keepdims=True)


def gelu(u):
    return 0.5 * u * (1.0 + jnp.tanh(GELU_A * (u + GELU_B * u * u * u)))


def gelu_slope(u):
    tanh = jnp.tanh(GELU_A * (u + GELU_B * u * u * u))
    rise = GELU_A * (1.0 + 3.0 * GELU_B * u * u)
    return 0.5 * (1.0 + tanh) + 0.5 * u * (1.0 - tanh * tanh) * rise


def lower_lanes(rows):
    return lax.broadcasted_iota(jnp.int32, (rows, PAIR), 1) < HEAD_DIM


def swapped(value):
    return pltpu.roll(value, HEAD_DIM, 1)


def split_groups(value):
    low = lower_lanes(value.shape[0])
    groups = []
    for base in (0, 384):
        t0, t1, t2 = (value[:, base + 128 * k : base + 128 * (k + 1)] for k in range(3))
        s1, s2 = swapped(t1), swapped(t2)
        groups.append(jnp.concatenate([t0, jnp.where(low, t1, 0.0)], 1))
        groups.append(jnp.concatenate([jnp.where(low, s1, s2), jnp.where(low, s2, 0.0)], 1))
    return groups


def join_groups(groups):
    low = lower_lanes(groups[0].shape[0])
    parts = []
    for first, second in ((groups[0], groups[1]), (groups[2], groups[3])):
        a0, b0, a1, b1 = first[:, :128], first[:, 128:], second[:, :128], second[:, 128:]
        s1 = swapped(a1)
        parts += [a0, jnp.where(low, b0, s1), jnp.where(low, s1, swapped(b1))]
    return jnp.concatenate(parts, 1)


def head_columns(group, at_upper):
    low = lower_lanes(group.shape[0])
    first, last = group[:, :128], group[:, 128:]
    if at_upper:
        return [
            jnp.where(low, 0.0, swapped(first)),
            jnp.where(low, 0.0, first),
            jnp.where(low, 0.0, swapped(last)),
        ]
    return [jnp.where(low, first, 0.0), jnp.where(low, swapped(first), 0.0), jnp.where(low, last, 0.0)]


class Links:
    def __init__(self, send_sems, recv_sems):
        self.send_sems, self.recv_sems, self.sent, self.count = send_sems, recv_sems, [], 0

    def copy(self, src, dst, recv_index, device_id):
        made = pltpu.make_async_remote_copy(
            src_ref=src,
            dst_ref=dst,
            send_sem=self.send_sems.at[self.count],
            recv_sem=self.recv_sems.at[recv_index],
            device_id=device_id,
            device_id_type=MESH,
        )
        self.count += 1
        return made

    def push(self, src, dst, recv_index, device_id, unless=None):
        made = self.copy(src, dst, recv_index, device_id)
        if unless is None:
            made.start()
        else:
            pl.when(jnp.logical_not(unless))(made.start)
        self.sent.append((made, unless))

    def arrived(self, dst, recv_index, unless=None):
        made = pltpu.make_async_remote_copy(
            src_ref=dst,
            dst_ref=dst,
            send_sem=self.send_sems.at[0],
            recv_sem=self.recv_sems.at[recv_index],
            device_id={"tensor": 1 - lax.axis_index("tensor")},
            device_id_type=MESH,
        )
        if unless is None:
            made.wait_recv()
        else:
            pl.when(jnp.logical_not(unless))(made.wait_recv)

    def finish(self):
        for made, unless in self.sent:
            if unless is None:
                made.wait_send()
            else:
                pl.when(jnp.logical_not(unless))(made.wait_send)


KV_AT, Q_AT, O_AT, PAIR_AT = 0, 8, 12, 16
UNITS = 1536
COLUMNS = (("q", 0, 3 * WIDTH), ("o", 3 * WIDTH, WIDTH), ("f", 4 * WIDTH, UNITS), ("p", 4 * WIDTH + UNITS, UNITS))


def load_weights(block, w_ref, buffers, sems):
    loads = []
    for index, ((_, start, size), buffer) in enumerate(zip(COLUMNS, buffers)):
        load = pltpu.make_async_copy(w_ref.at[block, :, pl.ds(start, size)], buffer, sems.at[index])
        load.start()
        loads.append(load)
    return loads


def allowed_keys(quarter, tensor, seg_keys, seg_queries):
    keys = 256 * (quarter + 1)
    rows = (2 * quarter + tensor) * TOKENS + lax.broadcasted_iota(jnp.int32, (TOKENS, keys), 0)
    columns = lax.broadcasted_iota(jnp.int32, (TOKENS, keys), 1)
    same = seg_keys[:, :keys] == seg_queries[quarter * TOKENS : (quarter + 1) * TOKENS, :]
    return (columns <= rows) & same


def head_rows(kv_all, quarter, head):
    spans = 2 * (quarter + 1)
    rows = kv_all[0:spans, :, head * PAIR : (head + 1) * PAIR]
    return rows.reshape(spans * TOKENS, PAIR)


def tiles(total, tile, body):
    def step(index, _):
        body(pl.ds(pl.multiple_of(index * tile, tile), tile))
        return 0

    lax.fori_loop(0, total // tile, step, 0)


def forward_body(
    block, x_ref, segk_ref, segq_ref, norms_ref, w_ref,
    y_out, a_out, q_out, kv_out, lse_out, mixed_out, resid_out, inner_out, up_out, act_out,
    wq, wo, wf, wp, kvb, kv_all, qb, q_all, ob, o_all, inner, down, down_in,
    send_sems, recv_sems, local_sems,
):
    context, tensor, span, spans = span_peers()
    greet([{"context": c, "tensor": t} for _, c, t in spans])
    loads = load_weights(block, w_ref, (wq, wo, wf, wp), local_sems)
    links = Links(send_sems, recv_sems)
    peer = {"tensor": 1 - tensor}

    x = x_ref[...].astype(F32)
    unit, _ = normalised(x)
    a_out[...] = (unit * norms_ref[0:1, :] + norms_ref[2:3, :]).astype(BF16)
    loads[0].wait()
    for step in range(1, 5):
        group = lax.rem(context + step, 4)
        columns = pl.ds(pl.multiple_of(WIDTH + group * KV_GROUP, 128), KV_GROUP)
        kvb[group] = dot(a_out[...], wq[:, columns]).astype(BF16)
        links.push(kvb.at[group], kv_all.at[span], KV_AT + span, {"context": group, "tensor": 1 - tensor})
        if step < 4:
            links.push(kvb.at[group], kv_all.at[span], KV_AT + span, {"context": group})
        else:
            kv_all[span] = kvb[group]
    for index, part in enumerate(split_groups(dot(a_out[...], wq[:, :WIDTH]))):
        qb[index] = part.astype(BF16)
    for step in range(1, 4):
        group = lax.rem(context + step, 4)
        links.push(qb.at[group], q_all.at[context], Q_AT + context, {"context": group})
    q_all[context] = qb[context]

    for quarter in range(GROUPS):
        for index in (2 * quarter, 2 * quarter + 1):
            links.arrived(kv_all.at[index], KV_AT + index, index == span)
        links.arrived(q_all.at[quarter], Q_AT + quarter, quarter == context)
        allowed = allowed_keys(quarter, tensor, segk_ref, segq_ref)
        queries = head_columns(q_all[quarter].astype(F32) * SCALE, False)
        low = lower_lanes(TOKENS)
        outs = []
        for head in range(GROUP_HEADS):
            rows = head_rows(kv_all, quarter, head)
            masked = jnp.where(allowed, dot_nt(queries[head].astype(BF16), rows), MASKED)
            top = jnp.max(masked, -1, keepdims=True)
            weight = jnp.exp(masked - top)
            total = jnp.sum(weight, -1, keepdims=True)
            lse_out[quarter * GROUP_HEADS + head] = top + jnp.log(total)
            outs.append(dot(weight.astype(BF16), rows) * (1.0 / total))
        pair = jnp.where(low, swapped(outs[0]), outs[1])
        last = jnp.where(low, swapped(outs[2]), 0.0)
        ob[quarter] = jnp.concatenate([pair, last], 1).astype(BF16)
        links.push(ob.at[quarter], o_all.at[context], O_AT + context, {"context": quarter}, quarter == context)
    o_all[context] = ob[context]
    q_out[...] = q_all[...]
    kv_out[...] = kv_all[...]
    for index in range(GROUPS):
        links.arrived(o_all.at[index], O_AT + index, index == context)
    mixed_out[...] = join_groups([o_all[index].astype(F32) for index in range(GROUPS)]).astype(BF16)
    loads[1].wait()
    resid = x + dot(mixed_out[...], wo[...])
    resid_out[...] = resid
    unit, _ = normalised(resid)
    inner[0] = (unit * norms_ref[1:2, :] + norms_ref[3:4, :]).astype(BF16)
    links.push(inner.at[0], inner.at[1], PAIR_AT, peer)
    loads[2].wait()
    loads[3].wait()

    def upward(half):
        rows = pl.ds(half * TOKENS, TOKENS)

        def tile(columns):
            up = dot(inner[half], wf[:, columns])
            up_out[rows, columns] = up
            act_out[rows, columns] = gelu(up).astype(BF16)

        tiles(UNITS, 512, tile)

    upward(0)
    links.arrived(inner.at[1], PAIR_AT)
    upward(1)

    def down_tile(half, columns):
        return dot_nt(act_out[half * TOKENS : (half + 1) * TOKENS, :], wp[columns, :])

    def down_peer(columns):
        down[:, columns] = down_tile(1, columns).astype(BF16)

    tiles(WIDTH, 256, down_peer)
    links.push(down, down_in, PAIR_AT + 1, peer)
    inner_out[0:TOKENS, :] = inner[0]
    inner_out[TOKENS:, :] = inner[1]
    own = resid_out[...] + down_tile(0, slice(None))
    links.arrived(down_in, PAIR_AT + 1)
    y_out[...] = (own + down_in[...].astype(F32)).astype(BF16)
    links.finish()


def shape(dims, kind=BF16):
    return jax.ShapeDtypeStruct(dims, kind)


def weight_buffers():
    return [pltpu.VMEM((WIDTH, size), BF16) for _, _, size in COLUMNS]


def forward_block(block, x, seg_keys, seg_queries, norms, full):
    return call_remote(
        functools.partial(forward_body, block),
        (
            shape((TOKENS, WIDTH)),
            shape((TOKENS, WIDTH)),
            shape((GROUPS, TOKENS, 256)),
            shape((SPANS, TOKENS, KV_GROUP)),
            shape((GROUPS * GROUP_HEADS, TOKENS, 1), F32),
            shape((TOKENS, WIDTH)),
            shape((TOKENS, WIDTH), F32),
            shape((2 * TOKENS, WIDTH)),
            shape((2 * TOKENS, UNITS), F32),
            shape((2 * TOKENS, UNITS)),
        ),
        20,
        6 + block,
        (x, seg_keys, seg_queries, norms, full),
        scratch=[
            *weight_buffers(),
            pltpu.VMEM((GROUPS, TOKENS, KV_GROUP), BF16),
            pltpu.VMEM((SPANS, TOKENS, KV_GROUP), BF16),
            pltpu.VMEM((GROUPS, TOKENS, 256), BF16),
            pltpu.VMEM((GROUPS, TOKENS, 256), BF16),
            pltpu.VMEM((GROUPS, TOKENS, 256), BF16),
            pltpu.VMEM((GROUPS, TOKENS, 256), BF16),
            pltpu.VMEM((2, TOKENS, WIDTH), BF16),
            pltpu.VMEM((TOKENS, WIDTH), BF16),
            pltpu.VMEM((TOKENS, WIDTH), BF16),
        ],
        locals_=4,
        specs=([VMEM] * 4 + [ANY], (VMEM,) * 10),
        vmem=48 * 1024 * 1024,
    )


def backward_body(
    block, dy_ref, x_ref, q_ref, kv_ref, lse_ref, resid_ref, up_ref, segk_ref, segq_ref, norms_ref, w_ref,
    dx_out, dqkv_out, low_out, dyall_out, du_out, vec_out,
    wq, wo, wf, wp, dyall, down, down_in, dob, do_all, dqb, dq_all, dkv_sum, dkvb, dkv_all,
    send_sems, recv_sems, local_sems,
):
    context, tensor, span, spans = span_peers()
    greet([{"context": c, "tensor": t} for _, c, t in spans])
    links = Links(send_sems, recv_sems)
    peer = {"tensor": 1 - tensor}
    dyall[0] = dy_ref[...]
    links.push(dyall.at[0], dyall.at[1], PAIR_AT, peer)
    loads = load_weights(block, w_ref, (wq, wo, wf, wp), local_sems)
    loads[3].wait()

    def upward(half):
        rows = pl.ds(half * TOKENS, TOKENS)

        def tile(columns):
            grad = dot(dyall[half], wp[:, columns])
            du_out[rows, columns] = (grad * gelu_slope(up_ref[rows, columns])).astype(BF16)

        tiles(UNITS, 512, tile)

    def inner_grad(half, columns):
        return dot_nt(du_out[half * TOKENS : (half + 1) * TOKENS, :], wf[columns, :])

    def down_peer(columns):
        down[:, columns] = inner_grad(1, columns).astype(BF16)

    upward(0)
    links.arrived(dyall.at[1], PAIR_AT)
    upward(1)
    loads[2].wait()
    tiles(WIDTH, 256, down_peer)
    links.push(down, down_in, PAIR_AT + 1, peer)
    own = inner_grad(0, slice(None))
    dyall_out[0:TOKENS, :] = dyall[0]
    dyall_out[TOKENS:, :] = dyall[1]
    links.arrived(down_in, PAIR_AT + 1)
    inner = own + down_in[...].astype(F32)
    pulled, gain_late, bias_late = norm_pull(resid_ref[...], norms_ref[1:2, :], inner)
    resid_grad = dy_ref[...].astype(F32) + pulled
    low_out[...] = resid_grad.astype(BF16)
    loads[1].wait()
    for index, part in enumerate(split_groups(dot_nt(low_out[...], wo[...]))):
        dob[index] = part.astype(BF16)
    for step in range(1, 4):
        group = lax.rem(context + step, 4)
        links.push(dob.at[group], do_all.at[context], O_AT + context, {"context": group})
    do_all[context] = dob[context]

    low = lower_lanes(TOKENS)
    for quarter in reversed(range(GROUPS)):
        links.arrived(do_all.at[quarter], O_AT + quarter, quarter == context)
        allowed = allowed_keys(quarter, tensor, segk_ref, segq_ref)
        queries = head_columns(q_ref[quarter].astype(F32) * SCALE, False)
        grads = head_columns(do_all[quarter].astype(F32), True)
        outs = []
        count = 2 * (quarter + 1)
        for head in range(GROUP_HEADS):
            rows = head_rows(kv_ref, quarter, head)
            query, grad = queries[head].astype(BF16), grads[head].astype(BF16)
            masked = jnp.where(allowed, dot_nt(query, rows), MASKED)
            probs = jnp.exp(masked - lse_ref[quarter * GROUP_HEADS + head])
            prob_grad = dot_nt(grad, rows)
            centre = jnp.sum(probs * prob_grad, -1, keepdims=True)
            score_grad = (probs * (prob_grad - centre)).astype(BF16)
            outs.append(dot(score_grad, rows) * SCALE)
            part = dot_tn(score_grad, query) + dot_tn(probs.astype(BF16), grad)
            part = part.reshape(count, TOKENS, PAIR)
            at = slice(head * PAIR, (head + 1) * PAIR)
            if quarter == GROUPS - 1:
                dkv_sum[0:count, :, at] = part
            else:
                dkv_sum[0:count, :, at] += part
        pair = jnp.where(low, outs[0], swapped(outs[1]))
        last = jnp.where(low, outs[2], 0.0)
        dqb[quarter] = jnp.concatenate([pair, last], 1).astype(BF16)
        links.push(dqb.at[quarter], dq_all.at[context], Q_AT + context, {"context": quarter}, quarter == context)
        for index in (2 * quarter, 2 * quarter + 1):
            dkvb[index] = dkv_sum[index].astype(BF16)
            links.push(
                dkvb.at[index], dkv_all.at[span], KV_AT + span,
                {"context": quarter, "tensor": index - 2 * quarter}, index == span,
            )
    dq_all[context] = dqb[context]
    dkv_all[span] = dkvb[span]
    for index in range(GROUPS):
        links.arrived(dq_all.at[index], Q_AT + index, index == context)
    joined = join_groups([dq_all[index].astype(F32) for index in range(GROUPS)])
    dqkv_out[:, :WIDTH] = joined.astype(BF16)
    for index in range(SPANS):
        links.arrived(dkv_all.at[index], KV_AT + index, index == span)
    for group in range(GROUPS):
        total = dkv_all[2 * group].astype(F32) + dkv_all[2 * group + 1].astype(F32)
        at = WIDTH + group * KV_GROUP
        dqkv_out[:, at : at + KV_GROUP] = total.astype(BF16)
    loads[0].wait()
    normed_grad = dot_nt(dqkv_out[...], wq[...])
    pulled, gain_early, bias_early = norm_pull(x_ref[...].astype(F32), norms_ref[0:1, :], normed_grad)
    dx_out[...] = (resid_grad + pulled).astype(BF16)
    vec_out[0:1, :] = gain_early
    vec_out[1:2, :] = gain_late
    vec_out[2:3, :] = bias_early
    vec_out[3:4, :] = bias_late
    vec_out[4:8, :] = jnp.zeros((4, WIDTH), F32)
    links.finish()


def backward_block(block, dy, x, q_all, kv_all, lse, resid, up, seg_keys, seg_queries, norms, full):
    return call_remote(
        functools.partial(backward_body, block),
        (
            shape((TOKENS, WIDTH)),
            shape((TOKENS, 3 * WIDTH)),
            shape((TOKENS, WIDTH)),
            shape((2 * TOKENS, WIDTH)),
            shape((2 * TOKENS, UNITS)),
            shape((8, WIDTH), F32),
        ),
        20,
        8 + block,
        (dy, x, q_all, kv_all, lse, resid, up, seg_keys, seg_queries, norms, full),
        scratch=[
            *weight_buffers(),
            pltpu.VMEM((2, TOKENS, WIDTH), BF16),
            pltpu.VMEM((TOKENS, WIDTH), BF16),
            pltpu.VMEM((TOKENS, WIDTH), BF16),
            pltpu.VMEM((GROUPS, TOKENS, 256), BF16),
            pltpu.VMEM((GROUPS, TOKENS, 256), BF16),
            pltpu.VMEM((GROUPS, TOKENS, 256), BF16),
            pltpu.VMEM((GROUPS, TOKENS, 256), BF16),
            pltpu.VMEM((SPANS, TOKENS, KV_GROUP), F32),
            pltpu.VMEM((SPANS, TOKENS, KV_GROUP), BF16),
            pltpu.VMEM((SPANS, TOKENS, KV_GROUP), BF16),
        ],
        locals_=4,
        specs=([VMEM] * 10 + [ANY], (VMEM,) * 6),
        vmem=48 * 1024 * 1024,
    )


def per_device(
    block_input, cotangent, segment_ids, w_qkv, w_out, w_fc, w_proj, norm_gains, norm_biases
):
    section = lax.axis_index("section")
    tensor = lax.axis_index("tensor")
    tokens, width = block_input.shape[2:]
    units = w_fc.shape[2]
    depth = w_qkv.shape[1]
    heads = width // HEAD_DIM

    pairs = w_qkv[0][:, width:].reshape(depth, 2, heads, HEAD_DIM).transpose(0, 2, 1, 3)
    vectors = jnp.concatenate([norm_gains[0], norm_biases[0]], 0)
    vectors = jnp.pad(vectors.T, ((0, 0), (0, 124)))
    own = jnp.concatenate(
        [
            w_qkv[0][:, :width],
            pairs.reshape(depth, 2 * width),
            w_out[0],
            w_fc[0],
            w_proj[0].T,
            vectors,
        ],
        1,
    )
    full = gather_weights(own).reshape(2, width, -1)
    norms = full[:, :, 4 * width + 2 * units : 4 * width + 2 * units + 8].transpose(0, 2, 1).astype(F32)

    def mine(stacked):
        return lax.dynamic_index_in_dim(stacked, section, 0, keepdims=False)

    seg_keys = mine(segment_ids)
    seg_queries = lax.dynamic_index_in_dim(
        seg_keys.reshape(4, 2, tokens), tensor, 1, keepdims=False
    ).reshape(-1, 1)

    def forward(block, entry):
        sent, normed, q_all, kv_all, lse, mixed, resid, inner, up, act = forward_block(
            block, entry, seg_keys, seg_queries, norms[block], full
        )
        return sent, (entry, q_all, kv_all, lse, resid, up), (normed, mixed, inner, act)

    def backward(block, incoming, kept, operands):
        sent, projected, low, incoming_all, up_grad, vectors = backward_block(
            block, incoming, *kept, seg_keys, seg_queries, norms[block], full
        )
        normed, mixed, inner, act = operands
        return sent, (normed, projected, mixed, low, inner, up_grad, incoming_all, act, vectors)

    first, kept_first, ops_first = forward(0, mine(block_input)[0])
    second, kept_second, ops_second = forward(1, first)
    grad_second, operands_second = backward(1, mine(cotangent)[0], kept_second, ops_second)
    grad_first, operands_first = backward(0, grad_second, kept_first, ops_first)

    def swap(of_first, of_second):
        keep = jnp.where(section == 0, of_first, of_second)
        send = jnp.where(section == 0, of_second, of_first)
        return keep, lax.ppermute(send, "section", [(0, 1), (1, 0)])

    def both(of_first, of_second):
        keep, got = swap(of_first, of_second)
        return jnp.concatenate([keep, got], 0)

    def in_order(of_first, of_second):
        keep, got = swap(of_first, of_second)
        return jnp.where(section == 0, jnp.stack([keep, got]), jnp.stack([got, keep]))

    normed, projected_grad, mixed, resid_low, inner_all, upward_grad, incoming_all, active = (
        both(one, two) for one, two in zip(operands_first[:-1], operands_second[:-1])
    )
    keep, got = swap(operands_first[-1], operands_second[-1])
    vector_grads = keep + got
    block_outputs = in_order(first, second)
    input_grads = in_order(grad_first, grad_second)

    ga = jnp.concatenate([dot_tn(normed, projected_grad), dot_tn(mixed, resid_low)], 1)
    gb = jnp.concatenate([dot_tn(inner_all, upward_grad), dot_tn(incoming_all, active)], 1)
    gn = vector_grads.reshape(8, 8, depth).transpose(1, 0, 2)
    gn = jnp.pad(gn, ((0, 0), (0, 0), (0, 128 - depth)))
    out_a, out_b, out_n = reduce_grads(
        ga.astype(BF16).reshape(8, depth, -1), gb.astype(BF16).reshape(8, depth, -1), gn
    )
    out_n = out_n[:4, :depth]
    pairs = out_a[:, width : 3 * width].reshape(depth, heads, 2, HEAD_DIM).transpose(0, 2, 1, 3)
    out_qkv = jnp.concatenate([out_a[:, :width], pairs.reshape(depth, 2 * width)], 1)
    return (
        block_outputs[None, :, None],
        input_grads[None, :, None],
        out_qkv[None],
        out_a[None, :, 3 * width :],
        out_b[None, :, :units],
        out_b[:, units:].T[None],
        out_n[None, :2],
        out_n[None, 2],
        out_n[None, 3],
    )


def solution(mesh):
    in_specs = (
        P(None, "shard", ("context", "tensor"), None),
        P(None, "shard", ("context", "tensor"), None),
        P(None, "shard", None),
        P("section", "shard", None),
        P("section", "shard", None),
        P("section", "shard", "tensor"),
        P("section", "tensor", "shard"),
        P("section", None, "shard"),
        P("section", None, "shard"),
    )
    out_specs = (
        P("section", None, "shard", ("context", "tensor"), None),
        P("section", None, "shard", ("context", "tensor"), None),
        P("section", "shard", None),
        P("section", "shard", None),
        P("section", "shard", "tensor"),
        P("section", "tensor", "shard"),
        P("section", None, "shard"),
        P("section", "shard"),
        P("section", "shard"),
    )
    return jax.shard_map(
        per_device, mesh=mesh, in_specs=in_specs, out_specs=out_specs, check_vma=False
    )
```

```python
import functools
import math

import jax
import jax.numpy as jnp
from jax import lax
from jax.experimental import pallas as pl
from jax.experimental.pallas import tpu as pltpu
from jax.sharding import PartitionSpec as P

HEAD_DIM = 64
EPSILON = 1e-05
MASKED = -1000000000.0
MESH = pl.DeviceIdType.MESH
BF16 = jnp.bfloat16
F32 = jnp.float32
ANY = pl.BlockSpec(memory_space=pl.ANY)
VMEM = pl.BlockSpec(memory_space=pltpu.VMEM)


class Copies:
    def __init__(self, send_sems, recv_sems):
        self.send_sems, self.recv_sems, self.made = send_sems, recv_sems, []

    def push(self, src, dst, device_id):
        index = len(self.made)
        copy = pltpu.make_async_remote_copy(
            src_ref=src,
            dst_ref=dst,
            send_sem=self.send_sems.at[index],
            recv_sem=self.recv_sems.at[index],
            device_id=device_id,
            device_id_type=MESH,
        )
        copy.start()
        self.made.append(copy)
        return copy

    def finish(self):
        for copy in self.made:
            copy.wait_send()


def greet(peers):
    barrier = pltpu.get_barrier_semaphore()
    for peer in peers:
        pl.semaphore_signal(barrier, inc=1, device_id=peer, device_id_type=MESH)
    pl.semaphore_wait(barrier, len(peers))


def call_remote(body, out_shape, copies, collective_id, args, scratch=(), locals_=1, specs=None, vmem=None):
    in_specs, out_specs = specs if specs else ([ANY] * len(args), jax.tree.map(lambda _: ANY, out_shape))
    return pl.pallas_call(
        body,
        out_shape=out_shape,
        in_specs=in_specs,
        out_specs=out_specs,
        scratch_shapes=[
            *scratch,
            pltpu.SemaphoreType.DMA((copies,)),
            pltpu.SemaphoreType.DMA((copies,)),
            pltpu.SemaphoreType.DMA((locals_,)),
        ],
        compiler_params=pltpu.CompilerParams(
            collective_id=collective_id, has_side_effects=True, vmem_limit_bytes=vmem
        ),
    )(*args)


def place():
    shard = lax.axis_index("shard")
    return lax.axis_index("section"), shard // 4, lax.rem(shard, 4)


GATHER_COPIES = 32


class Gather:
    def __init__(self, block, split, own, full, send_sems, recv_sems, local_sem):
        section, row, col = place()
        self.owner = section == block
        self.sems, self.made = (send_sems, recv_sems), []
        columns, half = own.shape[1], own.shape[0] // 2
        right, left, far = lax.rem(col + 1, 4), lax.rem(col + 3, 4), lax.rem(col + 2, 4)
        other = 1 - row
        to_right = {"shard": row * 4 + right}
        to_left = {"shard": row * 4 + left}
        to_row = {"shard": other * 4 + col}
        to_core = {"section": 1 - section}
        self.neighbours = [to_right, to_left, to_row, to_core]
        parts = (pl.ds(0, split), pl.ds(split, columns - split))
        rows = (pl.ds(0, half), pl.ds(half, half))

        def at(a_row, a_col, part, which=None):
            place_of = full.at[a_row * 4 + a_col]
            return place_of.at[:, parts[part]] if which is None else place_of.at[rows[which], parts[part]]

        def on(ref, to):
            return self.copy(ref, ref, to)

        own_a, own_b = own.at[:, parts[0]], own.at[:, parts[1]]
        b_row = self.copy(own_b, at(row, col, 1), to_row)
        a_right = self.copy(own_a, at(row, col, 0), to_right)
        a_left = self.copy(own_a, at(row, col, 0), to_left)
        a_row = self.copy(own_a, at(row, col, 0), to_row)
        b_right = self.copy(own_b, at(row, col, 1), to_right)
        b_left = self.copy(own_b, at(row, col, 1), to_left)
        a_far = [on(at(row, left, 0, 0), to_right), on(at(row, right, 0, 1), to_left)]
        a_row_left, a_row_right = on(at(row, left, 0), to_row), on(at(row, right, 0), to_row)
        b_other = [on(at(other, col, 1), to_right), on(at(other, col, 1), to_left)]
        a_row_far = on(at(row, far, 0), to_row)
        b_far = [on(at(row, left, 1, 0), to_right), on(at(row, right, 1, 1), to_left)]
        b_other_far = [on(at(other, left, 1, 0), to_right), on(at(other, right, 1, 1), to_left)]
        self.mine = pltpu.make_async_copy(own, full.at[row * 4 + col], local_sem)
        first_share = len(self.made)
        own_share = self.copy(own, full.at[row * 4 + col], to_core)

        def share(*where):
            return on(at(*where), to_core)

        self.stages = [
            ([], [b_row, a_right, a_left, a_row, b_right, b_left, self.mine, own_share]),
            (
                [a_right, a_left, b_row],
                [*a_far, a_row_left, a_row_right, *b_other]
                + [share(row, left, 0), share(row, right, 0), share(other, col, 1)],
            ),
            (
                [*a_far, b_right, b_left],
                [a_row_far, *b_far, share(row, far, 0), share(row, left, 1), share(row, right, 1)],
            ),
            (
                [a_row, *b_other],
                [*b_other_far, share(other, col, 0), share(other, left, 1), share(other, right, 1)],
            ),
            (
                [a_row_left, a_row_right, *b_far],
                [share(other, left, 0), share(other, right, 0), share(row, far, 1)],
            ),
            ([a_row_far, *b_other_far], [share(other, far, 0), share(other, far, 1)]),
        ]
        self.shares = self.made[first_share:]
        self.done = 0

    def copy(self, src, dst, to):
        index = len(self.made)
        made = pltpu.make_async_remote_copy(
            src_ref=src,
            dst_ref=dst,
            send_sem=self.sems[0].at[index],
            recv_sem=self.sems[1].at[index],
            device_id=to,
            device_id_type=MESH,
        )
        self.made.append(made)
        return made

    def stage(self):
        waits, starts = self.stages[self.done]
        self.done += 1

        @pl.when(self.owner)
        def _():
            for copy in waits:
                copy.wait_recv()
            for copy in starts:
                copy.start()

    def ready(self):
        while self.done < len(self.stages):
            self.stage()

        @pl.when(self.owner)
        def _():
            self.mine.wait()

        @pl.when(jnp.logical_not(self.owner))
        def _():
            for copy in self.shares:
                copy.wait_recv()

    def finish(self):
        @pl.when(self.owner)
        def _():
            for copy in self.made:
                copy.wait_send()


Q_SPLIT, R_SPLIT = 1024, 1664


def first_body(own_ref, vec_ref, full_ref, vec_out, send_sems, recv_sems, local_sems):
    section, row, col = place()
    shard = row * 4 + col
    gather = Gather(0, Q_SPLIT, own_ref, full_ref, send_sems, recv_sems, local_sems.at[0])
    peers = [
        {"section": lax.rem(section + core, 2), "shard": lax.rem(shard + step, 8)}
        for core in range(2)
        for step in range(8)
        if core + step > 0
    ]
    greet(peers)
    gather.stage()
    small = []
    for index, peer in enumerate(peers):
        small.append(
            pltpu.make_async_remote_copy(
                src_ref=vec_ref,
                dst_ref=vec_out.at[section, shard],
                send_sem=send_sems.at[GATHER_COPIES + index],
                recv_sem=recv_sems.at[GATHER_COPIES + index],
                device_id=peer,
                device_id_type=MESH,
            )
        )
        small[-1].start()
    own = pltpu.make_async_copy(vec_ref, vec_out.at[section, shard], local_sems.at[1])
    own.start()
    gather.ready()
    for copy in small:
        copy.wait_recv()
    gather.finish()
    for copy in small:
        copy.wait_send()
    own.wait()


def gather_first(own_q, vectors):
    return call_remote(
        first_body,
        (
            jax.ShapeDtypeStruct((8, *own_q.shape), own_q.dtype),
            jax.ShapeDtypeStruct((2, 8, *vectors.shape), vectors.dtype),
        ),
        GATHER_COPIES + 15,
        0,
        (own_q, vectors),
        locals_=2,
    )


def span_peers():
    context, tensor = lax.axis_index("context"), lax.axis_index("tensor")
    span = context * 2 + tensor
    peers = []
    for step in range(1, 8):
        peer = lax.rem(span + step, 8)
        peers.append((peer, peer // 2, lax.rem(peer, 2)))
    return context, tensor, span, peers


TOKENS = 128
SPANS = 8
GROUPS = 4
GROUP_HEADS = 3
WIDTH = 768
PAIR = 2 * HEAD_DIM
KV_GROUP = GROUP_HEADS * PAIR
SCALE = 1.0 / math.sqrt(HEAD_DIM)
GELU_A = math.sqrt(2.0 / math.pi)
GELU_B = 0.044715


def dot(first, second):
    return jnp.dot(first, second, preferred_element_type=F32)


def dot_tn(first, second):
    return lax.dot_general(first, second, (((0,), (0,)), ((), ())), preferred_element_type=F32)


def dot_nt(first, second):
    return lax.dot_general(first, second, (((1,), (1,)), ((), ())), preferred_element_type=F32)


def normalised(values):
    centred = values - jnp.mean(values, -1, keepdims=True)
    inverse = lax.rsqrt(jnp.mean(centred * centred, -1, keepdims=True) + EPSILON)
    return centred * inverse, inverse


def norm_pull(values, gain, grad):
    unit, inverse = normalised(values)
    scaled = grad * gain
    along = jnp.mean(scaled * unit, -1, keepdims=True)
    pulled = inverse * (scaled - jnp.mean(scaled, -1, keepdims=True) - unit * along)
    return pulled, jnp.sum(grad * unit, 0, keepdims=True), jnp.sum(grad, 0, keepdims=True)


def gelu(u):
    return 0.5 * u * (1.0 + jnp.tanh(GELU_A * (u + GELU_B * u * u * u)))


def gelu_slope(u):
    tanh = jnp.tanh(GELU_A * (u + GELU_B * u * u * u))
    rise = GELU_A * (1.0 + 3.0 * GELU_B * u * u)
    return 0.5 * (1.0 + tanh) + 0.5 * u * (1.0 - tanh * tanh) * rise


def lower_lanes(rows):
    return lax.broadcasted_iota(jnp.int32, (rows, PAIR), 1) < HEAD_DIM


def swapped(value):
    return pltpu.roll(value, HEAD_DIM, 1)


def split_groups(value):
    low = lower_lanes(value.shape[0])
    groups = []
    for base in (0, 384):
        t0, t1, t2 = (value[:, base + 128 * k : base + 128 * (k + 1)] for k in range(3))
        s1, s2 = swapped(t1), swapped(t2)
        groups.append(jnp.concatenate([t0, jnp.where(low, t1, 0.0)], 1))
        groups.append(jnp.concatenate([jnp.where(low, s1, s2), jnp.where(low, s2, 0.0)], 1))
    return groups


def join_groups(groups):
    low = lower_lanes(groups[0].shape[0])
    parts = []
    for first, second in ((groups[0], groups[1]), (groups[2], groups[3])):
        a0, b0, a1, b1 = first[:, :128], first[:, 128:], second[:, :128], second[:, 128:]
        s1 = swapped(a1)
        parts += [a0, jnp.where(low, b0, s1), jnp.where(low, s1, swapped(b1))]
    return jnp.concatenate(parts, 1)


def head_columns(group, at_upper):
    low = lower_lanes(group.shape[0])
    first, last = group[:, :128], group[:, 128:]
    if at_upper:
        return [
            jnp.where(low, 0.0, swapped(first)),
            jnp.where(low, 0.0, first),
            jnp.where(low, 0.0, swapped(last)),
        ]
    return [jnp.where(low, first, 0.0), jnp.where(low, swapped(first), 0.0), jnp.where(low, last, 0.0)]


class Links:
    def __init__(self, send_sems, recv_sems):
        self.send_sems, self.recv_sems, self.sent, self.count = send_sems, recv_sems, [], 0

    def copy(self, src, dst, recv_index, device_id):
        made = pltpu.make_async_remote_copy(
            src_ref=src,
            dst_ref=dst,
            send_sem=self.send_sems.at[self.count],
            recv_sem=self.recv_sems.at[recv_index],
            device_id=device_id,
            device_id_type=MESH,
        )
        self.count += 1
        return made

    def push(self, src, dst, recv_index, device_id, unless=None):
        made = self.copy(src, dst, recv_index, device_id)
        if unless is None:
            made.start()
        else:
            pl.when(jnp.logical_not(unless))(made.start)
        self.sent.append((made, unless))

    def arrived(self, dst, recv_index, unless=None):
        made = pltpu.make_async_remote_copy(
            src_ref=dst,
            dst_ref=dst,
            send_sem=self.send_sems.at[0],
            recv_sem=self.recv_sems.at[recv_index],
            device_id={"tensor": 1 - lax.axis_index("tensor")},
            device_id_type=MESH,
        )
        if unless is None:
            made.wait_recv()
        else:
            pl.when(jnp.logical_not(unless))(made.wait_recv)

    def finish(self):
        for made, unless in self.sent:
            if unless is None:
                made.wait_send()
            else:
                pl.when(jnp.logical_not(unless))(made.wait_send)


KV_AT, Q_AT, O_AT, PAIR_AT = 0, 8, 12, 16
UNITS = 1536
REST = WIDTH + 2 * UNITS
OUT_AT, FC_AT, PROJ_AT = 0, WIDTH, WIDTH + UNITS


def allowed_keys(quarter, tensor, seg_keys, seg_queries):
    keys = 256 * (quarter + 1)
    rows = (2 * quarter + tensor) * TOKENS + lax.broadcasted_iota(jnp.int32, (TOKENS, keys), 0)
    columns = lax.broadcasted_iota(jnp.int32, (TOKENS, keys), 1)
    same = seg_keys[:, :keys] == seg_queries[quarter * TOKENS : (quarter + 1) * TOKENS, :]
    return (columns <= rows) & same


def head_rows(kv_all, quarter, head):
    spans = 2 * (quarter + 1)
    rows = kv_all[0:spans, :, head * PAIR : (head + 1) * PAIR]
    return rows.reshape(spans * TOKENS, PAIR)


def tiles(total, tile, body):
    def step(index, _):
        body(pl.ds(pl.multiple_of(index * tile, tile), tile))
        return 0

    lax.fori_loop(0, total // tile, step, 0)


def forward_body(block, *refs):
    x_ref, segk_ref, segq_ref, norms_ref, wq_ref, own_r = refs[:6]
    own_q = refs[6] if block == 0 else None
    refs = refs[7:] if block == 0 else refs[6:]
    y_out, a_out, q_out, kv_out, lse_out, mixed_out, resid_out, inner_out, up_out, act_out = refs[:10]
    rest_out, refs = refs[10], refs[11:]
    next_out = refs[0] if block == 0 else None
    refs = refs[1:] if block == 0 else refs
    wq, wr, kvb, kv_all, qb, q_all, ob, o_all, inner, down, down_in = refs[:11]
    rest_sems, next_sems = refs[11:13], refs[13:15]
    send_sems, recv_sems, local_sems = refs[15:]

    context, tensor, span, spans = span_peers()
    rest = Gather(block, R_SPLIT, own_r, wr, *rest_sems, local_sems.at[1])
    following = None
    if block == 0:
        following = Gather(1, Q_SPLIT, own_q, next_out, *next_sems, local_sems.at[2])
    greet([{"context": c, "tensor": t} for _, c, t in spans] + rest.neighbours)
    load = pltpu.make_async_copy(wq_ref, wq, local_sems.at[0])
    load.start()
    rest.stage()
    links = Links(send_sems, recv_sems)
    peer = {"tensor": 1 - tensor}

    x = x_ref[...].astype(F32)
    unit, _ = normalised(x)
    a_out[...] = (unit * norms_ref[0:1, :] + norms_ref[2:3, :]).astype(BF16)
    load.wait()
    for step in range(1, 5):
        group = lax.rem(context + step, 4)
        columns = pl.ds(pl.multiple_of(WIDTH + group * KV_GROUP, 128), KV_GROUP)
        kvb[group] = dot(a_out[...], wq[:, columns]).astype(BF16)
        links.push(kvb.at[group], kv_all.at[span], KV_AT + span, {"context": group, "tensor": 1 - tensor})
        if step < 4:
            links.push(kvb.at[group], kv_all.at[span], KV_AT + span, {"context": group})
        else:
            kv_all[span] = kvb[group]
    for index, part in enumerate(split_groups(dot(a_out[...], wq[:, :WIDTH]))):
        qb[index] = part.astype(BF16)
    for step in range(1, 4):
        group = lax.rem(context + step, 4)
        links.push(qb.at[group], q_all.at[context], Q_AT + context, {"context": group})
    q_all[context] = qb[context]
    rest.stage()

    for quarter in range(GROUPS):
        for index in (2 * quarter, 2 * quarter + 1):
            links.arrived(kv_all.at[index], KV_AT + index, index == span)
        links.arrived(q_all.at[quarter], Q_AT + quarter, quarter == context)
        allowed = allowed_keys(quarter, tensor, segk_ref, segq_ref)
        queries = head_columns(q_all[quarter].astype(F32) * SCALE, False)
        low = lower_lanes(TOKENS)
        outs = []
        for head in range(GROUP_HEADS):
            rows = head_rows(kv_all, quarter, head)
            masked = jnp.where(allowed, dot_nt(queries[head].astype(BF16), rows), MASKED)
            top = jnp.max(masked, -1, keepdims=True)
            weight = jnp.exp(masked - top)
            total = jnp.sum(weight, -1, keepdims=True)
            lse_out[quarter * GROUP_HEADS + head] = top + jnp.log(total)
            outs.append(dot(weight.astype(BF16), rows) * (1.0 / total))
        pair = jnp.where(low, swapped(outs[0]), outs[1])
        last = jnp.where(low, swapped(outs[2]), 0.0)
        ob[quarter] = jnp.concatenate([pair, last], 1).astype(BF16)
        links.push(ob.at[quarter], o_all.at[context], O_AT + context, {"context": quarter}, quarter == context)
        rest.stage()
    if following is not None:
        following.stage()
    o_all[context] = ob[context]
    q_out[...] = q_all[...]
    kv_out[...] = kv_all[...]
    for index in range(GROUPS):
        links.arrived(o_all.at[index], O_AT + index, index == context)
    mixed_out[...] = join_groups([o_all[index].astype(F32) for index in range(GROUPS)]).astype(BF16)
    rest.ready()
    keep = pltpu.make_async_copy(wr, rest_out, local_sems.at[3])
    keep.start()

    def rest_columns(columns):
        return wr[:, :, columns].reshape(WIDTH, -1)

    resid = x + dot(mixed_out[...], rest_columns(pl.ds(OUT_AT, WIDTH)))
    resid_out[...] = resid
    unit, _ = normalised(resid)
    inner[0] = (unit * norms_ref[1:2, :] + norms_ref[3:4, :]).astype(BF16)
    links.push(inner.at[0], inner.at[1], PAIR_AT, peer)
    if following is not None:
        following.stage()

    def upward(half):
        rows = pl.ds(half * TOKENS, TOKENS)

        def tile(columns):
            up = dot(inner[half], rest_columns(pl.ds(FC_AT + columns.start, columns.size)))
            up_out[rows, columns] = up
            act_out[rows, columns] = gelu(up).astype(BF16)

        tiles(UNITS, 512, tile)

    upward(0)
    if following is not None:
        following.stage()
    links.arrived(inner.at[1], PAIR_AT)
    upward(1)

    def down_tile(half, shards):
        weights = wr[shards, :, PROJ_AT : PROJ_AT + UNITS].reshape(-1, UNITS)
        return dot_nt(act_out[half * TOKENS : (half + 1) * TOKENS, :], weights)

    for start in (0, 4):
        down[:, start * 96 : start * 96 + 384] = down_tile(1, slice(start, start + 4)).astype(BF16)
    links.push(down, down_in, PAIR_AT + 1, peer)
    if following is not None:
        following.stage()
    inner_out[0:TOKENS, :] = inner[0]
    inner_out[TOKENS:, :] = inner[1]
    own = resid_out[...] + down_tile(0, slice(None))
    if following is not None:
        following.stage()
    links.arrived(down_in, PAIR_AT + 1)
    y_out[...] = (own + down_in[...].astype(F32)).astype(BF16)
    if following is not None:
        following.ready()
        following.finish()
    rest.finish()
    links.finish()
    keep.wait()


def shape(dims, kind=BF16):
    return jax.ShapeDtypeStruct(dims, kind)


def forward_block(block, x, seg_keys, seg_queries, norms, full_q, own_r, own_q=None):
    first = own_q is not None
    shards, depth = full_q.shape[:2]
    made = call_remote(
        functools.partial(forward_body, block),
        (
            shape((TOKENS, WIDTH)),
            shape((TOKENS, WIDTH)),
            shape((GROUPS, TOKENS, 256)),
            shape((SPANS, TOKENS, KV_GROUP)),
            shape((GROUPS * GROUP_HEADS, TOKENS, 1), F32),
            shape((TOKENS, WIDTH)),
            shape((TOKENS, WIDTH), F32),
            shape((2 * TOKENS, WIDTH)),
            shape((2 * TOKENS, UNITS), F32),
            shape((2 * TOKENS, UNITS)),
            shape((shards, depth, REST)),
            *([shape(full_q.shape)] if first else []),
        ),
        20,
        6 + block,
        (x, seg_keys, seg_queries, norms, full_q.reshape(WIDTH, -1), own_r, *([own_q] if first else [])),
        scratch=[
            pltpu.VMEM((WIDTH, 3 * WIDTH), BF16),
            pltpu.VMEM((shards, depth, REST), BF16),
            pltpu.VMEM((GROUPS, TOKENS, KV_GROUP), BF16),
            pltpu.VMEM((SPANS, TOKENS, KV_GROUP), BF16),
            pltpu.VMEM((GROUPS, TOKENS, 256), BF16),
            pltpu.VMEM((GROUPS, TOKENS, 256), BF16),
            pltpu.VMEM((GROUPS, TOKENS, 256), BF16),
            pltpu.VMEM((GROUPS, TOKENS, 256), BF16),
            pltpu.VMEM((2, TOKENS, WIDTH), BF16),
            pltpu.VMEM((TOKENS, WIDTH), BF16),
            pltpu.VMEM((TOKENS, WIDTH), BF16),
            *[pltpu.SemaphoreType.DMA((GATHER_COPIES,))] * 4,
        ],
        locals_=4,
        specs=([VMEM] * 4 + [ANY] * (3 if first else 2), (VMEM,) * 10 + (ANY,) * (2 if first else 1)),
        vmem=48 * 1024 * 1024,
    )
    sent, normed, q_all, kv_all, lse, mixed, resid, inner, up, act, *weights = made
    return sent, (x, q_all, kv_all, lse, resid, up), (normed, mixed, inner, act), *weights


BLOCK = 16
HALF = 3 * WIDTH + WIDTH
PART = HALF // 2
DEPTH = WIDTH // SPANS


def add_rows(dst, terms, rows):
    def step(index, _):
        at = pl.ds(pl.multiple_of(index * BLOCK, BLOCK), BLOCK)
        total = terms[0][at, :].astype(F32)
        for term in terms[1:]:
            total = total + term[at, :].astype(F32)
        dst[at, :] = total.astype(BF16)
        return 0

    lax.fori_loop(0, rows // BLOCK, step, 0)


REDUCE_COPIES = 40
Z_SEND, BACK_SEND, SHARE_SEND = 15, 27, 39
REDUCE_BUFFERS = (
    (2, DEPTH, PART), (3, DEPTH, PART), (2, DEPTH, PART), (4, DEPTH, PART), (2, DEPTH // 2, PART),
    (2, DEPTH, PART), (SPANS, DEPTH, HALF // SPANS), (GROUPS, DEPTH, HALF // GROUPS), (DEPTH, HALF),
)


class Reduce:
    def __init__(self, block, grads, buffers, got, send_sems, recv_sems):
        self.section, self.row, self.col = place()
        self.block, self.grads, self.got = block, grads, got
        self.a1, self.a2, self.a3, self.b1, self.b2, self.b3, self.z8, self.z4, self.res = buffers
        self.send_sems, self.recv_sems = send_sems, recv_sems
        row, col = self.row, self.col
        self.other = 1 - row
        self.right, self.left, self.far = lax.rem(col + 1, 4), lax.rem(col + 3, 4), lax.rem(col + 2, 4)
        self.to_right = {"shard": row * 4 + self.right}
        self.to_left = {"shard": row * 4 + self.left}
        self.to_row = {"shard": self.other * 4 + col}
        self.to_core = {"section": 1 - self.section}
        self.context, self.tensor = lax.axis_index("context"), lax.axis_index("tensor")
        self.span = 2 * self.context + self.tensor
        self.waits, self.count = [], 0
        self.steps = [self.s0, self.s1, self.s2, self.s3, self.s4, self.s5, self.s6, self.s7, self.s8]
        self.done = 0

    def a(self, row, col):
        return self.grads.at[row * 4 + col, :, pl.ds(0, PART)]

    def b(self, row, col):
        return self.grads.at[row * 4 + col, :, pl.ds(PART, PART)]

    def copy(self, src, dst, to, send_index=None, recv_index=None):
        if send_index is None:
            send_index = recv_index = self.count
            self.count += 1
        made = pltpu.make_async_remote_copy(
            src_ref=src,
            dst_ref=dst,
            send_sem=self.send_sems.at[send_index],
            recv_sem=self.recv_sems.at[recv_index],
            device_id=to,
            device_id_type=MESH,
        )
        return made

    def push(self, src, dst, to):
        made = self.copy(src, dst, to)
        made.start()
        self.waits.append(made)
        return made

    def stage(self, count=1):
        for _ in range(count):
            if self.done < len(self.steps):
                self.steps[self.done]()
                self.done += 1

    def s0(self):
        far, other = self.far, self.other
        self.a_far_r = self.push(self.a(0, far), self.a1.at[0], self.to_right)
        self.a_far_l = self.push(self.a(1, far), self.a1.at[1], self.to_left)
        self.b_far = self.push(self.b(other, far), self.b1.at[0], self.to_row)
        self.b_right = self.push(self.b(other, self.right), self.b1.at[1], self.to_row)
        self.b_left = self.push(self.b(other, self.left), self.b1.at[2], self.to_row)
        self.b_own = self.push(self.b(other, self.col), self.b1.at[3], self.to_row)
        self.a_plain_r = self.push(self.a(1, self.right), self.a2.at[1], self.to_right)
        self.a_plain_l = self.push(self.a(0, self.left), self.a3.at[0], self.to_left)

    def s1(self):
        self.a_far_r.wait_recv()
        add_rows(self.a1.at[0], [self.a1.at[0], self.a(0, self.right)], DEPTH)
        self.a_sum_r = self.push(self.a1.at[0], self.a2.at[0], self.to_right)
        self.a_far_l.wait_recv()
        add_rows(self.a1.at[1], [self.a1.at[1], self.a(1, self.left)], DEPTH)
        self.a_sum_l = self.push(self.a1.at[1], self.a3.at[1], self.to_left)

    def s2(self):
        half = DEPTH // 2
        self.b_far.wait_recv()
        add_rows(self.b1.at[0], [self.b1.at[0], self.b(self.row, self.far)], DEPTH)
        self.b_far_r = self.push(self.b1.at[0, pl.ds(0, half)], self.b2.at[0], self.to_right)
        self.b_far_l = self.push(self.b1.at[0, pl.ds(half, half)], self.b2.at[1], self.to_left)
        self.b_right.wait_recv()
        add_rows(self.b1.at[1], [self.b1.at[1], self.b(self.row, self.right)], DEPTH)
        self.b_left.wait_recv()
        add_rows(self.b1.at[2], [self.b1.at[2], self.b(self.row, self.left)], DEPTH)

    def s3(self):
        row, other, col = self.row, self.other, self.col
        for copy in (self.a_plain_r, self.a_plain_l, self.a_sum_r, self.a_sum_l):
            copy.wait_recv()
        add_rows(self.a2.at[other], [self.a2.at[other], self.a3.at[other], self.a(other, col)], DEPTH)
        self.a_row = self.push(self.a2.at[other], self.a2.at[2], self.to_row)
        add_rows(self.a2.at[row], [self.a2.at[row], self.a3.at[row], self.a(row, col)], DEPTH)

    def s4(self):
        half = DEPTH // 2
        lower, upper = pl.ds(0, half), pl.ds(half, half)
        self.b_far_r.wait_recv()
        add_rows(self.b1.at[1, lower], [self.b1.at[1, lower], self.b2.at[0]], half)
        self.b_sum_r = self.push(self.b1.at[1], self.b3.at[0], self.to_right)
        self.b_far_l.wait_recv()
        add_rows(self.b1.at[2, upper], [self.b1.at[2, upper], self.b2.at[1]], half)
        self.b_sum_l = self.push(self.b1.at[2], self.b3.at[1], self.to_left)

    def pieces(self, total, first):
        self.piece_copies = getattr(self, "piece_copies", [])

        def each(section, count, me, slots, to, base):
            wide = HALF // count
            for index in range(count // 2):
                target = first * (count // 2) + index
                src = total.at[:, pl.ds(index * wide, wide)]
                copy = self.copy(src, slots.at[me], to(target), Z_SEND + base + target, Z_SEND + base + me)
                here = self.section == section
                away = jnp.logical_and(here, target != me)
                pl.when(away)(copy.start)
                self.piece_copies.append((copy, away))

                @pl.when(jnp.logical_and(here, target == me))
                def _(src=src, target=target):
                    slots[target] = src[...]

        each(0, SPANS, self.span, self.z8, lambda t: {"context": t // 2, "tensor": t % 2}, 0)
        each(1, GROUPS, self.context, self.z4, lambda t: {"context": t}, 8)

    def s5(self):
        self.a_row.wait_recv()
        total = self.a2.at[self.row]
        add_rows(total, [total, self.a2.at[2]], DEPTH)
        self.pieces(total, 0)

    def s6(self):
        for copy in (self.b_own, self.b_sum_r, self.b_sum_l):
            copy.wait_recv()
        total = self.b1.at[3]
        add_rows(total, [total, self.b(self.row, self.col), self.b3.at[0], self.b3.at[1]], DEPTH)
        self.pieces(total, 1)

    def sequence(self):
        return (
            (0, SPANS, self.span, self.z8, lambda t: {"context": t // 2, "tensor": t % 2}, 0),
            (1, GROUPS, self.context, self.z4, lambda t: {"context": t}, 8),
        )

    def s7(self):
        self.back_copies = []
        for section, count, me, slots, to, base in self.sequence():
            wide = HALF // count
            mine = self.res.at[:, pl.ds(pl.multiple_of(me * wide, 128), wide)]
            here = self.section == section
            arrivals = [
                (self.copy(slots.at[t], slots.at[t], to(t), 0, Z_SEND + base + t), t) for t in range(count)
            ]
            backs = [
                (self.copy(mine, mine, to(t), BACK_SEND + base + t, BACK_SEND + base + me), t)
                for t in range(count)
            ]

            @pl.when(here)
            def _(arrivals=arrivals, backs=backs, slots=slots, mine=mine, count=count, me=me):
                for copy, source in arrivals:
                    pl.when(source != me)(copy.wait_recv)
                add_rows(mine, [slots.at[t] for t in range(count)], DEPTH)
                for copy, target in backs:
                    pl.when(target != me)(copy.start)

            self.back_copies += [(copy, jnp.logical_and(here, t != me)) for copy, t in backs]

    def s8(self):
        for section, count, me, slots, to, base in self.sequence():
            wide = HALF // count
            here = self.section == section
            for t in range(count):
                at = self.res.at[:, pl.ds(t * wide, wide)]
                copy = self.copy(at, at, to(t), 0, BACK_SEND + base + t)
                pl.when(jnp.logical_and(here, t != me))(copy.wait_recv)
        self.share = self.copy(self.res, self.got, self.to_core, SHARE_SEND, SHARE_SEND)
        pl.when(self.section != self.block)(self.share.start)

    def finish(self):
        self.stage(len(self.steps))
        pl.when(self.section == self.block)(self.share.wait_recv)
        for copy in self.waits:
            copy.wait_send()
        for copy, started in self.piece_copies + self.back_copies:
            pl.when(started)(copy.wait_send)
        pl.when(self.section != self.block)(self.share.wait_send)


def backward_body(last, *refs):
    dy_ref, x_ref, q_ref, kv_ref, lse_ref, resid_ref, up_ref = refs[:7]
    normed_ref, mixed_ref, inner_ref, act_ref, segk_ref, segq_ref, norms_ref = refs[7:14]
    wq_ref, wr_ref = refs[14:16]
    refs = refs[16:]
    if last:
        later_ref, vec_ref, first_ref, second_ref = refs[:4]
        mine_out, vec_out, got_out, blocks_out, inputs_out = refs[4:9]
        refs = refs[9:]
    else:
        dx_out, grads, vec_out = refs[:3]
        refs = refs[3:]
    wq, wr, down, down_in, dob, do_all, dqb, dq_all, dkv_sum, dkvb, dkv_all = refs[:11]
    n2, q2, m2, l2, i2, u2, y2, t2, swap_send, swap_recv = refs[11:21]
    refs = refs[21:]
    if last:
        grads, dx, vec0, vec_got, vec8, vec64 = refs[:6]
        buffers = len(REDUCE_BUFFERS)
        later_buffers, now_buffers = refs[6 : 6 + buffers], refs[6 + buffers : 6 + 2 * buffers]
        late_sems = refs[6 + 2 * buffers : -3]
    send_sems, recv_sems, local_sems = refs[-3:]

    section, row, col = place()
    shard = row * 4 + col
    context, tensor, span, spans = span_peers()
    span_ids = [{"context": c, "tensor": t} for _, c, t in spans]
    to_core = {"section": 1 - section}
    shard_ids = [{"shard": lax.rem(shard + step, 8)} for step in range(1, 8)] if last else []
    greet(span_ids + [to_core] + shard_ids)
    links = Links(send_sems, recv_sems)
    peer = {"tensor": 1 - tensor}
    own, got = pl.ds(0, TOKENS), pl.ds(TOKENS, TOKENS)
    own2, got2 = pl.ds(0, 2 * TOKENS), pl.ds(2 * TOKENS, 2 * TOKENS)
    y2[own] = dy_ref[...]
    links.push(y2.at[own], y2.at[got], PAIR_AT, peer)
    loads = []
    for index, (start, size) in enumerate(((PROJ_AT, UNITS), (FC_AT, UNITS), (OUT_AT, WIDTH))):
        at = pl.ds(start, size)
        loads.append(pltpu.make_async_copy(wr_ref.at[:, at], wr.at[:, at], local_sems.at[index]))
    loads.append(pltpu.make_async_copy(wq_ref, wq, local_sems.at[3]))
    for load in loads:
        load.start()

    def moved(src, dst, index, sems=(swap_send, swap_recv)):
        return pltpu.make_async_remote_copy(
            src_ref=src,
            dst_ref=dst,
            send_sem=sems[0].at[index],
            recv_sem=sems[1].at[index],
            device_id=to_core,
            device_id_type=MESH,
        )

    to_first = [
        moved(normed_ref, n2.at[got], 0),
        moved(mixed_ref, m2.at[got], 1),
        moved(l2.at[own], l2.at[got], 2),
        moved(q2.at[own], q2.at[got], 3),
    ]
    to_second = [
        moved(inner_ref, i2.at[got2], 4),
        moved(act_ref, t2.at[got2], 5),
        moved(y2.at[own2], y2.at[got2], 6),
        moved(u2.at[own2], u2.at[got2], 7),
    ]

    def send_first(*which):
        @pl.when(section == 1)
        def _():
            for index in which:
                to_first[index].start()

    def send_second(*which):
        @pl.when(section == 0)
        def _():
            for index in which:
                to_second[index].start()

    reduce_later = None
    if last:
        reduce_later = Reduce(1, later_ref, later_buffers, got_out, *late_sems[0:2])
        reduce_now = Reduce(0, grads, now_buffers, got_out, *late_sems[2:4])
        out_sems = late_sems[4:6]
        for_second = [
            moved(second_ref, blocks_out.at[0], 0, out_sems),
            moved(dy_ref, inputs_out.at[0], 1, out_sems),
        ]
        for_first = [
            moved(first_ref, blocks_out.at[1], 0, out_sems),
            moved(dx, inputs_out.at[1], 1, out_sems),
        ]
        kept_second = [
            pltpu.make_async_copy(second_ref, blocks_out.at[1], local_sems.at[4]),
            pltpu.make_async_copy(dy_ref, inputs_out.at[1], local_sems.at[5]),
        ]
        kept_first = [
            pltpu.make_async_copy(first_ref, blocks_out.at[0], local_sems.at[4]),
            pltpu.make_async_copy(dx, inputs_out.at[0], local_sems.at[5]),
        ]

    def ride(count=1):
        if reduce_later is not None:
            reduce_later.stage(count)

    ride()
    send_first(0, 1)
    send_second(0, 1)
    if last:

        @pl.when(section == 0)
        def _():
            for copy in for_second:
                copy.start()
            kept_first[0].start()

        @pl.when(section == 1)
        def _():
            for_first[0].start()
            for copy in kept_second:
                copy.start()

    @pl.when(section == 0)
    def _():
        n2[own] = normed_ref[...]
        m2[own] = mixed_ref[...]

    @pl.when(section == 1)
    def _():
        i2[own2] = inner_ref[...]
        t2[own2] = act_ref[...]

    loads[0].wait()

    def upward(half):
        rows = pl.ds(half * TOKENS, TOKENS)

        def tile(columns):
            grad = dot(y2[rows], wr[:, pl.ds(PROJ_AT + columns.start, columns.size)])
            u2[rows, columns] = (grad * gelu_slope(up_ref[rows, columns])).astype(BF16)

        tiles(UNITS, 512, tile)

    def inner_grad(half, columns):
        return dot_nt(u2[half * TOKENS : (half + 1) * TOKENS, :], wr[columns, FC_AT : FC_AT + UNITS])

    def down_peer(columns):
        down[:, columns] = inner_grad(1, columns).astype(BF16)

    upward(0)
    links.arrived(y2.at[got], PAIR_AT)
    send_second(2)
    upward(1)
    send_second(3)
    loads[1].wait()
    tiles(WIDTH, 256, down_peer)
    links.push(down, down_in, PAIR_AT + 1, peer)
    inner_own = inner_grad(0, slice(None))
    ride()
    links.arrived(down_in, PAIR_AT + 1)
    inner = inner_own + down_in[...].astype(F32)
    pulled, gain_late, bias_late = norm_pull(resid_ref[...], norms_ref[1:2, :], inner)
    resid_grad = dy_ref[...].astype(F32) + pulled
    l2[own] = resid_grad.astype(BF16)
    send_first(2)
    loads[2].wait()
    for index, part in enumerate(split_groups(dot_nt(l2[own], wr[:, OUT_AT : OUT_AT + WIDTH]))):
        dob[index] = part.astype(BF16)
    for step in range(1, 4):
        group = lax.rem(context + step, 4)
        links.push(dob.at[group], do_all.at[context], O_AT + context, {"context": group})
    do_all[context] = dob[context]
    ride()

    low = lower_lanes(TOKENS)
    for quarter in reversed(range(GROUPS)):
        links.arrived(do_all.at[quarter], O_AT + quarter, quarter == context)
        allowed = allowed_keys(quarter, tensor, segk_ref, segq_ref)
        queries = head_columns(q_ref[quarter].astype(F32) * SCALE, False)
        grads_in = head_columns(do_all[quarter].astype(F32), True)
        outs = []
        count = 2 * (quarter + 1)
        for head in range(GROUP_HEADS):
            rows = head_rows(kv_ref, quarter, head)
            query, grad = queries[head].astype(BF16), grads_in[head].astype(BF16)
            masked = jnp.where(allowed, dot_nt(query, rows), MASKED)
            probs = jnp.exp(masked - lse_ref[quarter * GROUP_HEADS + head])
            prob_grad = dot_nt(grad, rows)
            centre = jnp.sum(probs * prob_grad, -1, keepdims=True)
            score_grad = (probs * (prob_grad - centre)).astype(BF16)
            outs.append(dot(score_grad, rows) * SCALE)
            part = dot_tn(score_grad, query) + dot_tn(probs.astype(BF16), grad)
            part = part.reshape(count, TOKENS, PAIR)
            at = slice(head * PAIR, (head + 1) * PAIR)
            if quarter == GROUPS - 1:
                dkv_sum[0:count, :, at] = part
            else:
                dkv_sum[0:count, :, at] += part
        pair = jnp.where(low, outs[0], swapped(outs[1]))
        last_head = jnp.where(low, outs[2], 0.0)
        dqb[quarter] = jnp.concatenate([pair, last_head], 1).astype(BF16)
        links.push(dqb.at[quarter], dq_all.at[context], Q_AT + context, {"context": quarter}, quarter == context)
        for index in (2 * quarter, 2 * quarter + 1):
            dkvb[index] = dkv_sum[index].astype(BF16)
            links.push(
                dkvb.at[index], dkv_all.at[span], KV_AT + span,
                {"context": quarter, "tensor": index - 2 * quarter}, index == span,
            )
        ride()
    dq_all[context] = dqb[context]
    dkv_all[span] = dkvb[span]
    for index in range(GROUPS):
        links.arrived(dq_all.at[index], Q_AT + index, index == context)
    joined = join_groups([dq_all[index].astype(F32) for index in range(GROUPS)])
    q2[own, :WIDTH] = joined.astype(BF16)
    for index in range(SPANS):
        links.arrived(dkv_all.at[index], KV_AT + index, index == span)
    for group in range(GROUPS):
        total = dkv_all[2 * group].astype(F32) + dkv_all[2 * group + 1].astype(F32)
        at = WIDTH + group * KV_GROUP
        q2[own, at : at + KV_GROUP] = total.astype(BF16)
    send_first(3)
    loads[3].wait()
    normed_grad = dot_nt(q2[own], wq[...])
    pulled, gain_early, bias_early = norm_pull(x_ref[...].astype(F32), norms_ref[0:1, :], normed_grad)
    dx_low = (resid_grad + pulled).astype(BF16)
    vec_here = vec0 if last else vec_out
    for index, vector in enumerate((gain_early, gain_late, bias_early, bias_late)):
        vec_here[index : index + 1, :] = vector
    vec_here[4:8, :] = jnp.zeros((4, WIDTH), F32)
    if last:
        dx[...] = dx_low
        vec_first = moved(vec0, vec_got, 2, out_sems)
        vec_second = moved(vec_ref, vec_got, 2, out_sems)

        @pl.when(section == 0)
        def _():
            kept_first[1].start()
            vec_second.start()

        @pl.when(section == 1)
        def _():
            for_first[1].start()
            vec_first.start()
    else:
        dx_out[...] = dx_low
    ride()

    def product(first, second, start):
        size = second.shape[1]
        for top in (0, 4):
            rows = first[:, top * DEPTH : (top + 4) * DEPTH]

            def tile(columns, top=top, rows=rows):
                part = dot_tn(rows, second[:, columns]).astype(BF16)
                grads[top : top + 4, :, pl.ds(start + columns.start, columns.size)] = part.reshape(
                    4, DEPTH, columns.size
                )

            tiles(size, 768, tile)

    @pl.when(section == 0)
    def _():
        for copy in to_first:
            copy.wait_recv()
        product(n2, q2, 0)
        product(m2, l2, 3 * WIDTH)

    @pl.when(section == 1)
    def _():
        for copy in to_second:
            copy.wait_recv()
        product(i2, u2, 0)
        product(y2, t2, UNITS)

    if last:
        reduce_now.stage()
        ride(9)
        vec_first.wait_recv()
        vec8[shard] = jnp.where(section == 0, vec0[...], vec_ref[...]) + vec_got[...]
        sems = late_sems[6:8]
        sums = []

        def spread(buffer, me, ids, sources, base):
            for index, target in enumerate(ids):
                copy = pltpu.make_async_remote_copy(
                    src_ref=buffer.at[me],
                    dst_ref=buffer.at[me],
                    send_sem=sems[0].at[base + index],
                    recv_sem=sems[1].at[base + index],
                    device_id=target,
                    device_id_type=MESH,
                )
                copy.start()
                sums.append(copy)

        spread(vec8, shard, shard_ids, None, 0)
        reduce_now.stage(2)
        for copy in sums[:7]:
            copy.wait_recv()
        vec64[span] = jnp.sum(vec8[...], 0)
        spread(vec64, span, span_ids, None, 7)
        reduce_now.stage(9)
        for copy in sums[7:]:
            copy.wait_recv()
        vec_out[...] = jnp.sum(vec64[...], 0)

        @pl.when(section == 0)
        def _():
            mine_out[...] = reduce_now.res[...]

        @pl.when(section == 1)
        def _():
            mine_out[...] = reduce_later.res[...]

        reduce_later.finish()
        reduce_now.finish()
        for copy in sums:
            copy.wait_send()
        for_second[0].wait_recv()
        for_second[1].wait_recv()

        @pl.when(section == 0)
        def _():
            for copy in for_second + [vec_second]:
                copy.wait_send()

        @pl.when(section == 1)
        def _():
            for copy in for_first + [vec_first]:
                copy.wait_send()

        for copy in kept_first:
            copy.wait()

    @pl.when(section == 1)
    def _():
        for copy in to_first:
            copy.wait_send()

    @pl.when(section == 0)
    def _():
        for copy in to_second:
            copy.wait_send()

    links.finish()


def backward_block(last, args, weights, extra=()):
    outputs, scratch = (
        (
            shape((DEPTH, HALF)),
            shape((8, WIDTH), F32),
            shape((DEPTH, HALF)),
            shape((2, TOKENS, WIDTH)),
            shape((2, TOKENS, WIDTH)),
        ),
        [
            pltpu.VMEM((SPANS, DEPTH, HALF), BF16),
            pltpu.VMEM((TOKENS, WIDTH), BF16),
            pltpu.VMEM((8, WIDTH), F32),
            pltpu.VMEM((8, WIDTH), F32),
            pltpu.VMEM((SPANS, 8, WIDTH), F32),
            pltpu.VMEM((SPANS, 8, WIDTH), F32),
            *[pltpu.VMEM(dims, BF16) for dims in REDUCE_BUFFERS],
            *[pltpu.VMEM(dims, BF16) for dims in REDUCE_BUFFERS],
            *[pltpu.SemaphoreType.DMA((REDUCE_COPIES,))] * 4,
            *[pltpu.SemaphoreType.DMA((4,))] * 2,
            *[pltpu.SemaphoreType.DMA((14,))] * 2,
        ],
    ) if last else (
        (shape((TOKENS, WIDTH)), shape((SPANS, DEPTH, HALF)), shape((8, WIDTH), F32)),
        [],
    )
    out_specs = (VMEM, VMEM, ANY, ANY, ANY) if last else (VMEM,) * 3
    return call_remote(
        functools.partial(backward_body, last),
        outputs,
        20,
        9 if last else 8,
        (*args, *weights, *extra),
        scratch=[
            pltpu.VMEM((WIDTH, 3 * WIDTH), BF16),
            pltpu.VMEM((WIDTH, REST), BF16),
            pltpu.VMEM((TOKENS, WIDTH), BF16),
            pltpu.VMEM((TOKENS, WIDTH), BF16),
            *[pltpu.VMEM((GROUPS, TOKENS, 256), BF16)] * 4,
            pltpu.VMEM((SPANS, TOKENS, KV_GROUP), F32),
            pltpu.VMEM((SPANS, TOKENS, KV_GROUP), BF16),
            pltpu.VMEM((SPANS, TOKENS, KV_GROUP), BF16),
            pltpu.VMEM((2 * TOKENS, WIDTH), BF16),
            pltpu.VMEM((2 * TOKENS, 3 * WIDTH), BF16),
            pltpu.VMEM((2 * TOKENS, WIDTH), BF16),
            pltpu.VMEM((2 * TOKENS, WIDTH), BF16),
            pltpu.VMEM((4 * TOKENS, WIDTH), BF16),
            pltpu.VMEM((4 * TOKENS, UNITS), BF16),
            pltpu.VMEM((4 * TOKENS, WIDTH), BF16),
            pltpu.VMEM((4 * TOKENS, UNITS), BF16),
            *[pltpu.SemaphoreType.DMA((8,))] * 2,
            *scratch,
        ],
        locals_=6,
        specs=([VMEM] * 14 + [ANY] * 2 + [VMEM] * len(extra), out_specs),
        vmem=60 * 1024 * 1024,
    )


def per_device(
    block_input, cotangent, segment_ids, w_qkv, w_out, w_fc, w_proj, norm_gains, norm_biases
):
    section = lax.axis_index("section")
    tensor = lax.axis_index("tensor")
    tokens, width = block_input.shape[2:]
    units = w_fc.shape[2]
    depth = w_qkv.shape[1]
    heads = width // HEAD_DIM

    pairs = w_qkv[0][:, width:].reshape(depth, 2, heads, HEAD_DIM).transpose(0, 2, 1, 3)
    own_q = jnp.concatenate([w_qkv[0][:, :width], pairs.reshape(depth, 2 * width)], 1)
    own_r = jnp.concatenate([w_out[0], w_fc[0], w_proj[0].T], 1)
    vectors = jnp.concatenate([norm_gains[0], norm_biases[0]], 0)
    vectors = jnp.pad(vectors, ((0, 12), (0, 128 - depth)))
    first_q, vectors = gather_first(own_q, vectors)
    norms = vectors[:, :, :8, :depth].transpose(0, 2, 1, 3).reshape(2, 8, width).astype(F32)

    def mine(stacked):
        return lax.dynamic_index_in_dim(stacked, section, 0, keepdims=False)

    seg_keys = mine(segment_ids)
    seg_queries = lax.dynamic_index_in_dim(
        seg_keys.reshape(4, 2, tokens), tensor, 1, keepdims=False
    ).reshape(-1, 1)

    entry = mine(block_input)[0]
    first, kept_first, ops_first, rest_first, second_q = forward_block(
        0, entry, seg_keys, seg_queries, norms[0], first_q, own_r, own_q
    )
    second, kept_second, ops_second, rest_second = forward_block(
        1, first, seg_keys, seg_queries, norms[1], second_q, own_r
    )

    def arguments(block, incoming, kept, operands):
        return (incoming, *kept, *operands, seg_keys, seg_queries, norms[block])

    def flat(*weights):
        return tuple(weight.reshape(width, -1) for weight in weights)

    grad_second, grads_second, vectors_second = backward_block(
        False, arguments(1, mine(cotangent)[0], kept_second, ops_second), flat(second_q, rest_second)
    )
    own_half, vector_grads, other_half, block_outputs, input_grads = backward_block(
        True,
        arguments(0, grad_second, kept_first, ops_first),
        flat(first_q, rest_first),
        (grads_second, vectors_second, first, second),
    )
    out_a = jnp.where(section == 0, own_half, other_half).astype(F32)
    out_b = jnp.where(section == 0, other_half, own_half).astype(F32)
    out_n = lax.dynamic_slice_in_dim(vector_grads, lax.axis_index("shard") * depth, depth, 1)
    pairs = out_a[:, width : 3 * width].reshape(depth, heads, 2, HEAD_DIM).transpose(0, 2, 1, 3)
    out_qkv = jnp.concatenate([out_a[:, :width], pairs.reshape(depth, 2 * width)], 1)
    return (
        block_outputs[None, :, None],
        input_grads[None, :, None],
        out_qkv[None],
        out_a[None, :, 3 * width :],
        out_b[None, :, :units],
        out_b[:, units:].T[None],
        out_n[None, :2],
        out_n[None, 2],
        out_n[None, 3],
    )


def solution(mesh):
    in_specs = (
        P(None, "shard", ("context", "tensor"), None),
        P(None, "shard", ("context", "tensor"), None),
        P(None, "shard", None),
        P("section", "shard", None),
        P("section", "shard", None),
        P("section", "shard", "tensor"),
        P("section", "tensor", "shard"),
        P("section", None, "shard"),
        P("section", None, "shard"),
    )
    out_specs = (
        P("section", None, "shard", ("context", "tensor"), None),
        P("section", None, "shard", ("context", "tensor"), None),
        P("section", "shard", None),
        P("section", "shard", None),
        P("section", "shard", "tensor"),
        P("section", "tensor", "shard"),
        P("section", None, "shard"),
        P("section", "shard"),
        P("section", "shard"),
    )
    return jax.shard_map(
        per_device, mesh=mesh, in_specs=in_specs, out_specs=out_specs, check_vma=False
    )
```

```python
import functools
import math

import jax
import jax.numpy as jnp
from jax import lax
from jax.experimental import pallas as pl
from jax.experimental.pallas import tpu as pltpu
from jax.sharding import PartitionSpec as P

HEAD_DIM = 64
EPSILON = 1e-05
MASKED = -1000000000.0
MESH = pl.DeviceIdType.MESH
BF16 = jnp.bfloat16
F32 = jnp.float32
ANY = pl.BlockSpec(memory_space=pl.ANY)
VMEM = pl.BlockSpec(memory_space=pltpu.VMEM)


class Copies:
    def __init__(self, send_sems, recv_sems):
        self.send_sems, self.recv_sems, self.made = send_sems, recv_sems, []

    def push(self, src, dst, device_id):
        index = len(self.made)
        copy = pltpu.make_async_remote_copy(
            src_ref=src,
            dst_ref=dst,
            send_sem=self.send_sems.at[index],
            recv_sem=self.recv_sems.at[index],
            device_id=device_id,
            device_id_type=MESH,
        )
        copy.start()
        self.made.append(copy)
        return copy

    def finish(self):
        for copy in self.made:
            copy.wait_send()


def greet(peers):
    barrier = pltpu.get_barrier_semaphore()
    for peer in peers:
        pl.semaphore_signal(barrier, inc=1, device_id=peer, device_id_type=MESH)
    pl.semaphore_wait(barrier, len(peers))


def call_remote(body, out_shape, copies, collective_id, args, scratch=(), locals_=1, specs=None, vmem=None):
    in_specs, out_specs = specs if specs else ([ANY] * len(args), jax.tree.map(lambda _: ANY, out_shape))
    return pl.pallas_call(
        body,
        out_shape=out_shape,
        in_specs=in_specs,
        out_specs=out_specs,
        scratch_shapes=[
            *scratch,
            pltpu.SemaphoreType.DMA((copies,)),
            pltpu.SemaphoreType.DMA((copies,)),
            pltpu.SemaphoreType.DMA((locals_,)),
        ],
        compiler_params=pltpu.CompilerParams(
            collective_id=collective_id, has_side_effects=True, vmem_limit_bytes=vmem
        ),
    )(*args)


def place():
    shard = lax.axis_index("shard")
    return lax.axis_index("section"), shard // 4, lax.rem(shard, 4)


GATHER_COPIES = 32


class Gather:
    def __init__(self, block, split, own, full, send_sems, recv_sems, local_sem):
        section, row, col = place()
        self.owner = section == block
        self.sems, self.made = (send_sems, recv_sems), []
        columns, half = own.shape[1], own.shape[0] // 2
        right, left, far = lax.rem(col + 1, 4), lax.rem(col + 3, 4), lax.rem(col + 2, 4)
        other = 1 - row
        to_right = {"shard": row * 4 + right}
        to_left = {"shard": row * 4 + left}
        to_row = {"shard": other * 4 + col}
        to_core = {"section": 1 - section}
        self.neighbours = [to_right, to_left, to_row, to_core]
        parts = (pl.ds(0, split), pl.ds(split, columns - split))
        rows = (pl.ds(0, half), pl.ds(half, half))

        def at(a_row, a_col, part, which=None):
            place_of = full.at[a_row * 4 + a_col]
            return place_of.at[:, parts[part]] if which is None else place_of.at[rows[which], parts[part]]

        def on(ref, to):
            return self.copy(ref, ref, to)

        own_a, own_b = own.at[:, parts[0]], own.at[:, parts[1]]
        b_row = self.copy(own_b, at(row, col, 1), to_row)
        b_right = self.copy(own_b, at(row, col, 1), to_right)
        b_left = self.copy(own_b, at(row, col, 1), to_left)
        b_other = [on(at(other, col, 1), to_right), on(at(other, col, 1), to_left)]
        b_far = [on(at(row, left, 1, 0), to_right), on(at(row, right, 1, 1), to_left)]
        b_other_far = [on(at(other, left, 1, 0), to_right), on(at(other, right, 1, 1), to_left)]
        if split:
            a_right = self.copy(own_a, at(row, col, 0), to_right)
            a_left = self.copy(own_a, at(row, col, 0), to_left)
            a_row = self.copy(own_a, at(row, col, 0), to_row)
            a_far = [on(at(row, left, 0, 0), to_right), on(at(row, right, 0, 1), to_left)]
            a_row_left, a_row_right = on(at(row, left, 0), to_row), on(at(row, right, 0), to_row)
            a_row_far = on(at(row, far, 0), to_row)
        self.mine = pltpu.make_async_copy(own, full.at[row * 4 + col], local_sem)
        first_share = len(self.made)
        own_share = self.copy(own, full.at[row * 4 + col], to_core)

        def share(*where):
            return on(at(*where), to_core)

        self.stages = [
            ([], [b_row, b_right, b_left, self.mine, own_share]),
            ([b_row], [*b_other, share(other, col, 1)]),
            ([b_right, b_left], [*b_far, share(row, left, 1), share(row, right, 1)]),
            (b_other, [*b_other_far, share(other, left, 1), share(other, right, 1)]),
            (b_far, [share(row, far, 1)]),
            (b_other_far, [share(other, far, 1)]),
        ]
        if split:
            of_a = [
                ([], [a_right, a_left, a_row]),
                ([a_right, a_left], [*a_far, a_row_left, a_row_right, share(row, left, 0), share(row, right, 0)]),
                (a_far, [a_row_far, share(row, far, 0)]),
                ([a_row], [share(other, col, 0)]),
                ([a_row_left, a_row_right], [share(other, left, 0), share(other, right, 0)]),
                ([a_row_far], [share(other, far, 0)]),
            ]
            self.stages = [(w + x, t + u) for (w, t), (x, u) in zip(self.stages, of_a)]
        self.shares = self.made[first_share:]
        self.done = 0

    def copy(self, src, dst, to):
        index = len(self.made)
        made = pltpu.make_async_remote_copy(
            src_ref=src,
            dst_ref=dst,
            send_sem=self.sems[0].at[index],
            recv_sem=self.sems[1].at[index],
            device_id=to,
            device_id_type=MESH,
        )
        self.made.append(made)
        return made

    def stage(self):
        if self.done == len(self.stages):
            return
        waits, starts = self.stages[self.done]
        self.done += 1

        @pl.when(self.owner)
        def _():
            for copy in waits:
                copy.wait_recv()
            for copy in starts:
                copy.start()

    def ready(self):
        while self.done < len(self.stages):
            self.stage()

        @pl.when(self.owner)
        def _():
            self.mine.wait()

        @pl.when(jnp.logical_not(self.owner))
        def _():
            for copy in self.shares:
                copy.wait_recv()

    def finish(self):
        @pl.when(self.owner)
        def _():
            for copy in self.made:
                copy.wait_send()


Q_SPLIT = 1024
RIDE_COPIES = 17


def first_body(
    own_ref, vec_ref, first_ref, second_ref, vec_out, later_send, later_recv, send_sems, recv_sems, local_sems
):
    section, row, col = place()
    shard = row * 4 + col
    gathers = [
        Gather(0, Q_SPLIT, own_ref, first_ref, send_sems, recv_sems, local_sems.at[0]),
        Gather(1, Q_SPLIT, own_ref, second_ref, later_send, later_recv, local_sems.at[2]),
    ]
    peers = [
        {"section": lax.rem(section + core, 2), "shard": lax.rem(shard + step, 8)}
        for core in range(2)
        for step in range(8)
        if core + step > 0
    ]
    greet(peers)
    small = []
    for index, peer in enumerate(peers):
        small.append(
            pltpu.make_async_remote_copy(
                src_ref=vec_ref,
                dst_ref=vec_out.at[section, shard],
                send_sem=send_sems.at[GATHER_COPIES + index],
                recv_sem=recv_sems.at[GATHER_COPIES + index],
                device_id=peer,
                device_id_type=MESH,
            )
        )
        small[-1].start()
    own = pltpu.make_async_copy(vec_ref, vec_out.at[section, shard], local_sems.at[1])
    own.start()
    for _ in range(6):
        for gather in gathers:
            gather.stage()
    for gather in gathers:
        gather.ready()
    for copy in small:
        copy.wait_recv()
    for gather in gathers:
        gather.finish()
    for copy in small:
        copy.wait_send()
    own.wait()


def gather_first(own_q, vectors):
    full = jax.ShapeDtypeStruct((8, *own_q.shape), own_q.dtype)
    return call_remote(
        first_body,
        (full, full, jax.ShapeDtypeStruct((2, 8, *vectors.shape), vectors.dtype)),
        GATHER_COPIES + 15,
        0,
        (own_q, vectors),
        scratch=[pltpu.SemaphoreType.DMA((GATHER_COPIES,))] * 2,
        locals_=3,
    )


def span_peers():
    context, tensor = lax.axis_index("context"), lax.axis_index("tensor")
    span = context * 2 + tensor
    peers = []
    for step in range(1, 8):
        peer = lax.rem(span + step, 8)
        peers.append((peer, peer // 2, lax.rem(peer, 2)))
    return context, tensor, span, peers


TOKENS = 128
SPANS = 8
GROUPS = 4
GROUP_HEADS = 3
WIDTH = 768
PAIR = 2 * HEAD_DIM
KV_GROUP = GROUP_HEADS * PAIR
SCALE = 1.0 / math.sqrt(HEAD_DIM)
GELU_A = math.sqrt(2.0 / math.pi)
GELU_B = 0.044715


def dot(first, second):
    return jnp.dot(first, second, preferred_element_type=F32)


def dot_tn(first, second):
    return lax.dot_general(first, second, (((0,), (0,)), ((), ())), preferred_element_type=F32)


def dot_nt(first, second):
    return lax.dot_general(first, second, (((1,), (1,)), ((), ())), preferred_element_type=F32)


def normalised(values):
    centred = values - jnp.mean(values, -1, keepdims=True)
    inverse = lax.rsqrt(jnp.mean(centred * centred, -1, keepdims=True) + EPSILON)
    return centred * inverse, inverse


def norm_pull(values, gain, grad):
    unit, inverse = normalised(values)
    scaled = grad * gain
    along = jnp.mean(scaled * unit, -1, keepdims=True)
    pulled = inverse * (scaled - jnp.mean(scaled, -1, keepdims=True) - unit * along)
    return pulled, jnp.sum(grad * unit, 0, keepdims=True), jnp.sum(grad, 0, keepdims=True)


def gelu(u):
    return 0.5 * u * (1.0 + jnp.tanh(GELU_A * (u + GELU_B * u * u * u)))


def gelu_and_slope(u):
    tanh = jnp.tanh(GELU_A * (u + GELU_B * u * u * u))
    rise = GELU_A * (1.0 + 3.0 * GELU_B * u * u)
    half = 0.5 * (1.0 + tanh)
    return u * half, half + 0.5 * u * (1.0 - tanh * tanh) * rise


def lower_lanes(rows):
    return lax.broadcasted_iota(jnp.int32, (rows, PAIR), 1) < HEAD_DIM


def swapped(value):
    return pltpu.roll(value, HEAD_DIM, 1)


def split_groups(value):
    low = lower_lanes(value.shape[0])
    groups = []
    for base in (0, 384):
        t0, t1, t2 = (value[:, base + 128 * k : base + 128 * (k + 1)] for k in range(3))
        s1, s2 = swapped(t1), swapped(t2)
        groups.append(jnp.concatenate([t0, jnp.where(low, t1, 0.0)], 1))
        groups.append(jnp.concatenate([jnp.where(low, s1, s2), jnp.where(low, s2, 0.0)], 1))
    return groups


def join_groups(groups):
    low = lower_lanes(groups[0].shape[0])
    parts = []
    for first, second in ((groups[0], groups[1]), (groups[2], groups[3])):
        a0, b0, a1, b1 = first[:, :128], first[:, 128:], second[:, :128], second[:, 128:]
        s1 = swapped(a1)
        parts += [a0, jnp.where(low, b0, s1), jnp.where(low, s1, swapped(b1))]
    return jnp.concatenate(parts, 1)


def head_columns(group, at_upper):
    low = lower_lanes(group.shape[0])
    first, last = group[:, :128], group[:, 128:]
    if at_upper:
        return [
            jnp.where(low, 0.0, swapped(first)),
            jnp.where(low, 0.0, first),
            jnp.where(low, 0.0, swapped(last)),
        ]
    return [jnp.where(low, first, 0.0), jnp.where(low, swapped(first), 0.0), jnp.where(low, last, 0.0)]


class Links:
    def __init__(self, send_sems, recv_sems):
        self.send_sems, self.recv_sems, self.sent, self.count = send_sems, recv_sems, [], 0

    def copy(self, src, dst, recv_index, device_id):
        made = pltpu.make_async_remote_copy(
            src_ref=src,
            dst_ref=dst,
            send_sem=self.send_sems.at[self.count],
            recv_sem=self.recv_sems.at[recv_index],
            device_id=device_id,
            device_id_type=MESH,
        )
        self.count += 1
        return made

    def push(self, src, dst, recv_index, device_id, unless=None):
        made = self.copy(src, dst, recv_index, device_id)
        if unless is None:
            made.start()
        else:
            pl.when(jnp.logical_not(unless))(made.start)
        self.sent.append((made, unless))

    def arrived(self, dst, recv_index, unless=None):
        made = pltpu.make_async_remote_copy(
            src_ref=dst,
            dst_ref=dst,
            send_sem=self.send_sems.at[0],
            recv_sem=self.recv_sems.at[recv_index],
            device_id={"tensor": 1 - lax.axis_index("tensor")},
            device_id_type=MESH,
        )
        if unless is None:
            made.wait_recv()
        else:
            pl.when(jnp.logical_not(unless))(made.wait_recv)

    def finish(self):
        for made, unless in self.sent:
            if unless is None:
                made.wait_send()
            else:
                pl.when(jnp.logical_not(unless))(made.wait_send)


KV_AT, Q_AT, O_AT, PAIR_AT = 0, 8, 12, 16
UNITS = 1536
REST = WIDTH + 2 * UNITS
OUT_AT, FC_AT, PROJ_AT = 0, WIDTH, WIDTH + UNITS


def allowed_keys(quarter, tensor, seg_keys, seg_queries):
    keys = 256 * (quarter + 1)
    rows = (2 * quarter + tensor) * TOKENS + lax.broadcasted_iota(jnp.int32, (TOKENS, keys), 0)
    columns = lax.broadcasted_iota(jnp.int32, (TOKENS, keys), 1)
    same = seg_keys[:, :keys] == seg_queries[quarter * TOKENS : (quarter + 1) * TOKENS, :]
    return (columns <= rows) & same


def head_rows(kv_all, quarter, head):
    spans = 2 * (quarter + 1)
    rows = kv_all[0:spans, :, head * PAIR : (head + 1) * PAIR]
    return rows.reshape(spans * TOKENS, PAIR)


def tiles(total, tile, body):
    def step(index, _):
        body(pl.ds(pl.multiple_of(index * tile, tile), tile))
        return 0

    lax.fori_loop(0, total // tile, step, 0)


def forward_body(block, *refs):
    x_ref, segk_ref, segq_ref, norms_ref, wq_ref, own_r = refs[:6]
    refs = refs[6:]
    y_out, *kept_out = refs[:9]
    rest_out, refs = refs[9], refs[10:]
    wq, wr, kvb, kv_all, qb, q_all, ob, o_all, inner, down, down_in = refs[:11]
    a_out, lse_out, mixed_out, resid_out, up_out, act_out = refs[11:17]
    ride_sems = refs[17:23]
    send_sems, recv_sems, local_sems = refs[23:]
    kept = [
        pltpu.make_async_copy(src, dst, local_sems.at[6 + index])
        for index, (src, dst) in enumerate(
            zip((a_out, q_all, kv_all, lse_out, mixed_out, resid_out, inner, up_out), kept_out)
        )
    ]
    keep_a, keep_q, keep_kv, keep_lse, keep_mixed, keep_resid, keep_inner, keep_up = kept

    context, tensor, span, spans = span_peers()
    pieces = []
    for index, (start, size) in enumerate(((OUT_AT, WIDTH), (FC_AT, UNITS), (PROJ_AT, UNITS))):
        at = pl.ds(start, size)
        sems = ride_sems[2 * index : 2 * index + 2]
        pieces.append(Gather(block, 0, own_r.at[:, at], wr.at[:, :, at], *sems, local_sems.at[1 + index]))
    of_out, of_fc, of_proj = pieces

    def ride(*gathers):
        for gather in gathers:
            gather.stage()

    greet([{"context": c, "tensor": t} for _, c, t in spans] + of_out.neighbours)
    load = pltpu.make_async_copy(wq_ref, wq, local_sems.at[0])
    load.start()
    ride(of_out, of_fc)
    links = Links(send_sems, recv_sems)
    peer = {"tensor": 1 - tensor}

    x = x_ref[...].astype(F32)
    unit, _ = normalised(x)
    a_out[...] = (unit * norms_ref[0:1, :] + norms_ref[2:3, :]).astype(BF16)
    keep_a.start()
    load.wait()
    for step in range(1, 5):
        group = lax.rem(context + step, 4)
        columns = pl.ds(pl.multiple_of(WIDTH + group * KV_GROUP, 128), KV_GROUP)
        kvb[group] = dot(a_out[...], wq[:, columns]).astype(BF16)
        links.push(kvb.at[group], kv_all.at[span], KV_AT + span, {"context": group, "tensor": 1 - tensor})
        if step < 4:
            links.push(kvb.at[group], kv_all.at[span], KV_AT + span, {"context": group})
        else:
            kv_all[span] = kvb[group]
    ride(of_out)
    for index, part in enumerate(split_groups(dot(a_out[...], wq[:, :WIDTH]))):
        qb[index] = part.astype(BF16)
    for step in range(1, 4):
        group = lax.rem(context + step, 4)
        links.push(qb.at[group], q_all.at[context], Q_AT + context, {"context": group})
    q_all[context] = qb[context]
    ride(of_fc, of_proj, of_out)

    for quarter in range(GROUPS):
        for index in (2 * quarter, 2 * quarter + 1):
            links.arrived(kv_all.at[index], KV_AT + index, index == span)
        links.arrived(q_all.at[quarter], Q_AT + quarter, quarter == context)
        allowed = allowed_keys(quarter, tensor, segk_ref, segq_ref)
        queries = head_columns(q_all[quarter].astype(F32) * SCALE, False)
        low = lower_lanes(TOKENS)
        outs = []
        for head in range(GROUP_HEADS):
            rows = head_rows(kv_all, quarter, head)
            masked = jnp.where(allowed, dot_nt(queries[head].astype(BF16), rows), MASKED)
            top = jnp.max(masked, -1, keepdims=True)
            weight = jnp.exp(masked - top)
            total = jnp.sum(weight, -1, keepdims=True)
            lse_out[quarter * GROUP_HEADS + head] = top + jnp.log(total)
            outs.append(dot(weight.astype(BF16), rows) * (1.0 / total))
        pair = jnp.where(low, swapped(outs[0]), outs[1])
        last = jnp.where(low, swapped(outs[2]), 0.0)
        ob[quarter] = jnp.concatenate([pair, last], 1).astype(BF16)
        links.push(ob.at[quarter], o_all.at[context], O_AT + context, {"context": quarter}, quarter == context)
        ride(*((of_out, of_fc, of_proj), (of_out, of_fc, of_proj), (of_out, of_fc), (of_proj, of_fc))[quarter])
    o_all[context] = ob[context]
    keep_q.start()
    keep_kv.start()
    keep_lse.start()
    for index in range(GROUPS):
        links.arrived(o_all.at[index], O_AT + index, index == context)
    mixed_out[...] = join_groups([o_all[index].astype(F32) for index in range(GROUPS)]).astype(BF16)
    keep_mixed.start()
    of_out.ready()

    def rest_columns(columns):
        return wr[:, :, columns].reshape(WIDTH, -1)

    resid = x + dot(mixed_out[...], rest_columns(pl.ds(OUT_AT, WIDTH)))
    resid_out[...] = resid
    keep_resid.start()
    unit, _ = normalised(resid)
    inner[0] = (unit * norms_ref[1:2, :] + norms_ref[3:4, :]).astype(BF16)
    links.push(inner.at[0], inner.at[1], PAIR_AT, peer)
    of_fc.ready()
    ride(of_proj)

    def upward(half):
        rows = pl.ds(half * TOKENS, TOKENS)

        def tile(columns):
            up = dot(inner[half], rest_columns(pl.ds(FC_AT + columns.start, columns.size)))
            up_out[rows, columns] = up
            act_out[rows, columns] = gelu(up).astype(BF16)

        tiles(UNITS, 512, tile)

    upward(0)
    ride(of_proj)
    links.arrived(inner.at[1], PAIR_AT)
    upward(1)
    of_proj.ready()
    keep = pltpu.make_async_copy(wr, rest_out, local_sems.at[5])
    keep.start()

    def down_tile(half, shards):
        weights = wr[shards, :, PROJ_AT : PROJ_AT + UNITS].reshape(-1, UNITS)
        return dot_nt(act_out[half * TOKENS : (half + 1) * TOKENS, :], weights)

    for start in (0, 4):
        down[:, start * 96 : start * 96 + 384] = down_tile(1, slice(start, start + 4)).astype(BF16)
    links.push(down, down_in, PAIR_AT + 1, peer)
    keep_inner.start()
    keep_up.start()
    own = resid_out[...] + down_tile(0, slice(None))
    links.arrived(down_in, PAIR_AT + 1)
    y_out[...] = (own + down_in[...].astype(F32)).astype(BF16)
    for gather in pieces:
        gather.finish()
    links.finish()
    for copy in (keep, *kept):
        copy.wait()


def shape(dims, kind=BF16):
    return jax.ShapeDtypeStruct(dims, kind)


def forward_block(block, x, seg_keys, seg_queries, norms, full_q, own_r):
    shards, depth = full_q.shape[:2]
    made = call_remote(
        functools.partial(forward_body, block),
        (
            shape((TOKENS, WIDTH)),
            shape((TOKENS, WIDTH)),
            shape((GROUPS, TOKENS, 256)),
            shape((SPANS, TOKENS, KV_GROUP)),
            shape((GROUPS * GROUP_HEADS, TOKENS, 1), F32),
            shape((TOKENS, WIDTH)),
            shape((TOKENS, WIDTH), F32),
            shape((2, TOKENS, WIDTH)),
            shape((2 * TOKENS, UNITS), F32),
            shape((shards, depth, REST)),
        ),
        20,
        6 + block,
        (x, seg_keys, seg_queries, norms, full_q.reshape(WIDTH, -1), own_r),
        scratch=[
            pltpu.VMEM((WIDTH, 3 * WIDTH), BF16),
            pltpu.VMEM((shards, depth, REST), BF16),
            pltpu.VMEM((GROUPS, TOKENS, KV_GROUP), BF16),
            pltpu.VMEM((SPANS, TOKENS, KV_GROUP), BF16),
            pltpu.VMEM((GROUPS, TOKENS, 256), BF16),
            pltpu.VMEM((GROUPS, TOKENS, 256), BF16),
            pltpu.VMEM((GROUPS, TOKENS, 256), BF16),
            pltpu.VMEM((GROUPS, TOKENS, 256), BF16),
            pltpu.VMEM((2, TOKENS, WIDTH), BF16),
            pltpu.VMEM((TOKENS, WIDTH), BF16),
            pltpu.VMEM((TOKENS, WIDTH), BF16),
            pltpu.VMEM((TOKENS, WIDTH), BF16),
            pltpu.VMEM((GROUPS * GROUP_HEADS, TOKENS, 1), F32),
            pltpu.VMEM((TOKENS, WIDTH), BF16),
            pltpu.VMEM((TOKENS, WIDTH), F32),
            pltpu.VMEM((2 * TOKENS, UNITS), F32),
            pltpu.VMEM((2 * TOKENS, UNITS), BF16),
            *[pltpu.SemaphoreType.DMA((RIDE_COPIES,))] * 6,
        ],
        locals_=14,
        specs=([VMEM] * 4 + [ANY] * 2, (VMEM,) + (ANY,) * 9),
        vmem=60 * 1024 * 1024,
    )
    sent, normed, q_all, kv_all, lse, mixed, resid, inner, up, *weights = made
    inner = inner.reshape(2 * TOKENS, WIDTH)
    return sent, (x, q_all, kv_all, lse, resid, up), (normed, mixed, inner), *weights


BLOCK = 16
HALF = 3 * WIDTH + WIDTH
PART = 3 * HALF // 4
DEPTH = WIDTH // SPANS


def add_rows(dst, terms, rows):
    def step(index, _):
        at = pl.ds(pl.multiple_of(index * BLOCK, BLOCK), BLOCK)
        total = terms[0][at, :].astype(F32)
        for term in terms[1:]:
            total = total + term[at, :].astype(F32)
        dst[at, :] = total.astype(BF16)
        return 0

    lax.fori_loop(0, rows // BLOCK, step, 0)


REDUCE_COPIES = 32
Z_AT, BACK_AT, SHARE_AT = 15, 23, 31
RIDE_BUFFERS = (
    (2, DEPTH, HALF), (3, DEPTH, HALF), (2, DEPTH, HALF),
    (SPANS, DEPTH, HALF // SPANS), (GROUPS, DEPTH, HALF // GROUPS), (DEPTH, HALF),
)
TAIL_BUFFERS = (
    (2, DEPTH, PART), (3, DEPTH, PART), (2, DEPTH, PART),
    (SPANS, DEPTH, HALF // SPANS), (GROUPS, DEPTH, HALF // GROUPS), (DEPTH, HALF),
    (4, DEPTH, HALF - PART), (2, DEPTH // 2, HALF - PART), (2, DEPTH, HALF - PART),
)


class Reduce:
    def __init__(self, core, split, grads, buffers, got, send_sems, recv_sems):
        section, row, col = place()
        self.here = section == core
        self.send_sems, self.recv_sems, self.count = send_sems, recv_sems, 0
        a1, a2, a3, z8, z4, self.res = buffers[:6]
        other = 1 - row
        right, left, far = lax.rem(col + 1, 4), lax.rem(col + 3, 4), lax.rem(col + 2, 4)
        to_right, to_left = {"shard": row * 4 + right}, {"shard": row * 4 + left}
        to_row = {"shard": other * 4 + col}
        context = lax.axis_index("context")
        span = 2 * context + lax.axis_index("tensor")

        def a(a_row, a_col):
            return grads.at[a_row * 4 + a_col, :, pl.ds(0, split)]

        def b(a_row, a_col):
            return grads.at[a_row * 4 + a_col, :, pl.ds(split, HALF - split)]

        a_far_r = self.copy(a(0, far), a1.at[0], to_right)
        a_far_l = self.copy(a(1, far), a1.at[1], to_left)
        a_plain_r = self.copy(a(1, right), a2.at[1], to_right)
        a_plain_l = self.copy(a(0, left), a3.at[0], to_left)
        a_sum_r = self.copy(a1.at[0], a2.at[0], to_right)
        a_sum_l = self.copy(a1.at[1], a3.at[1], to_left)
        a_row = self.copy(a2.at[other], a2.at[2], to_row)
        self.plain = [a_far_r, a_far_l, a_plain_r, a_plain_l, a_sum_r, a_sum_l, a_row]
        a_add_r = (a1.at[0], [a1.at[0], a(0, right)])
        a_add_l = (a1.at[1], [a1.at[1], a(1, left)])
        a_add_other = (a2.at[other], [a2.at[other], a3.at[other], a(other, col)])
        a_add_row = (a2.at[row], [a2.at[row], a3.at[row], a(row, col)])
        a_total = a2.at[row]
        a_add_total = (a_total, [a_total, a2.at[2]])
        if split < HALF:
            b1, b2, b3 = buffers[6:]
            half = DEPTH // 2
            lower, upper = pl.ds(0, half), pl.ds(half, half)
            b_far = self.copy(b(other, far), b1.at[0], to_row)
            b_right = self.copy(b(other, right), b1.at[1], to_row)
            b_left = self.copy(b(other, left), b1.at[2], to_row)
            b_own = self.copy(b(other, col), b1.at[3], to_row)
            b_far_r = self.copy(b1.at[0, lower], b2.at[0], to_right)
            b_far_l = self.copy(b1.at[0, upper], b2.at[1], to_left)
            b_sum_r = self.copy(b1.at[1], b3.at[0], to_right)
            b_sum_l = self.copy(b1.at[2], b3.at[1], to_left)
            self.plain += [b_far, b_right, b_left, b_own, b_far_r, b_far_l, b_sum_r, b_sum_l]
            b_add_far = (b1.at[0], [b1.at[0], b(row, far)])
            b_add_right = (b1.at[1], [b1.at[1], b(row, right)])
            b_add_left = (b1.at[2], [b1.at[2], b(row, left)])
            b_add_lower = (b1.at[1, lower], [b1.at[1, lower], b2.at[0]])
            b_add_upper = (b1.at[2, upper], [b1.at[2, upper], b2.at[1]])
            b_total = b1.at[3]
            b_add_total = (b_total, [b_total, b(row, col), b3.at[0], b3.at[1]])

        count = SPANS if core == 0 else GROUPS
        me, slots = (span, z8) if core == 0 else (context, z4)
        wide = HALF // count
        mine = self.res.at[:, pl.ds(pl.multiple_of(me * wide, 128), wide)]

        def name(t):
            return {"context": t // 2, "tensor": t % 2} if core == 0 else {"context": t}

        pieces, backs, locals_ = [], [], []
        for t in range(count):
            start = t * wide
            src = a_total.at[:, pl.ds(start, wide)] if start < split else b_total.at[:, pl.ds(start - split, wide)]
            away = t != me
            locals_.append((t == me, slots.at[t], src))
            arrival = self.copy(slots.at[t], slots.at[t], name(t), 0, Z_AT + t)
            pieces.append((self.copy(src, slots.at[me], name(t), Z_AT + t, Z_AT + me), arrival, away))
            at = self.res.at[:, pl.ds(start, wide)]
            arrival = self.copy(at, at, name(t), 0, BACK_AT + t)
            backs.append((self.copy(mine, mine, name(t), BACK_AT + t, BACK_AT + me), arrival, away))
        self.pieces, self.backs = pieces, backs
        self.share = None
        if got is not None:
            self.share = self.copy(self.res, got, {"section": 1 - section}, SHARE_AT, SHARE_AT)

        def add(*sums, rows=DEPTH):
            for dst, terms in sums:
                add_rows(dst, terms, rows)

        def start(*copies):
            for copy in copies:
                copy.start()

        def wait(*copies):
            for copy in copies:
                copy.wait_recv()

        def send_pieces(indices):
            for t in indices:
                pl.when(pieces[t][2])(pieces[t][0].start)
                at_home, dst, src = locals_[t]

                @pl.when(at_home)
                def _(dst=dst, src=src):
                    dst[...] = src[...]

        def s0():
            start(a_far_r, a_far_l)
            if split < HALF:
                start(b_far, b_right, b_left, b_own)
                start(a_plain_r, a_plain_l)

        def s1():
            wait(a_far_r)
            add(a_add_r)
            start(a_sum_r)
            wait(a_far_l)
            add(a_add_l)
            start(a_sum_l)
            if split == HALF:
                start(a_plain_r, a_plain_l)

        def s2():
            wait(b_far)
            add(b_add_far)
            start(b_far_r, b_far_l)
            wait(b_right)
            add(b_add_right)
            wait(b_left)
            add(b_add_left)

        def s3():
            wait(a_plain_r, a_plain_l, a_sum_r, a_sum_l)
            add(a_add_other)
            start(a_row)
            add(a_add_row)

        def s4():
            wait(b_far_r)
            add(b_add_lower, rows=DEPTH // 2)
            start(b_sum_r)
            wait(b_far_l)
            add(b_add_upper, rows=DEPTH // 2)
            start(b_sum_l)

        def s5():
            wait(a_row)
            add(a_add_total)
            send_pieces([t for t in range(count) if t * wide < split])

        def s6():
            wait(b_own, b_sum_r, b_sum_l)
            add(b_add_total)
            send_pieces([t for t in range(count) if t * wide >= split])

        def s7():
            for _, arrival, away in pieces:
                pl.when(away)(arrival.wait_recv)
            add_rows(mine, [slots.at[t] for t in range(count)], DEPTH)
            for copy, _, away in backs:
                pl.when(away)(copy.start)

        def s8():
            for _, arrival, away in backs:
                pl.when(away)(arrival.wait_recv)
            if self.share is not None:
                self.share.start()

        self.steps = [s0, s1, s3, s5, s7, s8] if split == HALF else [s0, s1, s2, s3, s4, s5, s6, s7, s8]
        self.done = 0

    def copy(self, src, dst, to, send_index=None, recv_index=None):
        if send_index is None:
            send_index = recv_index = self.count
            self.count += 1
        return pltpu.make_async_remote_copy(
            src_ref=src,
            dst_ref=dst,
            send_sem=self.send_sems.at[send_index],
            recv_sem=self.recv_sems.at[recv_index],
            device_id=to,
            device_id_type=MESH,
        )

    def stage(self, count=1):
        for _ in range(count):
            if self.done < len(self.steps):
                pl.when(self.here)(self.steps[self.done])
                self.done += 1

    def finish(self):
        self.stage(len(self.steps))

        @pl.when(self.here)
        def _():
            for copy in self.plain:
                copy.wait_send()
            for copy, _, away in self.pieces + self.backs:
                pl.when(away)(copy.wait_send)
            if self.share is not None:
                self.share.wait_send()

        if self.share is not None:
            pl.when(jnp.logical_not(self.here))(self.share.wait_recv)


def backward_body(last, *refs):
    dy_ref, x_ref, *saved = refs[:7]
    normed_ref, mixed_ref, inner_ref, segk_ref, segq_ref, norms_ref = refs[7:13]
    wq_ref, wr_ref = refs[13:15]
    refs = refs[15:]
    if last:
        later_ref, vec_ref, first_ref, second_ref = refs[:4]
        mine_out, vec_out, got_out, blocks_out, inputs_out = refs[4:9]
        refs = refs[9:]
    else:
        dx_out, grads, vec_out = refs[:3]
        refs = refs[3:]
    wq, wr, down, down_in, dob, do_all, dqb, dq_all, dkv_sum, dkvb, dkv_all = refs[:11]
    n2, q2, m2, l2, i2, u2, y2, t2, swap_send, swap_recv = refs[11:21]
    fetched = refs[21:26]
    q_ref, kv_ref, lse_ref, resid_ref, up_ref = fetched
    refs = refs[26:]
    if last:
        ride_buffers, refs = refs[: len(RIDE_BUFFERS)], refs[len(RIDE_BUFFERS) :]
        ride_sems, refs = refs[:2], refs[2:]
        grads, dx, vec0, vec_got, vec8, vec64 = refs[:6]
        tail_buffers = refs[6 : 6 + len(TAIL_BUFFERS)]
        late_sems = refs[6 + len(TAIL_BUFFERS) : -3]
    send_sems, recv_sems, local_sems = refs[-3:]

    section, row, col = place()
    shard = row * 4 + col
    context, tensor, span, spans = span_peers()
    span_ids = [{"context": c, "tensor": t} for _, c, t in spans]
    to_core = {"section": 1 - section}
    shard_ids = [{"shard": lax.rem(shard + step, 8)} for step in range(1, 8)] if last else []
    greet(span_ids + [to_core] + shard_ids)
    links = Links(send_sems, recv_sems)
    peer = {"tensor": 1 - tensor}
    own, got = pl.ds(0, TOKENS), pl.ds(TOKENS, TOKENS)
    own2, got2 = pl.ds(0, 2 * TOKENS), pl.ds(2 * TOKENS, 2 * TOKENS)
    y2[own] = dy_ref[...]
    links.push(y2.at[own], y2.at[got], PAIR_AT, peer)
    loads = []
    for index, (start, size) in enumerate(((PROJ_AT, UNITS), (FC_AT, UNITS), (OUT_AT, WIDTH))):
        at = pl.ds(start, size)
        loads.append(pltpu.make_async_copy(wr_ref.at[:, at], wr.at[:, at], local_sems.at[index]))
    loads.append(pltpu.make_async_copy(wq_ref, wq, local_sems.at[3]))
    fetch_q, fetch_kv, fetch_lse, fetch_resid, fetch_up = fetches = [
        pltpu.make_async_copy(src, dst, local_sems.at[6 + index])
        for index, (src, dst) in enumerate(zip(saved, fetched))
    ]
    own_fetches = [
        pltpu.make_async_copy(normed_ref, n2.at[own], local_sems.at[11]),
        pltpu.make_async_copy(mixed_ref, m2.at[own], local_sems.at[12]),
        pltpu.make_async_copy(inner_ref, i2.at[own2], local_sems.at[13]),
    ]
    for load in (loads[0], fetch_up, *loads[1:], *fetches[:4], *own_fetches):
        load.start()

    def moved(src, dst, index, sems=(swap_send, swap_recv)):
        return pltpu.make_async_remote_copy(
            src_ref=src,
            dst_ref=dst,
            send_sem=sems[0].at[index],
            recv_sem=sems[1].at[index],
            device_id=to_core,
            device_id_type=MESH,
        )

    to_first = [
        moved(normed_ref, n2.at[got], 0),
        moved(mixed_ref, m2.at[got], 1),
        moved(l2.at[own], l2.at[got], 2),
        moved(q2.at[own], q2.at[got], 3),
    ]
    to_second = [
        moved(inner_ref, i2.at[got2], 4),
        moved(t2.at[own2], t2.at[got2], 5),
        moved(y2.at[own2], y2.at[got2], 6),
        moved(u2.at[own2], u2.at[got2], 7),
    ]

    def send_first(*which):
        @pl.when(section == 1)
        def _():
            for index in which:
                to_first[index].start()

    def send_second(*which):
        @pl.when(section == 0)
        def _():
            for index in which:
                to_second[index].start()

    riding, tail = [], []
    if last:
        riding = [
            Reduce(0, HALF, later_ref, ride_buffers, got_out, *ride_sems),
            Reduce(1, HALF, later_ref, ride_buffers, None, *ride_sems),
        ]
        tail = [
            Reduce(0, PART, grads, tail_buffers, None, *late_sems[0:2]),
            Reduce(1, PART, grads, tail_buffers, got_out, *late_sems[0:2]),
        ]
        out_sems = late_sems[2:4]
        for_second = [
            moved(second_ref, blocks_out.at[0], 0, out_sems),
            moved(dy_ref, inputs_out.at[0], 1, out_sems),
        ]
        for_first = [
            moved(first_ref, blocks_out.at[1], 0, out_sems),
            moved(dx, inputs_out.at[1], 1, out_sems),
        ]
        kept_second = [
            pltpu.make_async_copy(second_ref, blocks_out.at[1], local_sems.at[4]),
            pltpu.make_async_copy(dy_ref, inputs_out.at[1], local_sems.at[5]),
        ]
        kept_first = [
            pltpu.make_async_copy(first_ref, blocks_out.at[0], local_sems.at[4]),
            pltpu.make_async_copy(dx, inputs_out.at[0], local_sems.at[5]),
        ]

    def stage(reductions, count=1):
        for _ in range(count):
            for reduction in reductions:
                reduction.stage()

    stage(riding)
    send_first(0, 1)
    send_second(0)
    if last:

        @pl.when(section == 0)
        def _():
            for copy in for_second:
                copy.start()
            kept_first[0].start()

        @pl.when(section == 1)
        def _():
            for_first[0].start()
            for copy in kept_second:
                copy.start()

    def product(first, second, start):
        size = second.shape[1]
        for top in (0, 4):
            rows = first[:, top * DEPTH : (top + 4) * DEPTH]

            def tile(columns, top=top, rows=rows):
                part = dot_tn(rows, second[:, columns]).astype(BF16)
                grads[top : top + 4, :, pl.ds(start + columns.start, columns.size)] = part.reshape(
                    4, DEPTH, columns.size
                )

            tiles(size, 768, tile)

    loads[0].wait()
    fetch_up.wait()

    def upward(half):
        rows = pl.ds(half * TOKENS, TOKENS)

        def tile(columns):
            grad = dot(y2[rows], wr[:, pl.ds(PROJ_AT + columns.start, columns.size)])
            value, slope = gelu_and_slope(up_ref[rows, columns])
            u2[rows, columns] = (grad * slope).astype(BF16)
            t2[rows, columns] = value.astype(BF16)

        tiles(UNITS, 512, tile)

    def inner_grad(half, columns):
        return dot_nt(u2[half * TOKENS : (half + 1) * TOKENS, :], wr[columns, FC_AT : FC_AT + UNITS])

    def down_peer(columns):
        down[:, columns] = inner_grad(1, columns).astype(BF16)

    upward(0)
    links.arrived(y2.at[got], PAIR_AT)
    send_second(2)
    upward(1)
    send_second(1, 3)
    loads[1].wait()
    tiles(WIDTH, 256, down_peer)
    links.push(down, down_in, PAIR_AT + 1, peer)
    inner_own = inner_grad(0, slice(None))

    stage(riding)
    links.arrived(down_in, PAIR_AT + 1)
    inner = inner_own + down_in[...].astype(F32)
    fetch_resid.wait()
    pulled, gain_late, bias_late = norm_pull(resid_ref[...], norms_ref[1:2, :], inner)
    resid_grad = dy_ref[...].astype(F32) + pulled
    l2[own] = resid_grad.astype(BF16)
    send_first(2)
    loads[2].wait()
    for index, part in enumerate(split_groups(dot_nt(l2[own], wr[:, OUT_AT : OUT_AT + WIDTH]))):
        dob[index] = part.astype(BF16)
    for step in range(1, 4):
        group = lax.rem(context + step, 4)
        links.push(dob.at[group], do_all.at[context], O_AT + context, {"context": group})
    do_all[context] = dob[context]

    fetch_q.wait()
    fetch_kv.wait()
    fetch_lse.wait()
    low = lower_lanes(TOKENS)
    for quarter in reversed(range(GROUPS)):
        links.arrived(do_all.at[quarter], O_AT + quarter, quarter == context)
        allowed = allowed_keys(quarter, tensor, segk_ref, segq_ref)
        queries = head_columns(q_ref[quarter].astype(F32) * SCALE, False)
        grads_in = head_columns(do_all[quarter].astype(F32), True)
        outs = []
        count = 2 * (quarter + 1)
        for head in range(GROUP_HEADS):
            rows = head_rows(kv_ref, quarter, head)
            query, grad = queries[head].astype(BF16), grads_in[head].astype(BF16)
            masked = jnp.where(allowed, dot_nt(query, rows), MASKED)
            probs = jnp.exp(masked - lse_ref[quarter * GROUP_HEADS + head])
            prob_grad = dot_nt(grad, rows)
            centre = jnp.sum(probs * prob_grad, -1, keepdims=True)
            score_grad = (probs * (prob_grad - centre)).astype(BF16)
            outs.append(dot(score_grad, rows) * SCALE)
            part = dot_tn(score_grad, query) + dot_tn(probs.astype(BF16), grad)
            part = part.reshape(count, TOKENS, PAIR)
            at = slice(head * PAIR, (head + 1) * PAIR)
            if quarter == GROUPS - 1:
                dkv_sum[0:count, :, at] = part
            else:
                dkv_sum[0:count, :, at] += part
        pair = jnp.where(low, outs[0], swapped(outs[1]))
        last_head = jnp.where(low, outs[2], 0.0)
        dqb[quarter] = jnp.concatenate([pair, last_head], 1).astype(BF16)
        links.push(dqb.at[quarter], dq_all.at[context], Q_AT + context, {"context": quarter}, quarter == context)
        for index in (2 * quarter, 2 * quarter + 1):
            dkvb[index] = dkv_sum[index].astype(BF16)
            links.push(
                dkvb.at[index], dkv_all.at[span], KV_AT + span,
                {"context": quarter, "tensor": index - 2 * quarter}, index == span,
            )
    dq_all[context] = dqb[context]
    dkv_all[span] = dkvb[span]
    for index in range(GROUPS):
        links.arrived(dq_all.at[index], Q_AT + index, index == context)
    joined = join_groups([dq_all[index].astype(F32) for index in range(GROUPS)])
    q2[own, :WIDTH] = joined.astype(BF16)
    for index in range(SPANS):
        links.arrived(dkv_all.at[index], KV_AT + index, index == span)
    for group in range(GROUPS):
        total = dkv_all[2 * group].astype(F32) + dkv_all[2 * group + 1].astype(F32)
        at = WIDTH + group * KV_GROUP
        q2[own, at : at + KV_GROUP] = total.astype(BF16)
    send_first(3)
    loads[3].wait()
    normed_grad = dot_nt(q2[own], wq[...])
    pulled, gain_early, bias_early = norm_pull(x_ref[...].astype(F32), norms_ref[0:1, :], normed_grad)
    dx_low = (resid_grad + pulled).astype(BF16)
    vec_here = vec0 if last else vec_out
    for index, vector in enumerate((gain_early, gain_late, bias_early, bias_late)):
        vec_here[index : index + 1, :] = vector
    vec_here[4:8, :] = jnp.zeros((4, WIDTH), F32)
    if last:
        dx[...] = dx_low
        vec_first = moved(vec0, vec_got, 2, out_sems)
        vec_second = moved(vec_ref, vec_got, 2, out_sems)

        @pl.when(section == 0)
        def _():
            kept_first[1].start()
            vec_second.start()

        @pl.when(section == 1)
        def _():
            for_first[1].start()
            vec_first.start()
    else:
        dx_out[...] = dx_low
    stage(riding)

    for fetch in own_fetches:
        fetch.wait()

    @pl.when(section == 0)
    def _():
        for copy in to_first:
            copy.wait_recv()
        product(n2, q2, 0)
        product(m2, l2, 3 * WIDTH)

    @pl.when(section == 1)
    def _():
        for copy in to_second:
            copy.wait_recv()
        product(i2, u2, 0)
        product(y2, t2, UNITS)

    if last:
        stage(tail)
        stage(riding)
        vec_first.wait_recv()
        vec8[shard] = jnp.where(section == 0, vec0[...], vec_ref[...]) + vec_got[...]
        sems = late_sems[4:6]
        sums = []

        def spread(buffer, me, ids, sources, base):
            for index, target in enumerate(ids):
                copy = pltpu.make_async_remote_copy(
                    src_ref=buffer.at[me],
                    dst_ref=buffer.at[me],
                    send_sem=sems[0].at[base + index],
                    recv_sem=sems[1].at[base + index],
                    device_id=target,
                    device_id_type=MESH,
                )
                copy.start()
                sums.append(copy)

        spread(vec8, shard, shard_ids, None, 0)
        stage(tail)
        stage(riding)
        stage(tail)
        stage(riding)
        for copy in sums[:7]:
            copy.wait_recv()
        vec64[span] = jnp.sum(vec8[...], 0)
        spread(vec64, span, span_ids, None, 7)
        stage(tail, 9)
        for copy in sums[7:]:
            copy.wait_recv()
        vec_out[...] = jnp.sum(vec64[...], 0)

        @pl.when(section == 0)
        def _():
            mine_out[...] = tail[0].res[...]

        @pl.when(section == 1)
        def _():
            mine_out[...] = riding[1].res[...]

        for reduction in riding + tail:
            reduction.finish()
        for copy in sums:
            copy.wait_send()
        for_second[0].wait_recv()
        for_second[1].wait_recv()

        @pl.when(section == 0)
        def _():
            for copy in for_second + [vec_second]:
                copy.wait_send()

        @pl.when(section == 1)
        def _():
            for copy in for_first + [vec_first]:
                copy.wait_send()

        for copy in kept_first:
            copy.wait()

    @pl.when(section == 1)
    def _():
        for copy in to_first:
            copy.wait_send()

    @pl.when(section == 0)
    def _():
        for copy in to_second:
            copy.wait_send()

    links.finish()


def backward_block(last, args, weights, extra=()):
    outputs, scratch = (
        (
            shape((DEPTH, HALF)),
            shape((8, WIDTH), F32),
            shape((DEPTH, HALF)),
            shape((2, TOKENS, WIDTH)),
            shape((2, TOKENS, WIDTH)),
        ),
        [
            *[pltpu.VMEM(dims, BF16) for dims in RIDE_BUFFERS],
            *[pltpu.SemaphoreType.DMA((REDUCE_COPIES,))] * 2,
            pltpu.VMEM((SPANS, DEPTH, HALF), BF16),
            pltpu.VMEM((TOKENS, WIDTH), BF16),
            pltpu.VMEM((8, WIDTH), F32),
            pltpu.VMEM((8, WIDTH), F32),
            pltpu.VMEM((SPANS, 8, WIDTH), F32),
            pltpu.VMEM((SPANS, 8, WIDTH), F32),
            *[pltpu.VMEM(dims, BF16) for dims in TAIL_BUFFERS],
            *[pltpu.SemaphoreType.DMA((REDUCE_COPIES,))] * 2,
            *[pltpu.SemaphoreType.DMA((4,))] * 2,
            *[pltpu.SemaphoreType.DMA((14,))] * 2,
        ],
    ) if last else (
        (shape((TOKENS, WIDTH)), shape((SPANS, DEPTH, HALF)), shape((8, WIDTH), F32)),
        [],
    )
    out_specs = (VMEM, VMEM, ANY, ANY, ANY) if last else (VMEM,) * 3
    return call_remote(
        functools.partial(backward_body, last),
        outputs,
        20,
        9 if last else 8,
        (*args, *weights, *extra),
        scratch=[
            pltpu.VMEM((WIDTH, 3 * WIDTH), BF16),
            pltpu.VMEM((WIDTH, REST), BF16),
            pltpu.VMEM((TOKENS, WIDTH), BF16),
            pltpu.VMEM((TOKENS, WIDTH), BF16),
            *[pltpu.VMEM((GROUPS, TOKENS, 256), BF16)] * 4,
            pltpu.VMEM((SPANS, TOKENS, KV_GROUP), F32),
            pltpu.VMEM((SPANS, TOKENS, KV_GROUP), BF16),
            pltpu.VMEM((SPANS, TOKENS, KV_GROUP), BF16),
            pltpu.VMEM((2 * TOKENS, WIDTH), BF16),
            pltpu.VMEM((2 * TOKENS, 3 * WIDTH), BF16),
            pltpu.VMEM((2 * TOKENS, WIDTH), BF16),
            pltpu.VMEM((2 * TOKENS, WIDTH), BF16),
            pltpu.VMEM((4 * TOKENS, WIDTH), BF16),
            pltpu.VMEM((4 * TOKENS, UNITS), BF16),
            pltpu.VMEM((4 * TOKENS, WIDTH), BF16),
            pltpu.VMEM((4 * TOKENS, UNITS), BF16),
            *[pltpu.SemaphoreType.DMA((8,))] * 2,
            pltpu.VMEM((GROUPS, TOKENS, 256), BF16),
            pltpu.VMEM((SPANS, TOKENS, KV_GROUP), BF16),
            pltpu.VMEM((GROUPS * GROUP_HEADS, TOKENS, 1), F32),
            pltpu.VMEM((TOKENS, WIDTH), F32),
            pltpu.VMEM((2 * TOKENS, UNITS), F32),
            *scratch,
        ],
        locals_=14,
        specs=([VMEM] * 2 + [ANY] * 8 + [VMEM] * 3 + [ANY] * 2 + [VMEM] * len(extra), out_specs),
        vmem=60 * 1024 * 1024,
    )


def per_device(
    block_input, cotangent, segment_ids, w_qkv, w_out, w_fc, w_proj, norm_gains, norm_biases
):
    section = lax.axis_index("section")
    tensor = lax.axis_index("tensor")
    tokens, width = block_input.shape[2:]
    units = w_fc.shape[2]
    depth = w_qkv.shape[1]
    heads = width // HEAD_DIM

    pairs = w_qkv[0][:, width:].reshape(depth, 2, heads, HEAD_DIM).transpose(0, 2, 1, 3)
    own_q = jnp.concatenate([w_qkv[0][:, :width], pairs.reshape(depth, 2 * width)], 1)
    own_r = jnp.concatenate([w_out[0], w_fc[0], w_proj[0].T], 1)
    vectors = jnp.concatenate([norm_gains[0], norm_biases[0]], 0)
    vectors = jnp.pad(vectors, ((0, 12), (0, 128 - depth)))
    first_q, second_q, vectors = gather_first(own_q, vectors)
    norms = vectors[:, :, :8, :depth].transpose(0, 2, 1, 3).reshape(2, 8, width).astype(F32)

    def mine(stacked):
        return lax.dynamic_index_in_dim(stacked, section, 0, keepdims=False)

    seg_keys = mine(segment_ids)
    seg_queries = lax.dynamic_index_in_dim(
        seg_keys.reshape(4, 2, tokens), tensor, 1, keepdims=False
    ).reshape(-1, 1)

    entry = mine(block_input)[0]
    first, kept_first, ops_first, rest_first = forward_block(
        0, entry, seg_keys, seg_queries, norms[0], first_q, own_r
    )
    second, kept_second, ops_second, rest_second = forward_block(
        1, first, seg_keys, seg_queries, norms[1], second_q, own_r
    )

    def arguments(block, incoming, kept, operands):
        return (incoming, *kept, *operands, seg_keys, seg_queries, norms[block])

    def flat(*weights):
        return tuple(weight.reshape(width, -1) for weight in weights)

    grad_second, grads_second, vectors_second = backward_block(
        False, arguments(1, mine(cotangent)[0], kept_second, ops_second), flat(second_q, rest_second)
    )
    own_half, vector_grads, other_half, block_outputs, input_grads = backward_block(
        True,
        arguments(0, grad_second, kept_first, ops_first),
        flat(first_q, rest_first),
        (grads_second, vectors_second, first, second),
    )
    out_a = jnp.where(section == 0, own_half, other_half).astype(F32)
    out_b = jnp.where(section == 0, other_half, own_half).astype(F32)
    out_n = lax.dynamic_slice_in_dim(vector_grads, lax.axis_index("shard") * depth, depth, 1)
    pairs = out_a[:, width : 3 * width].reshape(depth, heads, 2, HEAD_DIM).transpose(0, 2, 1, 3)
    out_qkv = jnp.concatenate([out_a[:, :width], pairs.reshape(depth, 2 * width)], 1)
    return (
        block_outputs[None, :, None],
        input_grads[None, :, None],
        out_qkv[None],
        out_a[None, :, 3 * width :],
        out_b[None, :, :units],
        out_b[:, units:].T[None],
        out_n[None, :2],
        out_n[None, 2],
        out_n[None, 3],
    )


def solution(mesh):
    in_specs = (
        P(None, "shard", ("context", "tensor"), None),
        P(None, "shard", ("context", "tensor"), None),
        P(None, "shard", None),
        P("section", "shard", None),
        P("section", "shard", None),
        P("section", "shard", "tensor"),
        P("section", "tensor", "shard"),
        P("section", None, "shard"),
        P("section", None, "shard"),
    )
    out_specs = (
        P("section", None, "shard", ("context", "tensor"), None),
        P("section", None, "shard", ("context", "tensor"), None),
        P("section", "shard", None),
        P("section", "shard", None),
        P("section", "shard", "tensor"),
        P("section", "tensor", "shard"),
        P("section", None, "shard"),
        P("section", "shard"),
        P("section", "shard"),
    )
    return jax.shard_map(
        per_device, mesh=mesh, in_specs=in_specs, out_specs=out_specs, check_vma=False
    )
```

```python
import functools
import math

import jax
import jax.numpy as jnp
from jax import lax
from jax.experimental import pallas as pl
from jax.experimental.pallas import tpu as pltpu
from jax.sharding import PartitionSpec as P

HEAD_DIM = 64
EPSILON = 1e-05
MASKED = -1000000000.0
MESH = pl.DeviceIdType.MESH
BF16 = jnp.bfloat16
F32 = jnp.float32
ANY = pl.BlockSpec(memory_space=pl.ANY)
VMEM = pl.BlockSpec(memory_space=pltpu.VMEM)


class Copies:
    def __init__(self, send_sems, recv_sems):
        self.send_sems, self.recv_sems, self.made = send_sems, recv_sems, []

    def push(self, src, dst, device_id):
        index = len(self.made)
        copy = pltpu.make_async_remote_copy(
            src_ref=src,
            dst_ref=dst,
            send_sem=self.send_sems.at[index],
            recv_sem=self.recv_sems.at[index],
            device_id=device_id,
            device_id_type=MESH,
        )
        copy.start()
        self.made.append(copy)
        return copy

    def finish(self):
        for copy in self.made:
            copy.wait_send()


def greet(peers):
    barrier = pltpu.get_barrier_semaphore()
    for peer in peers:
        pl.semaphore_signal(barrier, inc=1, device_id=peer, device_id_type=MESH)
    pl.semaphore_wait(barrier, len(peers))


def call_remote(body, out_shape, copies, collective_id, args, scratch=(), locals_=1, specs=None, vmem=None):
    in_specs, out_specs = specs if specs else ([ANY] * len(args), jax.tree.map(lambda _: ANY, out_shape))
    return pl.pallas_call(
        body,
        out_shape=out_shape,
        in_specs=in_specs,
        out_specs=out_specs,
        scratch_shapes=[
            *scratch,
            pltpu.SemaphoreType.DMA((copies,)),
            pltpu.SemaphoreType.DMA((copies,)),
            pltpu.SemaphoreType.DMA((locals_,)),
        ],
        compiler_params=pltpu.CompilerParams(
            collective_id=collective_id, has_side_effects=True, vmem_limit_bytes=vmem
        ),
    )(*args)


def place():
    shard = lax.axis_index("shard")
    return lax.axis_index("section"), shard // 4, lax.rem(shard, 4)


GATHER_COPIES = 32


class Gather:
    def __init__(self, block, split, own, full, send_sems, recv_sems, local_sem):
        section, row, col = place()
        self.owner = section == block
        self.sems, self.made = (send_sems, recv_sems), []
        columns, half = own.shape[1], own.shape[0] // 2
        right, left, far = lax.rem(col + 1, 4), lax.rem(col + 3, 4), lax.rem(col + 2, 4)
        other = 1 - row
        to_right = {"shard": row * 4 + right}
        to_left = {"shard": row * 4 + left}
        to_row = {"shard": other * 4 + col}
        to_core = {"section": 1 - section}
        self.neighbours = [to_right, to_left, to_row, to_core]
        parts = (pl.ds(0, split), pl.ds(split, columns - split))
        rows = (pl.ds(0, half), pl.ds(half, half))

        def at(a_row, a_col, part, which=None):
            place_of = full.at[a_row * 4 + a_col]
            return place_of.at[:, parts[part]] if which is None else place_of.at[rows[which], parts[part]]

        def on(ref, to):
            return self.copy(ref, ref, to)

        own_a, own_b = own.at[:, parts[0]], own.at[:, parts[1]]
        b_row = self.copy(own_b, at(row, col, 1), to_row)
        b_right = self.copy(own_b, at(row, col, 1), to_right)
        b_left = self.copy(own_b, at(row, col, 1), to_left)
        b_other = [on(at(other, col, 1), to_right), on(at(other, col, 1), to_left)]
        b_far = [on(at(row, left, 1, 0), to_right), on(at(row, right, 1, 1), to_left)]
        b_other_far = [on(at(other, left, 1, 0), to_right), on(at(other, right, 1, 1), to_left)]
        if split:
            a_right = self.copy(own_a, at(row, col, 0), to_right)
            a_left = self.copy(own_a, at(row, col, 0), to_left)
            a_row = self.copy(own_a, at(row, col, 0), to_row)
            a_far = [on(at(row, left, 0, 0), to_right), on(at(row, right, 0, 1), to_left)]
            a_row_left, a_row_right = on(at(row, left, 0), to_row), on(at(row, right, 0), to_row)
            a_row_far = on(at(row, far, 0), to_row)
        self.mine = pltpu.make_async_copy(own, full.at[row * 4 + col], local_sem)
        first_share = len(self.made)
        own_share = self.copy(own, full.at[row * 4 + col], to_core)

        def share(*where):
            return on(at(*where), to_core)

        self.stages = [
            ([], [b_row, b_right, b_left, self.mine, own_share]),
            ([b_row], [*b_other, share(other, col, 1)]),
            ([b_right, b_left], [*b_far, share(row, left, 1), share(row, right, 1)]),
            (b_other, [*b_other_far, share(other, left, 1), share(other, right, 1)]),
            (b_far, [share(row, far, 1)]),
            (b_other_far, [share(other, far, 1)]),
        ]
        if split:
            of_a = [
                ([], [a_right, a_left, a_row]),
                ([a_right, a_left], [*a_far, a_row_left, a_row_right, share(row, left, 0), share(row, right, 0)]),
                (a_far, [a_row_far, share(row, far, 0)]),
                ([a_row], [share(other, col, 0)]),
                ([a_row_left, a_row_right], [share(other, left, 0), share(other, right, 0)]),
                ([a_row_far], [share(other, far, 0)]),
            ]
            self.stages = [(w + x, t + u) for (w, t), (x, u) in zip(self.stages, of_a)]
        self.shares = self.made[first_share:]
        self.done = 0

    def copy(self, src, dst, to):
        index = len(self.made)
        made = pltpu.make_async_remote_copy(
            src_ref=src,
            dst_ref=dst,
            send_sem=self.sems[0].at[index],
            recv_sem=self.sems[1].at[index],
            device_id=to,
            device_id_type=MESH,
        )
        self.made.append(made)
        return made

    def stage(self):
        if self.done == len(self.stages):
            return
        waits, starts = self.stages[self.done]
        self.done += 1

        @pl.when(self.owner)
        def _():
            for copy in waits:
                copy.wait_recv()
            for copy in starts:
                copy.start()

    def ready(self):
        while self.done < len(self.stages):
            self.stage()

        @pl.when(self.owner)
        def _():
            self.mine.wait()

        @pl.when(jnp.logical_not(self.owner))
        def _():
            for copy in self.shares:
                copy.wait_recv()

    def finish(self):
        @pl.when(self.owner)
        def _():
            for copy in self.made:
                copy.wait_send()


Q_SPLIT = 1024
RIDE_COPIES = 17


def first_body(
    own_ref, vec_ref, first_ref, second_ref, vec_out, later_send, later_recv, send_sems, recv_sems, local_sems
):
    section, row, col = place()
    shard = row * 4 + col
    gathers = [
        Gather(0, Q_SPLIT, own_ref, first_ref, send_sems, recv_sems, local_sems.at[0]),
        Gather(1, Q_SPLIT, own_ref, second_ref, later_send, later_recv, local_sems.at[2]),
    ]
    peers = [
        {"section": lax.rem(section + core, 2), "shard": lax.rem(shard + step, 8)}
        for core in range(2)
        for step in range(8)
        if core + step > 0
    ]
    greet(peers)
    small = []
    for index, peer in enumerate(peers):
        small.append(
            pltpu.make_async_remote_copy(
                src_ref=vec_ref,
                dst_ref=vec_out.at[section, shard],
                send_sem=send_sems.at[GATHER_COPIES + index],
                recv_sem=recv_sems.at[GATHER_COPIES + index],
                device_id=peer,
                device_id_type=MESH,
            )
        )
        small[-1].start()
    own = pltpu.make_async_copy(vec_ref, vec_out.at[section, shard], local_sems.at[1])
    own.start()
    for _ in range(6):
        for gather in gathers:
            gather.stage()
    for gather in gathers:
        gather.ready()
    for copy in small:
        copy.wait_recv()
    for gather in gathers:
        gather.finish()
    for copy in small:
        copy.wait_send()
    own.wait()


def gather_first(own_q, vectors):
    full = jax.ShapeDtypeStruct((8, *own_q.shape), own_q.dtype)
    return call_remote(
        first_body,
        (full, full, jax.ShapeDtypeStruct((2, 8, *vectors.shape), vectors.dtype)),
        GATHER_COPIES + 15,
        0,
        (own_q, vectors),
        scratch=[pltpu.SemaphoreType.DMA((GATHER_COPIES,))] * 2,
        locals_=3,
    )


def span_peers():
    context, tensor = lax.axis_index("context"), lax.axis_index("tensor")
    span = context * 2 + tensor
    peers = []
    for step in range(1, 8):
        peer = lax.rem(span + step, 8)
        peers.append((peer, peer // 2, lax.rem(peer, 2)))
    return context, tensor, span, peers


TOKENS = 128
SPANS = 8
GROUPS = 4
GROUP_HEADS = 3
WIDTH = 768
DEPTH = WIDTH // SPANS
PAIR = 2 * HEAD_DIM
KV_GROUP = GROUP_HEADS * PAIR
SCALE = 1.0 / math.sqrt(HEAD_DIM)
GELU_A = math.sqrt(2.0 / math.pi)
GELU_B = 0.044715


def dot(first, second):
    return jnp.dot(first, second, preferred_element_type=F32)


def dot_tn(first, second):
    return lax.dot_general(first, second, (((0,), (0,)), ((), ())), preferred_element_type=F32)


def dot_nt(first, second):
    return lax.dot_general(first, second, (((1,), (1,)), ((), ())), preferred_element_type=F32)


def normalised(values):
    centred = values - jnp.mean(values, -1, keepdims=True)
    inverse = lax.rsqrt(jnp.mean(centred * centred, -1, keepdims=True) + EPSILON)
    return centred * inverse, inverse


def norm_pull(values, gain, grad):
    unit, inverse = normalised(values)
    scaled = grad * gain
    along = jnp.mean(scaled * unit, -1, keepdims=True)
    pulled = inverse * (scaled - jnp.mean(scaled, -1, keepdims=True) - unit * along)
    return pulled, jnp.sum(grad * unit, 0, keepdims=True), jnp.sum(grad, 0, keepdims=True)


def gelu(u):
    return 0.5 * u * (1.0 + jnp.tanh(GELU_A * (u + GELU_B * u * u * u)))


def gelu_and_slope(u):
    tanh = jnp.tanh(GELU_A * (u + GELU_B * u * u * u))
    rise = GELU_A * (1.0 + 3.0 * GELU_B * u * u)
    half = 0.5 * (1.0 + tanh)
    return u * half, half + 0.5 * u * (1.0 - tanh * tanh) * rise


def lower_lanes(rows):
    return lax.broadcasted_iota(jnp.int32, (rows, PAIR), 1) < HEAD_DIM


def swapped(value):
    return pltpu.roll(value, HEAD_DIM, 1)


def split_groups(value):
    low = lower_lanes(value.shape[0])
    groups = []
    for base in (0, 384):
        t0, t1, t2 = (value[:, base + 128 * k : base + 128 * (k + 1)] for k in range(3))
        s1, s2 = swapped(t1), swapped(t2)
        groups.append(jnp.concatenate([t0, jnp.where(low, t1, 0.0)], 1))
        groups.append(jnp.concatenate([jnp.where(low, s1, s2), jnp.where(low, s2, 0.0)], 1))
    return groups


def join_groups(groups):
    low = lower_lanes(groups[0].shape[0])
    parts = []
    for first, second in ((groups[0], groups[1]), (groups[2], groups[3])):
        a0, b0, a1, b1 = first[:, :128], first[:, 128:], second[:, :128], second[:, 128:]
        s1 = swapped(a1)
        parts += [a0, jnp.where(low, b0, s1), jnp.where(low, s1, swapped(b1))]
    return jnp.concatenate(parts, 1)


def head_columns(group, at_upper):
    low = lower_lanes(group.shape[0])
    first, last = group[:, :128], group[:, 128:]
    if at_upper:
        return [
            jnp.where(low, 0.0, swapped(first)),
            jnp.where(low, 0.0, first),
            jnp.where(low, 0.0, swapped(last)),
        ]
    return [jnp.where(low, first, 0.0), jnp.where(low, swapped(first), 0.0), jnp.where(low, last, 0.0)]


class Links:
    def __init__(self, send_sems, recv_sems):
        self.send_sems, self.recv_sems, self.sent, self.count = send_sems, recv_sems, [], 0

    def copy(self, src, dst, recv_index, device_id):
        made = pltpu.make_async_remote_copy(
            src_ref=src,
            dst_ref=dst,
            send_sem=self.send_sems.at[self.count],
            recv_sem=self.recv_sems.at[recv_index],
            device_id=device_id,
            device_id_type=MESH,
        )
        self.count += 1
        return made

    def push(self, src, dst, recv_index, device_id, unless=None):
        made = self.copy(src, dst, recv_index, device_id)
        if unless is None:
            made.start()
        else:
            pl.when(jnp.logical_not(unless))(made.start)
        self.sent.append((made, unless))

    def arrived(self, dst, recv_index, unless=None):
        made = pltpu.make_async_remote_copy(
            src_ref=dst,
            dst_ref=dst,
            send_sem=self.send_sems.at[0],
            recv_sem=self.recv_sems.at[recv_index],
            device_id={"tensor": 1 - lax.axis_index("tensor")},
            device_id_type=MESH,
        )
        if unless is None:
            made.wait_recv()
        else:
            pl.when(jnp.logical_not(unless))(made.wait_recv)

    def finish(self):
        for made, unless in self.sent:
            if unless is None:
                made.wait_send()
            else:
                pl.when(jnp.logical_not(unless))(made.wait_send)


KV_AT, Q_AT, O_AT, PAIR_AT = 0, 8, 12, 16
UNITS = 1536
REST = WIDTH + 2 * UNITS
OUT_AT, FC_AT, PROJ_AT = 0, WIDTH, WIDTH + UNITS


def allowed_keys(quarter, tensor, seg_keys, seg_queries):
    keys = 256 * (quarter + 1)
    rows = (2 * quarter + tensor) * TOKENS + lax.broadcasted_iota(jnp.int32, (TOKENS, keys), 0)
    columns = lax.broadcasted_iota(jnp.int32, (TOKENS, keys), 1)
    same = seg_keys[:, :keys] == seg_queries[quarter * TOKENS : (quarter + 1) * TOKENS, :]
    return (columns <= rows) & same


def head_rows(kv_all, quarter, head):
    spans = 2 * (quarter + 1)
    rows = kv_all[0:spans, :, head * PAIR : (head + 1) * PAIR]
    return rows.reshape(spans * TOKENS, PAIR)


def tiles(total, tile, body):
    def step(index, _):
        body(pl.ds(pl.multiple_of(index * tile, tile), tile))
        return 0

    lax.fori_loop(0, total // tile, step, 0)


def join_vectors(norms, vectors_ref, block):
    for shard in range(SPANS):
        piece = vectors_ref[block, shard].astype(F32)
        norms[0:4, shard * DEPTH : (shard + 1) * DEPTH] = piece[0:4, :DEPTH]


def forward_body(block, *refs):
    x_ref, segk_ref, segq_ref, vectors_ref, wq_ref, own_r = refs[:6]
    refs = refs[6:]
    y_out, *kept_out = refs[:9]
    rest_out, refs = refs[9], refs[10:]
    wq, wr, kvb, kv_all, qb, q_all, ob, o_all, inner, down, down_in = refs[:11]
    a_out, lse_out, mixed_out, resid_out, up_out, act_out, norms_ref = refs[11:18]
    ride_sems = refs[18:24]
    send_sems, recv_sems, local_sems = refs[24:]
    kept = [
        pltpu.make_async_copy(src, dst, local_sems.at[6 + index])
        for index, (src, dst) in enumerate(
            zip((a_out, q_all, kv_all, lse_out, mixed_out, resid_out, inner, up_out), kept_out)
        )
    ]
    keep_a, keep_q, keep_kv, keep_lse, keep_mixed, keep_resid, keep_inner, keep_up = kept

    context, tensor, span, spans = span_peers()
    pieces = []
    for index, (start, size) in enumerate(((OUT_AT, WIDTH), (FC_AT, UNITS), (PROJ_AT, UNITS))):
        at = pl.ds(start, size)
        sems = ride_sems[2 * index : 2 * index + 2]
        pieces.append(Gather(block, 0, own_r.at[:, at], wr.at[:, :, at], *sems, local_sems.at[1 + index]))
    of_out, of_fc, of_proj = pieces

    def ride(*gathers):
        for gather in gathers:
            gather.stage()

    greet([{"context": c, "tensor": t} for _, c, t in spans] + of_out.neighbours)
    load = pltpu.make_async_copy(wq_ref, wq, local_sems.at[0])
    load.start()
    ride(of_out, of_fc)
    links = Links(send_sems, recv_sems)
    peer = {"tensor": 1 - tensor}

    join_vectors(norms_ref, vectors_ref, block)
    x = x_ref[...].astype(F32)
    unit, _ = normalised(x)
    a_out[...] = (unit * norms_ref[0:1, :] + norms_ref[2:3, :]).astype(BF16)
    keep_a.start()
    load.wait()
    for step in range(1, 5):
        group = lax.rem(context + step, 4)
        columns = pl.ds(pl.multiple_of(WIDTH + group * KV_GROUP, 128), KV_GROUP)
        kvb[group] = dot(a_out[...], wq[:, columns]).astype(BF16)
        links.push(kvb.at[group], kv_all.at[span], KV_AT + span, {"context": group, "tensor": 1 - tensor})
        if step < 4:
            links.push(kvb.at[group], kv_all.at[span], KV_AT + span, {"context": group})
        else:
            kv_all[span] = kvb[group]
    ride(of_out)
    for index, part in enumerate(split_groups(dot(a_out[...], wq[:, :WIDTH]))):
        qb[index] = part.astype(BF16)
    for step in range(1, 4):
        group = lax.rem(context + step, 4)
        links.push(qb.at[group], q_all.at[context], Q_AT + context, {"context": group})
    q_all[context] = qb[context]
    ride(of_fc, of_proj, of_out)

    for quarter in range(GROUPS):
        for index in (2 * quarter, 2 * quarter + 1):
            links.arrived(kv_all.at[index], KV_AT + index, index == span)
        links.arrived(q_all.at[quarter], Q_AT + quarter, quarter == context)
        allowed = allowed_keys(quarter, tensor, segk_ref, segq_ref)
        queries = head_columns(q_all[quarter].astype(F32) * SCALE, False)
        low = lower_lanes(TOKENS)
        outs = []
        for head in range(GROUP_HEADS):
            rows = head_rows(kv_all, quarter, head)
            masked = jnp.where(allowed, dot_nt(queries[head].astype(BF16), rows), MASKED)
            top = jnp.max(masked, -1, keepdims=True)
            weight = jnp.exp(masked - top)
            total = jnp.sum(weight, -1, keepdims=True)
            lse_out[quarter * GROUP_HEADS + head] = top + jnp.log(total)
            outs.append(dot(weight.astype(BF16), rows) * (1.0 / total))
        pair = jnp.where(low, swapped(outs[0]), outs[1])
        last = jnp.where(low, swapped(outs[2]), 0.0)
        ob[quarter] = jnp.concatenate([pair, last], 1).astype(BF16)
        links.push(ob.at[quarter], o_all.at[context], O_AT + context, {"context": quarter}, quarter == context)
        ride(*((of_out, of_fc, of_proj), (of_out, of_fc, of_proj), (of_out, of_fc), (of_proj, of_fc))[quarter])
    o_all[context] = ob[context]
    keep_q.start()
    keep_kv.start()
    keep_lse.start()
    for index in range(GROUPS):
        links.arrived(o_all.at[index], O_AT + index, index == context)
    mixed_out[...] = join_groups([o_all[index].astype(F32) for index in range(GROUPS)]).astype(BF16)
    keep_mixed.start()
    of_out.ready()

    def rest_columns(columns):
        return wr[:, :, columns].reshape(WIDTH, -1)

    resid = x + dot(mixed_out[...], rest_columns(pl.ds(OUT_AT, WIDTH)))
    resid_out[...] = resid
    keep_resid.start()
    unit, _ = normalised(resid)
    inner[0] = (unit * norms_ref[1:2, :] + norms_ref[3:4, :]).astype(BF16)
    links.push(inner.at[0], inner.at[1], PAIR_AT, peer)
    of_fc.ready()
    ride(of_proj)

    def upward(half):
        rows = pl.ds(half * TOKENS, TOKENS)

        def tile(columns):
            up = dot(inner[half], rest_columns(pl.ds(FC_AT + columns.start, columns.size)))
            up_out[rows, columns] = up
            act_out[rows, columns] = gelu(up).astype(BF16)

        tiles(UNITS, 512, tile)

    upward(0)
    ride(of_proj)
    links.arrived(inner.at[1], PAIR_AT)
    upward(1)
    of_proj.ready()
    keep = pltpu.make_async_copy(wr, rest_out, local_sems.at[5])
    keep.start()

    def down_tile(half, shards):
        weights = wr[shards, :, PROJ_AT : PROJ_AT + UNITS].reshape(-1, UNITS)
        return dot_nt(act_out[half * TOKENS : (half + 1) * TOKENS, :], weights)

    for start in (0, 4):
        down[:, start * 96 : start * 96 + 384] = down_tile(1, slice(start, start + 4)).astype(BF16)
    links.push(down, down_in, PAIR_AT + 1, peer)
    keep_inner.start()
    keep_up.start()
    own = resid_out[...] + down_tile(0, slice(None))
    links.arrived(down_in, PAIR_AT + 1)
    y_out[...] = (own + down_in[...].astype(F32)).astype(BF16)
    for gather in pieces:
        gather.finish()
    links.finish()
    for copy in (keep, *kept):
        copy.wait()


def shape(dims, kind=BF16):
    return jax.ShapeDtypeStruct(dims, kind)


def forward_block(block, x, seg_keys, seg_queries, vectors, full_q, own_r):
    shards, depth = full_q.shape[:2]
    made = call_remote(
        functools.partial(forward_body, block),
        (
            shape((TOKENS, WIDTH)),
            shape((TOKENS, WIDTH)),
            shape((GROUPS, TOKENS, 256)),
            shape((SPANS, TOKENS, KV_GROUP)),
            shape((GROUPS * GROUP_HEADS, TOKENS, 1), F32),
            shape((TOKENS, WIDTH)),
            shape((TOKENS, WIDTH), F32),
            shape((2, TOKENS, WIDTH)),
            shape((2 * TOKENS, UNITS), F32),
            shape((shards, depth, REST)),
        ),
        20,
        6 + block,
        (x, seg_keys, seg_queries, vectors, full_q.reshape(WIDTH, -1), own_r),
        scratch=[
            pltpu.VMEM((WIDTH, 3 * WIDTH), BF16),
            pltpu.VMEM((shards, depth, REST), BF16),
            pltpu.VMEM((GROUPS, TOKENS, KV_GROUP), BF16),
            pltpu.VMEM((SPANS, TOKENS, KV_GROUP), BF16),
            pltpu.VMEM((GROUPS, TOKENS, 256), BF16),
            pltpu.VMEM((GROUPS, TOKENS, 256), BF16),
            pltpu.VMEM((GROUPS, TOKENS, 256), BF16),
            pltpu.VMEM((GROUPS, TOKENS, 256), BF16),
            pltpu.VMEM((2, TOKENS, WIDTH), BF16),
            pltpu.VMEM((TOKENS, WIDTH), BF16),
            pltpu.VMEM((TOKENS, WIDTH), BF16),
            pltpu.VMEM((TOKENS, WIDTH), BF16),
            pltpu.VMEM((GROUPS * GROUP_HEADS, TOKENS, 1), F32),
            pltpu.VMEM((TOKENS, WIDTH), BF16),
            pltpu.VMEM((TOKENS, WIDTH), F32),
            pltpu.VMEM((2 * TOKENS, UNITS), F32),
            pltpu.VMEM((2 * TOKENS, UNITS), BF16),
            pltpu.VMEM((8, WIDTH), F32),
            *[pltpu.SemaphoreType.DMA((RIDE_COPIES,))] * 6,
        ],
        locals_=14,
        specs=([VMEM] * 4 + [ANY] * 2, (VMEM,) + (ANY,) * 9),
        vmem=60 * 1024 * 1024,
    )
    sent, normed, q_all, kv_all, lse, mixed, resid, inner, up, *weights = made
    inner = inner.reshape(2 * TOKENS, WIDTH)
    return sent, (x, q_all, kv_all, lse, resid, up), (normed, mixed, inner), *weights


BLOCK = 16
HALF = 3 * WIDTH + WIDTH
PART = HALF // 3


def add_rows(dst, terms, rows):
    def step(index, _):
        at = pl.ds(pl.multiple_of(index * BLOCK, BLOCK), BLOCK)
        total = terms[0][at, :].astype(F32)
        for term in terms[1:]:
            total = total + term[at, :].astype(F32)
        dst[at, :] = total.astype(BF16)
        return 0

    lax.fori_loop(0, rows // BLOCK, step, 0)


REDUCE_COPIES = 48
Z_AT, BACK_AT, SHARE_AT = 15, 23, 31
C_Z_AT, C_BACK_AT, C_PAIR_AT, C_AT = 32, 36, 40, 41
QUARTER = PART // GROUPS
RIDE_BUFFERS = (
    (2, DEPTH, HALF), (3, DEPTH, HALF), (2, DEPTH, HALF),
    (SPANS, DEPTH, HALF // SPANS), (GROUPS, DEPTH, HALF // GROUPS), (DEPTH, HALF),
)
TAIL_BUFFERS = (
    (2, DEPTH, PART), (3, DEPTH, PART), (2, DEPTH, PART),
    (SPANS, DEPTH, 2 * PART // SPANS), (GROUPS, DEPTH, 2 * PART // GROUPS), (DEPTH, HALF),
    (4, DEPTH, PART), (2, DEPTH // 2, PART), (2, DEPTH, PART),
    (GROUPS, SPANS, DEPTH, QUARTER), (SPANS, DEPTH, QUARTER),
    (2, DEPTH, QUARTER), (3, DEPTH, QUARTER), (2, DEPTH, QUARTER), (DEPTH, QUARTER),
)


class Reduce:
    def __init__(self, core, split, grads, buffers, got, send_sems, recv_sems):
        section, row, col = place()
        self.here = section == core
        self.send_sems, self.recv_sems, self.count = send_sems, recv_sems, 0
        a1, a2, a3, z8, z4, self.res = buffers[:6]
        other = 1 - row
        right, left, far = lax.rem(col + 1, 4), lax.rem(col + 3, 4), lax.rem(col + 2, 4)
        to_right, to_left = {"shard": row * 4 + right}, {"shard": row * 4 + left}
        to_row = {"shard": other * 4 + col}
        context = lax.axis_index("context")
        span = 2 * context + lax.axis_index("tensor")

        def a(a_row, a_col):
            return grads.at[a_row * 4 + a_col, :, pl.ds(0, split)]

        def b(a_row, a_col):
            return grads.at[a_row * 4 + a_col, :, pl.ds(split, PART)]

        a_far_r = self.copy(a(0, far), a1.at[0], to_right)
        a_far_l = self.copy(a(1, far), a1.at[1], to_left)
        a_plain_r = self.copy(a(1, right), a2.at[1], to_right)
        a_plain_l = self.copy(a(0, left), a3.at[0], to_left)
        a_sum_r = self.copy(a1.at[0], a2.at[0], to_right)
        a_sum_l = self.copy(a1.at[1], a3.at[1], to_left)
        a_row = self.copy(a2.at[other], a2.at[2], to_row)
        self.plain = [a_far_r, a_far_l, a_plain_r, a_plain_l, a_sum_r, a_sum_l, a_row]
        a_add_r = (a1.at[0], [a1.at[0], a(0, right)])
        a_add_l = (a1.at[1], [a1.at[1], a(1, left)])
        a_add_other = (a2.at[other], [a2.at[other], a3.at[other], a(other, col)])
        a_add_row = (a2.at[row], [a2.at[row], a3.at[row], a(row, col)])
        a_total = a2.at[row]
        a_add_total = (a_total, [a_total, a2.at[2]])
        if split < HALF:
            b1, b2, b3, zc, zs, c1, c2, c3, pair = buffers[6:]
            half = DEPTH // 2
            lower, upper = pl.ds(0, half), pl.ds(half, half)
            b_far = self.copy(b(other, far), b1.at[0], to_row)
            b_right = self.copy(b(other, right), b1.at[1], to_row)
            b_left = self.copy(b(other, left), b1.at[2], to_row)
            b_own = self.copy(b(other, col), b1.at[3], to_row)
            b_far_r = self.copy(b1.at[0, lower], b2.at[0], to_right)
            b_far_l = self.copy(b1.at[0, upper], b2.at[1], to_left)
            b_sum_r = self.copy(b1.at[1], b3.at[0], to_right)
            b_sum_l = self.copy(b1.at[2], b3.at[1], to_left)
            self.plain += [b_far, b_right, b_left, b_own, b_far_r, b_far_l, b_sum_r, b_sum_l]
            b_add_far = (b1.at[0], [b1.at[0], b(row, far)])
            b_add_right = (b1.at[1], [b1.at[1], b(row, right)])
            b_add_left = (b1.at[2], [b1.at[2], b(row, left)])
            b_add_lower = (b1.at[1, lower], [b1.at[1, lower], b2.at[0]])
            b_add_upper = (b1.at[2, upper], [b1.at[2, upper], b2.at[1]])
            b_total = b1.at[3]
            b_add_total = (b_total, [b_total, b(row, col), b3.at[0], b3.at[1]])

        count = SPANS if core == 0 else GROUPS
        me, slots = (span, z8) if core == 0 else (context, z4)
        wide = (HALF if split == HALF else 2 * PART) // count
        mine = self.res.at[:, pl.ds(pl.multiple_of(me * wide, 128), wide)]

        def name(t):
            return {"context": t // 2, "tensor": t % 2} if core == 0 else {"context": t}

        pieces, backs, locals_ = [], [], []
        for t in range(count):
            start = t * wide
            src = a_total.at[:, pl.ds(start, wide)] if start < split else b_total.at[:, pl.ds(start - split, wide)]
            away = t != me
            locals_.append((t == me, slots.at[t], src))
            arrival = self.copy(slots.at[t], slots.at[t], name(t), 0, Z_AT + t)
            pieces.append((self.copy(src, slots.at[me], name(t), Z_AT + t, Z_AT + me), arrival, away))
            at = self.res.at[:, pl.ds(start, wide)]
            arrival = self.copy(at, at, name(t), 0, BACK_AT + t)
            backs.append((self.copy(mine, mine, name(t), BACK_AT + t, BACK_AT + me), arrival, away))
        self.pieces, self.backs = pieces, backs
        if split < HALF:
            base = 2 * PART
            quarter = pl.ds(pl.multiple_of(base + context * QUARTER, 128), QUARTER)
            c_mine = self.res.at[:, quarter]
            c_sent, c_backs = [], []
            for t in range(GROUPS):
                to, away = {"context": t}, t != context
                at = pl.ds(base + t * QUARTER, QUARTER)
                c_sent.append(
                    (
                        self.copy(grads.at[:, :, at], zc.at[context], to, C_Z_AT + t, C_Z_AT + context),
                        self.copy(zc.at[t], zc.at[t], to, 0, C_Z_AT + t),
                        away,
                    )
                )
                c_backs.append(
                    (
                        self.copy(c_mine, c_mine, to, C_BACK_AT + t, C_BACK_AT + context),
                        self.copy(self.res.at[:, at], self.res.at[:, at], to, 0, C_BACK_AT + t),
                        away,
                    )
                )
            steps = (
                (zs.at[far], c1.at[0], to_right),
                (zs.at[4 + far], c1.at[1], to_left),
                (zs.at[4 + right], c2.at[1], to_right),
                (zs.at[left], c3.at[0], to_left),
                (c1.at[0], c2.at[0], to_right),
                (c1.at[1], c3.at[1], to_left),
                (c2.at[other], c2.at[2], to_row),
            )
            c_far_r, c_far_l, c_plain_r, c_plain_l, c_sum_r, c_sum_l, c_row = c_steps = [
                self.copy(src, dst, to, C_AT + index, C_AT + index)
                for index, (src, dst, to) in enumerate(steps)
            ]
            self.plain += c_steps
            self.backs = backs + c_sent + c_backs
            c_add_r = (c1.at[0], [c1.at[0], zs.at[right]])
            c_add_l = (c1.at[1], [c1.at[1], zs.at[4 + left]])
            c_add_other = (c2.at[other], [c2.at[other], c3.at[other], zs.at[other * 4 + col]])
            c_add_row = (c2.at[row], [c2.at[row], c3.at[row], zs.at[row * 4 + col]])
            c_total = c2.at[row]
            c_add_total = (c_total, [c_total, c2.at[2]])
            c_pair = None
            if core == 0:
                peer = {"tensor": 1 - lax.axis_index("tensor")}
                c_pair = self.copy(c_total, pair, peer, C_PAIR_AT, C_PAIR_AT)
                self.plain.append(c_pair)
        self.share = None
        if got is not None:
            self.share = self.copy(self.res, got, {"section": 1 - section}, SHARE_AT, SHARE_AT)

        def add(*sums, rows=DEPTH):
            for dst, terms in sums:
                add_rows(dst, terms, rows)

        def start(*copies):
            for copy in copies:
                copy.start()

        def wait(*copies):
            for copy in copies:
                copy.wait_recv()

        def send_pieces(indices):
            for t in indices:
                pl.when(pieces[t][2])(pieces[t][0].start)
                at_home, dst, src = locals_[t]

                @pl.when(at_home)
                def _(dst=dst, src=src):
                    dst[...] = src[...]

        def s0():
            start(a_far_r, a_far_l)
            if split < HALF:
                start(b_far, b_right, b_left, b_own)
                start(a_plain_r, a_plain_l)
                for copy, _, away in c_sent:
                    pl.when(away)(copy.start)

        def s1():
            wait(a_far_r)
            add(a_add_r)
            start(a_sum_r)
            wait(a_far_l)
            add(a_add_l)
            start(a_sum_l)
            if split == HALF:
                start(a_plain_r, a_plain_l)

        def s2():
            wait(b_far)
            add(b_add_far)
            start(b_far_r, b_far_l)
            wait(b_right)
            add(b_add_right)
            wait(b_left)
            add(b_add_left)

        def s3():
            wait(a_plain_r, a_plain_l, a_sum_r, a_sum_l)
            add(a_add_other)
            start(a_row)
            add(a_add_row)

        def s4():
            wait(b_far_r)
            add(b_add_lower, rows=DEPTH // 2)
            start(b_sum_r)
            wait(b_far_l)
            add(b_add_upper, rows=DEPTH // 2)
            start(b_sum_l)

        def s5():
            wait(a_row)
            add(a_add_total)
            send_pieces([t for t in range(count) if t * wide < split])

        def s6():
            wait(b_own, b_sum_r, b_sum_l)
            add(b_add_total)
            send_pieces([t for t in range(count) if t * wide >= split])

        def s7():
            for _, arrival, away in pieces:
                pl.when(away)(arrival.wait_recv)
            add_rows(mine, [slots.at[t] for t in range(count)], DEPTH)
            for copy, _, away in backs:
                pl.when(away)(copy.start)

        def s8():
            for _, arrival, away in backs:
                pl.when(away)(arrival.wait_recv)

        def s9():
            if self.share is not None:
                self.share.start()

        def k1():
            for _, arrival, away in c_sent:
                pl.when(away)(arrival.wait_recv)
            zc[context] = grads[:, :, quarter]
            for shard in range(SPANS):
                add_rows(zs.at[shard], [zc.at[t, shard] for t in range(GROUPS)], DEPTH)
            start(c_far_r, c_far_l, c_plain_r, c_plain_l)

        def k2():
            wait(c_far_r)
            add(c_add_r)
            start(c_sum_r)
            wait(c_far_l)
            add(c_add_l)
            start(c_sum_l)

        def k3():
            wait(c_plain_r, c_plain_l, c_sum_r, c_sum_l)
            add(c_add_other)
            start(c_row)
            add(c_add_row)

        def k4():
            wait(c_row)
            add(c_add_total)
            if c_pair is not None:
                c_pair.start()

        def k5():
            if c_pair is None:
                add_rows(c_mine, [c_total], DEPTH)
            else:
                wait(c_pair)
                add_rows(c_mine, [c_total, pair], DEPTH)
            for copy, _, away in c_backs:
                pl.when(away)(copy.start)

        def k6():
            for _, arrival, away in c_backs:
                pl.when(away)(arrival.wait_recv)

        self.steps = [s0, s1, s3, s5, s7, s8, s9]
        if split < HALF:
            self.steps = [s0, s1, s2, k1, s3, s4, k2, s5, s6, k3, s7, k4, k5, s8, k6, s9]
        self.done = 0

    def copy(self, src, dst, to, send_index=None, recv_index=None):
        if send_index is None:
            send_index = recv_index = self.count
            self.count += 1
        return pltpu.make_async_remote_copy(
            src_ref=src,
            dst_ref=dst,
            send_sem=self.send_sems.at[send_index],
            recv_sem=self.recv_sems.at[recv_index],
            device_id=to,
            device_id_type=MESH,
        )

    def stage(self, count=1):
        for _ in range(count):
            if self.done < len(self.steps):
                pl.when(self.here)(self.steps[self.done])
                self.done += 1

    def finish(self):
        self.stage(len(self.steps))

        @pl.when(self.here)
        def _():
            for copy in self.plain:
                copy.wait_send()
            for copy, _, away in self.pieces + self.backs:
                pl.when(away)(copy.wait_send)
            if self.share is not None:
                self.share.wait_send()

        if self.share is not None:
            pl.when(jnp.logical_not(self.here))(self.share.wait_recv)


def backward_body(last, *refs):
    dy_ref, x_ref, *saved = refs[:7]
    normed_ref, mixed_ref, inner_ref, segk_ref, segq_ref, vectors_ref = refs[7:13]
    wq_ref, wr_ref = refs[13:15]
    refs = refs[15:]
    if last:
        later_ref, vec_ref, first_ref, second_ref = refs[:4]
        mine_out, vec_out, got_out, blocks_out, inputs_out = refs[4:9]
        refs = refs[9:]
    else:
        dx_out, grads, vec_out = refs[:3]
        refs = refs[3:]
    wq, wr, down, down_in, dob, do_all, dqb, dq_all, dkv_sum, dkvb, dkv_all = refs[:11]
    n2, q2, m2, l2, i2, u2, y2, t2, swap_send, swap_recv = refs[11:21]
    fetched = refs[21:26]
    q_ref, kv_ref, lse_ref, resid_ref, up_ref = fetched
    norms_ref, refs = refs[26], refs[27:]
    join_vectors(norms_ref, vectors_ref, 0 if last else 1)
    if last:
        ride_buffers, refs = refs[: len(RIDE_BUFFERS)], refs[len(RIDE_BUFFERS) :]
        ride_sems, refs = refs[:2], refs[2:]
        grads, dx, vec0, vec_got, vec8, vec64 = refs[:6]
        tail_buffers = refs[6 : 6 + len(TAIL_BUFFERS)]
        late_sems = refs[6 + len(TAIL_BUFFERS) : -3]
    send_sems, recv_sems, local_sems = refs[-3:]

    section, row, col = place()
    shard = row * 4 + col
    context, tensor, span, spans = span_peers()
    span_ids = [{"context": c, "tensor": t} for _, c, t in spans]
    to_core = {"section": 1 - section}
    shard_ids = [{"shard": lax.rem(shard + step, 8)} for step in range(1, 8)] if last else []
    greet(span_ids + [to_core] + shard_ids)
    links = Links(send_sems, recv_sems)
    peer = {"tensor": 1 - tensor}
    own, got = pl.ds(0, TOKENS), pl.ds(TOKENS, TOKENS)
    own2, got2 = pl.ds(0, 2 * TOKENS), pl.ds(2 * TOKENS, 2 * TOKENS)
    y2[own] = dy_ref[...]
    links.push(y2.at[own], y2.at[got], PAIR_AT, peer)
    loads = []
    for index, (start, size) in enumerate(((PROJ_AT, UNITS), (FC_AT, UNITS), (OUT_AT, WIDTH))):
        at = pl.ds(start, size)
        loads.append(pltpu.make_async_copy(wr_ref.at[:, at], wr.at[:, at], local_sems.at[index]))
    loads.append(pltpu.make_async_copy(wq_ref, wq, local_sems.at[3]))
    fetch_q, fetch_kv, fetch_lse, fetch_resid, fetch_up = fetches = [
        pltpu.make_async_copy(src, dst, local_sems.at[6 + index])
        for index, (src, dst) in enumerate(zip(saved, fetched))
    ]
    own_fetches = [
        pltpu.make_async_copy(normed_ref, n2.at[own], local_sems.at[11]),
        pltpu.make_async_copy(mixed_ref, m2.at[own], local_sems.at[12]),
        pltpu.make_async_copy(inner_ref, i2.at[own2], local_sems.at[13]),
    ]
    for load in (loads[0], fetch_up, *loads[1:], *fetches[:4], *own_fetches):
        load.start()

    def moved(src, dst, index, sems=(swap_send, swap_recv)):
        return pltpu.make_async_remote_copy(
            src_ref=src,
            dst_ref=dst,
            send_sem=sems[0].at[index],
            recv_sem=sems[1].at[index],
            device_id=to_core,
            device_id_type=MESH,
        )

    to_first = [
        moved(normed_ref, n2.at[got], 0),
        moved(mixed_ref, m2.at[got], 1),
        moved(l2.at[own], l2.at[got], 2),
        moved(q2.at[own], q2.at[got], 3),
    ]
    to_second = [
        moved(inner_ref, i2.at[got2], 4),
        moved(t2.at[own2], t2.at[got2], 5),
        moved(y2.at[own2], y2.at[got2], 6),
        moved(u2.at[own2], u2.at[got2], 7),
    ]

    def send_first(*which):
        @pl.when(section == 1)
        def _():
            for index in which:
                to_first[index].start()

    def send_second(*which):
        @pl.when(section == 0)
        def _():
            for index in which:
                to_second[index].start()

    riding, tail = [], []
    if last:
        riding = [
            Reduce(0, HALF, later_ref, ride_buffers, got_out, *ride_sems),
            Reduce(1, HALF, later_ref, ride_buffers, None, *ride_sems),
        ]
        tail = [
            Reduce(0, PART, grads, tail_buffers, None, *late_sems[0:2]),
            Reduce(1, PART, grads, tail_buffers, got_out, *late_sems[0:2]),
        ]
        out_sems = late_sems[2:4]
        for_second = [
            moved(second_ref, blocks_out.at[0], 0, out_sems),
            moved(dy_ref, inputs_out.at[0], 1, out_sems),
        ]
        for_first = [
            moved(first_ref, blocks_out.at[1], 0, out_sems),
            moved(dx, inputs_out.at[1], 1, out_sems),
        ]
        kept_second = [
            pltpu.make_async_copy(second_ref, blocks_out.at[1], local_sems.at[4]),
            pltpu.make_async_copy(dy_ref, inputs_out.at[1], local_sems.at[5]),
        ]
        kept_first = [
            pltpu.make_async_copy(first_ref, blocks_out.at[0], local_sems.at[4]),
            pltpu.make_async_copy(dx, inputs_out.at[0], local_sems.at[5]),
        ]

    def stage(reductions, count=1):
        for _ in range(count):
            for reduction in reductions:
                reduction.stage()

    stage(riding)
    send_first(0, 1)
    send_second(0)
    if last:

        @pl.when(section == 0)
        def _():
            for copy in for_second:
                copy.start()
            kept_first[0].start()

        @pl.when(section == 1)
        def _():
            for_first[0].start()
            for copy in kept_second:
                copy.start()

    def product(first, second, start):
        size = second.shape[1]
        for top in (0, 4):
            rows = first[:, top * DEPTH : (top + 4) * DEPTH]

            def tile(columns, top=top, rows=rows):
                part = dot_tn(rows, second[:, columns]).astype(BF16)
                grads[top : top + 4, :, pl.ds(start + columns.start, columns.size)] = part.reshape(
                    4, DEPTH, columns.size
                )

            tiles(size, 768, tile)

    loads[0].wait()
    fetch_up.wait()

    def upward(half):
        rows = pl.ds(half * TOKENS, TOKENS)

        def tile(columns):
            grad = dot(y2[rows], wr[:, pl.ds(PROJ_AT + columns.start, columns.size)])
            value, slope = gelu_and_slope(up_ref[rows, columns])
            u2[rows, columns] = (grad * slope).astype(BF16)
            t2[rows, columns] = value.astype(BF16)

        tiles(UNITS, 512, tile)

    def inner_grad(half, columns):
        return dot_nt(u2[half * TOKENS : (half + 1) * TOKENS, :], wr[columns, FC_AT : FC_AT + UNITS])

    def down_peer(columns):
        down[:, columns] = inner_grad(1, columns).astype(BF16)

    upward(0)
    links.arrived(y2.at[got], PAIR_AT)
    send_second(2)
    upward(1)
    send_second(1, 3)
    loads[1].wait()
    tiles(WIDTH, 256, down_peer)
    links.push(down, down_in, PAIR_AT + 1, peer)
    inner_own = inner_grad(0, slice(None))
    stage(riding)

    def feed_products():
        @pl.when(section == 1)
        def _():
            for copy in to_second:
                copy.wait_recv()
            own_fetches[2].wait()
            product(i2, u2, 0)
            product(y2, t2, UNITS)

    if last:
        feed_products()
        tail[1].stage()
    links.arrived(down_in, PAIR_AT + 1)
    inner = inner_own + down_in[...].astype(F32)
    fetch_resid.wait()
    pulled, gain_late, bias_late = norm_pull(resid_ref[...], norms_ref[1:2, :], inner)
    resid_grad = dy_ref[...].astype(F32) + pulled
    l2[own] = resid_grad.astype(BF16)
    send_first(2)
    loads[2].wait()
    for index, part in enumerate(split_groups(dot_nt(l2[own], wr[:, OUT_AT : OUT_AT + WIDTH]))):
        dob[index] = part.astype(BF16)
    for step in range(1, 4):
        group = lax.rem(context + step, 4)
        links.push(dob.at[group], do_all.at[context], O_AT + context, {"context": group})
    do_all[context] = dob[context]

    fetch_q.wait()
    fetch_kv.wait()
    fetch_lse.wait()
    low = lower_lanes(TOKENS)
    for quarter in reversed(range(GROUPS)):
        links.arrived(do_all.at[quarter], O_AT + quarter, quarter == context)
        allowed = allowed_keys(quarter, tensor, segk_ref, segq_ref)
        queries = head_columns(q_ref[quarter].astype(F32) * SCALE, False)
        grads_in = head_columns(do_all[quarter].astype(F32), True)
        outs = []
        count = 2 * (quarter + 1)
        for head in range(GROUP_HEADS):
            rows = head_rows(kv_ref, quarter, head)
            query, grad = queries[head].astype(BF16), grads_in[head].astype(BF16)
            masked = jnp.where(allowed, dot_nt(query, rows), MASKED)
            probs = jnp.exp(masked - lse_ref[quarter * GROUP_HEADS + head])
            prob_grad = dot_nt(grad, rows)
            centre = jnp.sum(probs * prob_grad, -1, keepdims=True)
            score_grad = (probs * (prob_grad - centre)).astype(BF16)
            outs.append(dot(score_grad, rows) * SCALE)
            part = dot_tn(score_grad, query) + dot_tn(probs.astype(BF16), grad)
            part = part.reshape(count, TOKENS, PAIR)
            at = slice(head * PAIR, (head + 1) * PAIR)
            if quarter == GROUPS - 1:
                dkv_sum[0:count, :, at] = part
            else:
                dkv_sum[0:count, :, at] += part
        pair = jnp.where(low, outs[0], swapped(outs[1]))
        last_head = jnp.where(low, outs[2], 0.0)
        dqb[quarter] = jnp.concatenate([pair, last_head], 1).astype(BF16)
        links.push(dqb.at[quarter], dq_all.at[context], Q_AT + context, {"context": quarter}, quarter == context)
        for index in (2 * quarter, 2 * quarter + 1):
            dkvb[index] = dkv_sum[index].astype(BF16)
            links.push(
                dkvb.at[index], dkv_all.at[span], KV_AT + span,
                {"context": quarter, "tensor": index - 2 * quarter}, index == span,
            )
    dq_all[context] = dqb[context]
    dkv_all[span] = dkvb[span]
    for index in range(GROUPS):
        links.arrived(dq_all.at[index], Q_AT + index, index == context)
    joined = join_groups([dq_all[index].astype(F32) for index in range(GROUPS)])
    q2[own, :WIDTH] = joined.astype(BF16)
    for index in range(SPANS):
        links.arrived(dkv_all.at[index], KV_AT + index, index == span)
    for group in range(GROUPS):
        total = dkv_all[2 * group].astype(F32) + dkv_all[2 * group + 1].astype(F32)
        at = WIDTH + group * KV_GROUP
        q2[own, at : at + KV_GROUP] = total.astype(BF16)
    send_first(3)
    loads[3].wait()
    normed_grad = dot_nt(q2[own], wq[...])
    pulled, gain_early, bias_early = norm_pull(x_ref[...].astype(F32), norms_ref[0:1, :], normed_grad)
    dx_low = (resid_grad + pulled).astype(BF16)
    vec_here = vec0 if last else vec_out
    for index, vector in enumerate((gain_early, gain_late, bias_early, bias_late)):
        vec_here[index : index + 1, :] = vector
    vec_here[4:8, :] = jnp.zeros((4, WIDTH), F32)
    if last:
        dx[...] = dx_low
        vec_first = moved(vec0, vec_got, 2, out_sems)
        vec_second = moved(vec_ref, vec_got, 2, out_sems)

        @pl.when(section == 0)
        def _():
            kept_first[1].start()
            vec_second.start()

        @pl.when(section == 1)
        def _():
            for_first[1].start()
            vec_first.start()
    else:
        dx_out[...] = dx_low
    stage(riding)

    for fetch in own_fetches[:2]:
        fetch.wait()
    pl.when(section == 0)(own_fetches[2].wait)

    @pl.when(section == 0)
    def _():
        for copy in to_first:
            copy.wait_recv()
        product(n2, q2, 0)
        product(m2, l2, 3 * WIDTH)

    if not last:
        feed_products()

    if last:
        tail[0].stage()
        vec_first.wait_recv()
        vec8[shard] = jnp.where(section == 0, vec0[...], vec_ref[...]) + vec_got[...]
        sems = late_sems[4:6]
        sums = []

        def spread(buffer, me, ids, sources, base):
            for index, target in enumerate(ids):
                copy = pltpu.make_async_remote_copy(
                    src_ref=buffer.at[me],
                    dst_ref=buffer.at[me],
                    send_sem=sems[0].at[base + index],
                    recv_sem=sems[1].at[base + index],
                    device_id=target,
                    device_id_type=MESH,
                )
                copy.start()
                sums.append(copy)

        spread(vec8, shard, shard_ids, None, 0)
        stage(tail)
        stage(riding)
        stage(tail)
        for copy in sums[:7]:
            copy.wait_recv()
        vec64[span] = jnp.sum(vec8[...], 0)
        spread(vec64, span, span_ids, None, 7)
        stage(tail, 2)
        stage(riding)
        stage(tail, 5)
        stage(riding, 2)
        stage(tail, 16)
        for copy in sums[7:]:
            copy.wait_recv()
        vec_out[...] = jnp.sum(vec64[...], 0)

        @pl.when(section == 0)
        def _():
            mine_out[...] = tail[0].res[...]

        @pl.when(section == 1)
        def _():
            mine_out[...] = riding[1].res[...]

        for reduction in riding + tail:
            reduction.finish()
        for copy in sums:
            copy.wait_send()
        for_second[0].wait_recv()
        for_second[1].wait_recv()

        @pl.when(section == 0)
        def _():
            for copy in for_second + [vec_second]:
                copy.wait_send()

        @pl.when(section == 1)
        def _():
            for copy in for_first + [vec_first]:
                copy.wait_send()

        for copy in kept_first:
            copy.wait()

    @pl.when(section == 1)
    def _():
        for copy in to_first:
            copy.wait_send()

    @pl.when(section == 0)
    def _():
        for copy in to_second:
            copy.wait_send()

    links.finish()


def backward_block(last, args, weights, extra=()):
    outputs, scratch = (
        (
            shape((DEPTH, HALF)),
            shape((8, WIDTH), F32),
            shape((DEPTH, HALF)),
            shape((2, TOKENS, WIDTH)),
            shape((2, TOKENS, WIDTH)),
        ),
        [
            *[pltpu.VMEM(dims, BF16) for dims in RIDE_BUFFERS],
            *[pltpu.SemaphoreType.DMA((REDUCE_COPIES,))] * 2,
            pltpu.VMEM((SPANS, DEPTH, HALF), BF16),
            pltpu.VMEM((TOKENS, WIDTH), BF16),
            pltpu.VMEM((8, WIDTH), F32),
            pltpu.VMEM((8, WIDTH), F32),
            pltpu.VMEM((SPANS, 8, WIDTH), F32),
            pltpu.VMEM((SPANS, 8, WIDTH), F32),
            *[pltpu.VMEM(dims, BF16) for dims in TAIL_BUFFERS],
            *[pltpu.SemaphoreType.DMA((REDUCE_COPIES,))] * 2,
            *[pltpu.SemaphoreType.DMA((4,))] * 2,
            *[pltpu.SemaphoreType.DMA((14,))] * 2,
        ],
    ) if last else (
        (shape((TOKENS, WIDTH)), shape((SPANS, DEPTH, HALF)), shape((8, WIDTH), F32)),
        [],
    )
    out_specs = (VMEM, VMEM, ANY, ANY, ANY) if last else (VMEM,) * 3
    return call_remote(
        functools.partial(backward_body, last),
        outputs,
        20,
        9 if last else 8,
        (*args, *weights, *extra),
        scratch=[
            pltpu.VMEM((WIDTH, 3 * WIDTH), BF16),
            pltpu.VMEM((WIDTH, REST), BF16),
            pltpu.VMEM((TOKENS, WIDTH), BF16),
            pltpu.VMEM((TOKENS, WIDTH), BF16),
            *[pltpu.VMEM((GROUPS, TOKENS, 256), BF16)] * 4,
            pltpu.VMEM((SPANS, TOKENS, KV_GROUP), F32),
            pltpu.VMEM((SPANS, TOKENS, KV_GROUP), BF16),
            pltpu.VMEM((SPANS, TOKENS, KV_GROUP), BF16),
            pltpu.VMEM((2 * TOKENS, WIDTH), BF16),
            pltpu.VMEM((2 * TOKENS, 3 * WIDTH), BF16),
            pltpu.VMEM((2 * TOKENS, WIDTH), BF16),
            pltpu.VMEM((2 * TOKENS, WIDTH), BF16),
            pltpu.VMEM((4 * TOKENS, WIDTH), BF16),
            pltpu.VMEM((4 * TOKENS, UNITS), BF16),
            pltpu.VMEM((4 * TOKENS, WIDTH), BF16),
            pltpu.VMEM((4 * TOKENS, UNITS), BF16),
            *[pltpu.SemaphoreType.DMA((8,))] * 2,
            pltpu.VMEM((GROUPS, TOKENS, 256), BF16),
            pltpu.VMEM((SPANS, TOKENS, KV_GROUP), BF16),
            pltpu.VMEM((GROUPS * GROUP_HEADS, TOKENS, 1), F32),
            pltpu.VMEM((TOKENS, WIDTH), F32),
            pltpu.VMEM((2 * TOKENS, UNITS), F32),
            pltpu.VMEM((8, WIDTH), F32),
            *scratch,
        ],
        locals_=14,
        specs=([VMEM] * 2 + [ANY] * 8 + [VMEM] * 3 + [ANY] * 2 + [VMEM] * len(extra), out_specs),
        vmem=60 * 1024 * 1024,
    )


def per_device(
    block_input, cotangent, segment_ids, w_qkv, w_out, w_fc, w_proj, norm_gains, norm_biases
):
    section = lax.axis_index("section")
    tensor = lax.axis_index("tensor")
    tokens, width = block_input.shape[2:]
    units = w_fc.shape[2]
    depth = w_qkv.shape[1]
    heads = width // HEAD_DIM

    pairs = w_qkv[0][:, width:].reshape(depth, 2, heads, HEAD_DIM).transpose(0, 2, 1, 3)
    own_q = jnp.concatenate([w_qkv[0][:, :width], pairs.reshape(depth, 2 * width)], 1)
    own_r = jnp.concatenate([w_out[0], w_fc[0], w_proj[0].T], 1)
    vectors = jnp.concatenate([norm_gains[0], norm_biases[0]], 0)
    vectors = jnp.pad(vectors, ((0, 12), (0, 128 - depth)))
    first_q, second_q, vectors = gather_first(own_q, vectors)

    def mine(stacked):
        return lax.dynamic_index_in_dim(stacked, section, 0, keepdims=False)

    seg_keys = mine(segment_ids)
    seg_queries = lax.dynamic_index_in_dim(
        seg_keys.reshape(4, 2, tokens), tensor, 1, keepdims=False
    ).reshape(-1, 1)

    entry = mine(block_input)[0]
    first, kept_first, ops_first, rest_first = forward_block(
        0, entry, seg_keys, seg_queries, vectors, first_q, own_r
    )
    second, kept_second, ops_second, rest_second = forward_block(
        1, first, seg_keys, seg_queries, vectors, second_q, own_r
    )

    def arguments(block, incoming, kept, operands):
        return (incoming, *kept, *operands, seg_keys, seg_queries, vectors)

    def flat(*weights):
        return tuple(weight.reshape(width, -1) for weight in weights)

    grad_second, grads_second, vectors_second = backward_block(
        False, arguments(1, mine(cotangent)[0], kept_second, ops_second), flat(second_q, rest_second)
    )
    own_half, vector_grads, other_half, block_outputs, input_grads = backward_block(
        True,
        arguments(0, grad_second, kept_first, ops_first),
        flat(first_q, rest_first),
        (grads_second, vectors_second, first, second),
    )
    out_a = jnp.where(section == 0, own_half, other_half).astype(F32)
    out_b = jnp.where(section == 0, other_half, own_half).astype(F32)
    out_n = lax.dynamic_slice_in_dim(vector_grads, lax.axis_index("shard") * depth, depth, 1)
    pairs = out_a[:, width : 3 * width].reshape(depth, heads, 2, HEAD_DIM).transpose(0, 2, 1, 3)
    out_qkv = jnp.concatenate([out_a[:, :width], pairs.reshape(depth, 2 * width)], 1)
    return (
        block_outputs[None, :, None],
        input_grads[None, :, None],
        out_qkv[None],
        out_a[None, :, 3 * width :],
        out_b[None, :, :units],
        out_b[:, units:].T[None],
        out_n[None, :2],
        out_n[None, 2],
        out_n[None, 3],
    )


def solution(mesh):
    in_specs = (
        P(None, "shard", ("context", "tensor"), None),
        P(None, "shard", ("context", "tensor"), None),
        P(None, "shard", None),
        P("section", "shard", None),
        P("section", "shard", None),
        P("section", "shard", "tensor"),
        P("section", "tensor", "shard"),
        P("section", None, "shard"),
        P("section", None, "shard"),
    )
    out_specs = (
        P("section", None, "shard", ("context", "tensor"), None),
        P("section", None, "shard", ("context", "tensor"), None),
        P("section", "shard", None),
        P("section", "shard", None),
        P("section", "shard", "tensor"),
        P("section", "tensor", "shard"),
        P("section", None, "shard"),
        P("section", "shard"),
        P("section", "shard"),
    )
    return jax.shard_map(
        per_device, mesh=mesh, in_specs=in_specs, out_specs=out_specs, check_vma=False
    )
```

```python
import functools
import math

import jax
import jax.numpy as jnp
from jax import lax
from jax.experimental import pallas as pl
from jax.experimental.pallas import tpu as pltpu
from jax.sharding import PartitionSpec as P

HEAD_DIM = 64
EPSILON = 1e-05
MASKED = -1000000000.0
MESH = pl.DeviceIdType.MESH
BF16 = jnp.bfloat16
F32 = jnp.float32
ANY = pl.BlockSpec(memory_space=pl.ANY)
VMEM = pl.BlockSpec(memory_space=pltpu.VMEM)


class Copies:
    def __init__(self, send_sems, recv_sems):
        self.send_sems, self.recv_sems, self.made = send_sems, recv_sems, []

    def push(self, src, dst, device_id):
        index = len(self.made)
        copy = pltpu.make_async_remote_copy(
            src_ref=src,
            dst_ref=dst,
            send_sem=self.send_sems.at[index],
            recv_sem=self.recv_sems.at[index],
            device_id=device_id,
            device_id_type=MESH,
        )
        copy.start()
        self.made.append(copy)
        return copy

    def finish(self):
        for copy in self.made:
            copy.wait_send()


def greet(peers):
    barrier = pltpu.get_barrier_semaphore()
    for peer in peers:
        pl.semaphore_signal(barrier, inc=1, device_id=peer, device_id_type=MESH)
    pl.semaphore_wait(barrier, len(peers))


def call_remote(body, out_shape, copies, collective_id, args, scratch=(), locals_=1, specs=None, vmem=None):
    in_specs, out_specs = specs if specs else ([ANY] * len(args), jax.tree.map(lambda _: ANY, out_shape))
    return pl.pallas_call(
        body,
        out_shape=out_shape,
        in_specs=in_specs,
        out_specs=out_specs,
        scratch_shapes=[
            *scratch,
            pltpu.SemaphoreType.DMA((copies,)),
            pltpu.SemaphoreType.DMA((copies,)),
            pltpu.SemaphoreType.DMA((locals_,)),
        ],
        compiler_params=pltpu.CompilerParams(
            collective_id=collective_id, has_side_effects=True, vmem_limit_bytes=vmem
        ),
    )(*args)


def place():
    shard = lax.axis_index("shard")
    return lax.axis_index("section"), shard // 4, lax.rem(shard, 4)


GATHER_COPIES = 32


class Gather:
    def __init__(self, block, split, own, full, send_sems, recv_sems, local_sem):
        section, row, col = place()
        self.owner = section == block
        self.sems, self.made = (send_sems, recv_sems), []
        columns, half = own.shape[1], own.shape[0] // 2
        right, left, far = lax.rem(col + 1, 4), lax.rem(col + 3, 4), lax.rem(col + 2, 4)
        other = 1 - row
        to_right = {"shard": row * 4 + right}
        to_left = {"shard": row * 4 + left}
        to_row = {"shard": other * 4 + col}
        to_core = {"section": 1 - section}
        self.neighbours = [to_right, to_left, to_row, to_core]
        parts = (pl.ds(0, split), pl.ds(split, columns - split))
        rows = (pl.ds(0, half), pl.ds(half, half))

        def at(a_row, a_col, part, which=None):
            place_of = full.at[a_row * 4 + a_col]
            return place_of.at[:, parts[part]] if which is None else place_of.at[rows[which], parts[part]]

        def on(ref, to):
            return self.copy(ref, ref, to)

        own_a, own_b = own.at[:, parts[0]], own.at[:, parts[1]]
        b_row = self.copy(own_b, at(row, col, 1), to_row)
        b_right = self.copy(own_b, at(row, col, 1), to_right)
        b_left = self.copy(own_b, at(row, col, 1), to_left)
        b_other = [on(at(other, col, 1), to_right), on(at(other, col, 1), to_left)]
        b_far = [on(at(row, left, 1, 0), to_right), on(at(row, right, 1, 1), to_left)]
        b_other_far = [on(at(other, left, 1, 0), to_right), on(at(other, right, 1, 1), to_left)]
        if split:
            a_right = self.copy(own_a, at(row, col, 0), to_right)
            a_left = self.copy(own_a, at(row, col, 0), to_left)
            a_row = self.copy(own_a, at(row, col, 0), to_row)
            a_far = [on(at(row, left, 0, 0), to_right), on(at(row, right, 0, 1), to_left)]
            a_row_left, a_row_right = on(at(row, left, 0), to_row), on(at(row, right, 0), to_row)
            a_row_far = on(at(row, far, 0), to_row)
        self.mine = pltpu.make_async_copy(own, full.at[row * 4 + col], local_sem)
        first_share = len(self.made)
        own_share = self.copy(own, full.at[row * 4 + col], to_core)

        def share(*where):
            return on(at(*where), to_core)

        self.stages = [
            ([], [b_row, b_right, b_left, self.mine, own_share]),
            ([b_row], [*b_other, share(other, col, 1)]),
            ([b_right, b_left], [*b_far, share(row, left, 1), share(row, right, 1)]),
            (b_other, [*b_other_far, share(other, left, 1), share(other, right, 1)]),
            (b_far, [share(row, far, 1)]),
            (b_other_far, [share(other, far, 1)]),
        ]
        if split:
            of_a = [
                ([], [a_right, a_left, a_row]),
                ([a_right, a_left], [*a_far, a_row_left, a_row_right, share(row, left, 0), share(row, right, 0)]),
                (a_far, [a_row_far, share(row, far, 0)]),
                ([a_row], [share(other, col, 0)]),
                ([a_row_left, a_row_right], [share(other, left, 0), share(other, right, 0)]),
                ([a_row_far], [share(other, far, 0)]),
            ]
            self.stages = [(w + x, t + u) for (w, t), (x, u) in zip(self.stages, of_a)]
        self.shares = self.made[first_share:]
        self.done = 0

    def copy(self, src, dst, to):
        index = len(self.made)
        made = pltpu.make_async_remote_copy(
            src_ref=src,
            dst_ref=dst,
            send_sem=self.sems[0].at[index],
            recv_sem=self.sems[1].at[index],
            device_id=to,
            device_id_type=MESH,
        )
        self.made.append(made)
        return made

    def stage(self):
        if self.done == len(self.stages):
            return
        waits, starts = self.stages[self.done]
        self.done += 1

        @pl.when(self.owner)
        def _():
            for copy in waits:
                copy.wait_recv()
            for copy in starts:
                copy.start()

    def ready(self):
        while self.done < len(self.stages):
            self.stage()

        @pl.when(self.owner)
        def _():
            self.mine.wait()

        @pl.when(jnp.logical_not(self.owner))
        def _():
            for copy in self.shares:
                copy.wait_recv()

    def finish(self):
        @pl.when(self.owner)
        def _():
            for copy in self.made:
                copy.wait_send()


Q_SPLIT = 1024
RIDE_COPIES = 17


def first_body(
    own_ref, vec_ref, first_ref, second_ref, vec_out, later_send, later_recv, send_sems, recv_sems, local_sems
):
    section, row, col = place()
    shard = row * 4 + col
    gathers = [
        Gather(0, Q_SPLIT, own_ref, first_ref, send_sems, recv_sems, local_sems.at[0]),
        Gather(1, Q_SPLIT, own_ref, second_ref, later_send, later_recv, local_sems.at[2]),
    ]
    peers = [
        {"section": lax.rem(section + core, 2), "shard": lax.rem(shard + step, 8)}
        for core in range(2)
        for step in range(8)
        if core + step > 0
    ]
    greet(peers)
    small = []
    for index, peer in enumerate(peers):
        small.append(
            pltpu.make_async_remote_copy(
                src_ref=vec_ref,
                dst_ref=vec_out.at[section, shard],
                send_sem=send_sems.at[GATHER_COPIES + index],
                recv_sem=recv_sems.at[GATHER_COPIES + index],
                device_id=peer,
                device_id_type=MESH,
            )
        )
        small[-1].start()
    own = pltpu.make_async_copy(vec_ref, vec_out.at[section, shard], local_sems.at[1])
    own.start()
    for _ in range(6):
        for gather in gathers:
            gather.stage()
    for gather in gathers:
        gather.ready()
    for copy in small:
        copy.wait_recv()
    for gather in gathers:
        gather.finish()
    for copy in small:
        copy.wait_send()
    own.wait()


def gather_first(own_q, vectors):
    full = jax.ShapeDtypeStruct((8, *own_q.shape), own_q.dtype)
    return call_remote(
        first_body,
        (full, full, jax.ShapeDtypeStruct((2, 8, *vectors.shape), vectors.dtype)),
        GATHER_COPIES + 15,
        0,
        (own_q, vectors),
        scratch=[pltpu.SemaphoreType.DMA((GATHER_COPIES,))] * 2,
        locals_=3,
    )


def span_peers():
    context, tensor = lax.axis_index("context"), lax.axis_index("tensor")
    span = context * 2 + tensor
    peers = []
    for step in range(1, 8):
        peer = lax.rem(span + step, 8)
        peers.append((peer, peer // 2, lax.rem(peer, 2)))
    return context, tensor, span, peers


TOKENS = 128
SPANS = 8
GROUPS = 4
GROUP_HEADS = 3
WIDTH = 768
DEPTH = WIDTH // SPANS
PAIR = 2 * HEAD_DIM
KV_GROUP = GROUP_HEADS * PAIR
SCALE = 1.0 / math.sqrt(HEAD_DIM)
GELU_A = math.sqrt(2.0 / math.pi)
GELU_B = 0.044715


def dot(first, second):
    return jnp.dot(first, second, preferred_element_type=F32)


def dot_tn(first, second):
    return lax.dot_general(first, second, (((0,), (0,)), ((), ())), preferred_element_type=F32)


def dot_nt(first, second):
    return lax.dot_general(first, second, (((1,), (1,)), ((), ())), preferred_element_type=F32)


def normalised(values):
    centred = values - jnp.mean(values, -1, keepdims=True)
    inverse = lax.rsqrt(jnp.mean(centred * centred, -1, keepdims=True) + EPSILON)
    return centred * inverse, inverse


def norm_pull(values, gain, grad):
    unit, inverse = normalised(values)
    scaled = grad * gain
    along = jnp.mean(scaled * unit, -1, keepdims=True)
    pulled = inverse * (scaled - jnp.mean(scaled, -1, keepdims=True) - unit * along)
    return pulled, jnp.sum(grad * unit, 0, keepdims=True), jnp.sum(grad, 0, keepdims=True)


def gelu(u):
    return 0.5 * u * (1.0 + jnp.tanh(GELU_A * (u + GELU_B * u * u * u)))


def gelu_and_slope(u):
    tanh = jnp.tanh(GELU_A * (u + GELU_B * u * u * u))
    rise = GELU_A * (1.0 + 3.0 * GELU_B * u * u)
    half = 0.5 * (1.0 + tanh)
    return u * half, half + 0.5 * u * (1.0 - tanh * tanh) * rise


def lower_lanes(rows):
    return lax.broadcasted_iota(jnp.int32, (rows, PAIR), 1) < HEAD_DIM


def swapped(value):
    return pltpu.roll(value, HEAD_DIM, 1)


def split_groups(value):
    low = lower_lanes(value.shape[0])
    groups = []
    for base in (0, 384):
        t0, t1, t2 = (value[:, base + 128 * k : base + 128 * (k + 1)] for k in range(3))
        s1, s2 = swapped(t1), swapped(t2)
        groups.append(jnp.concatenate([t0, jnp.where(low, t1, 0.0)], 1))
        groups.append(jnp.concatenate([jnp.where(low, s1, s2), jnp.where(low, s2, 0.0)], 1))
    return groups


def join_groups(groups):
    low = lower_lanes(groups[0].shape[0])
    parts = []
    for first, second in ((groups[0], groups[1]), (groups[2], groups[3])):
        a0, b0, a1, b1 = first[:, :128], first[:, 128:], second[:, :128], second[:, 128:]
        s1 = swapped(a1)
        parts += [a0, jnp.where(low, b0, s1), jnp.where(low, s1, swapped(b1))]
    return jnp.concatenate(parts, 1)


def head_columns(group, at_upper):
    low = lower_lanes(group.shape[0])
    first, last = group[:, :128], group[:, 128:]
    if at_upper:
        return [
            jnp.where(low, 0.0, swapped(first)),
            jnp.where(low, 0.0, first),
            jnp.where(low, 0.0, swapped(last)),
        ]
    return [jnp.where(low, first, 0.0), jnp.where(low, swapped(first), 0.0), jnp.where(low, last, 0.0)]


class Links:
    def __init__(self, send_sems, recv_sems):
        self.send_sems, self.recv_sems, self.sent, self.count = send_sems, recv_sems, [], 0

    def copy(self, src, dst, recv_index, device_id):
        made = pltpu.make_async_remote_copy(
            src_ref=src,
            dst_ref=dst,
            send_sem=self.send_sems.at[self.count],
            recv_sem=self.recv_sems.at[recv_index],
            device_id=device_id,
            device_id_type=MESH,
        )
        self.count += 1
        return made

    def push(self, src, dst, recv_index, device_id, unless=None):
        made = self.copy(src, dst, recv_index, device_id)
        if unless is None:
            made.start()
        else:
            pl.when(jnp.logical_not(unless))(made.start)
        self.sent.append((made, unless))

    def arrived(self, dst, recv_index, unless=None):
        made = pltpu.make_async_remote_copy(
            src_ref=dst,
            dst_ref=dst,
            send_sem=self.send_sems.at[0],
            recv_sem=self.recv_sems.at[recv_index],
            device_id={"tensor": 1 - lax.axis_index("tensor")},
            device_id_type=MESH,
        )
        if unless is None:
            made.wait_recv()
        else:
            pl.when(jnp.logical_not(unless))(made.wait_recv)

    def finish(self):
        for made, unless in self.sent:
            if unless is None:
                made.wait_send()
            else:
                pl.when(jnp.logical_not(unless))(made.wait_send)


KV_AT, Q_AT, O_AT, PAIR_AT = 0, 8, 12, 16
UNITS = 1536
REST = WIDTH + 2 * UNITS
OUT_AT, FC_AT, PROJ_AT = 0, WIDTH, WIDTH + UNITS


def allowed_keys(quarter, tensor, seg_keys, seg_queries):
    keys = 256 * (quarter + 1)
    rows = (2 * quarter + tensor) * TOKENS + lax.broadcasted_iota(jnp.int32, (TOKENS, keys), 0)
    columns = lax.broadcasted_iota(jnp.int32, (TOKENS, keys), 1)
    same = seg_keys[:, :keys] == seg_queries[quarter * TOKENS : (quarter + 1) * TOKENS, :]
    return (columns <= rows) & same


def head_rows(kv_all, quarter, head):
    spans = 2 * (quarter + 1)
    rows = kv_all[0:spans, :, head * PAIR : (head + 1) * PAIR]
    return rows.reshape(spans * TOKENS, PAIR)


def tiles(total, tile, body):
    def step(index, _):
        body(pl.ds(pl.multiple_of(index * tile, tile), tile))
        return 0

    lax.fori_loop(0, total // tile, step, 0)


def join_vectors(norms, vectors_ref, block):
    for shard in range(SPANS):
        piece = vectors_ref[block, shard].astype(F32)
        norms[0:4, shard * DEPTH : (shard + 1) * DEPTH] = piece[0:4, :DEPTH]


def forward_body(block, *refs):
    x_ref, segk_ref, segq_ref, vectors_ref, wq_ref, own_r = refs[:6]
    refs = refs[6:]
    y_out, *kept_out = refs[:9]
    rest_out, refs = refs[9], refs[10:]
    wq, wr, kvb, kv_all, qb, q_all, ob, o_all, inner, down, down_in = refs[:11]
    a_out, lse_out, mixed_out, resid_out, up_out, act_out, norms_ref = refs[11:18]
    ride_sems = refs[18:24]
    send_sems, recv_sems, local_sems = refs[24:]
    kept = [
        pltpu.make_async_copy(src, dst, local_sems.at[6 + index])
        for index, (src, dst) in enumerate(
            zip((a_out, q_all, kv_all, lse_out, mixed_out, resid_out, inner, up_out), kept_out)
        )
    ]
    keep_a, keep_q, keep_kv, keep_lse, keep_mixed, keep_resid, keep_inner, keep_up = kept

    context, tensor, span, spans = span_peers()
    pieces = []
    for index, (start, size) in enumerate(((OUT_AT, WIDTH), (FC_AT, UNITS), (PROJ_AT, UNITS))):
        at = pl.ds(start, size)
        sems = ride_sems[2 * index : 2 * index + 2]
        pieces.append(Gather(block, 0, own_r.at[:, at], wr.at[:, :, at], *sems, local_sems.at[1 + index]))
    of_out, of_fc, of_proj = pieces

    def ride(*gathers):
        for gather in gathers:
            gather.stage()

    greet([{"context": c, "tensor": t} for _, c, t in spans] + of_out.neighbours)
    load = pltpu.make_async_copy(wq_ref, wq, local_sems.at[0])
    load.start()
    ride(of_out, of_fc)
    links = Links(send_sems, recv_sems)
    peer = {"tensor": 1 - tensor}

    join_vectors(norms_ref, vectors_ref, block)
    x = x_ref[...].astype(F32)
    unit, _ = normalised(x)
    a_out[...] = (unit * norms_ref[0:1, :] + norms_ref[2:3, :]).astype(BF16)
    keep_a.start()
    load.wait()
    for step in range(1, 5):
        group = lax.rem(context + step, 4)
        columns = pl.ds(pl.multiple_of(WIDTH + group * KV_GROUP, 128), KV_GROUP)
        kvb[group] = dot(a_out[...], wq[:, columns]).astype(BF16)
        links.push(kvb.at[group], kv_all.at[span], KV_AT + span, {"context": group, "tensor": 1 - tensor})
        if step < 4:
            links.push(kvb.at[group], kv_all.at[span], KV_AT + span, {"context": group})
        else:
            kv_all[span] = kvb[group]
    ride(of_out)
    for index, part in enumerate(split_groups(dot(a_out[...], wq[:, :WIDTH]))):
        qb[index] = part.astype(BF16)
    for step in range(1, 4):
        group = lax.rem(context + step, 4)
        links.push(qb.at[group], q_all.at[context], Q_AT + context, {"context": group})
    q_all[context] = qb[context]
    ride(of_fc, of_proj, of_out)

    for quarter in range(GROUPS):
        for index in (2 * quarter, 2 * quarter + 1):
            links.arrived(kv_all.at[index], KV_AT + index, index == span)
        links.arrived(q_all.at[quarter], Q_AT + quarter, quarter == context)
        allowed = allowed_keys(quarter, tensor, segk_ref, segq_ref)
        queries = head_columns(q_all[quarter].astype(F32) * SCALE, False)
        low = lower_lanes(TOKENS)
        outs = []
        for head in range(GROUP_HEADS):
            rows = head_rows(kv_all, quarter, head)
            masked = jnp.where(allowed, dot_nt(queries[head].astype(BF16), rows), MASKED)
            top = jnp.max(masked, -1, keepdims=True)
            weight = jnp.exp(masked - top)
            total = jnp.sum(weight, -1, keepdims=True)
            lse_out[quarter * GROUP_HEADS + head] = top + jnp.log(total)
            outs.append(dot(weight.astype(BF16), rows) * (1.0 / total))
        pair = jnp.where(low, swapped(outs[0]), outs[1])
        last = jnp.where(low, swapped(outs[2]), 0.0)
        ob[quarter] = jnp.concatenate([pair, last], 1).astype(BF16)
        links.push(ob.at[quarter], o_all.at[context], O_AT + context, {"context": quarter}, quarter == context)
        ride(*((of_out, of_fc, of_proj), (of_out, of_fc, of_proj), (of_out, of_fc), (of_proj, of_fc))[quarter])
    o_all[context] = ob[context]
    keep_q.start()
    keep_kv.start()
    keep_lse.start()
    for index in range(GROUPS):
        links.arrived(o_all.at[index], O_AT + index, index == context)
    mixed_out[...] = join_groups([o_all[index].astype(F32) for index in range(GROUPS)]).astype(BF16)
    keep_mixed.start()
    of_out.ready()

    def rest_columns(columns):
        return wr[:, :, columns].reshape(WIDTH, -1)

    resid = x + dot(mixed_out[...], rest_columns(pl.ds(OUT_AT, WIDTH)))
    resid_out[...] = resid
    keep_resid.start()
    unit, _ = normalised(resid)
    inner[0] = (unit * norms_ref[1:2, :] + norms_ref[3:4, :]).astype(BF16)
    links.push(inner.at[0], inner.at[1], PAIR_AT, peer)
    of_fc.ready()
    ride(of_proj)

    def upward(half):
        rows = pl.ds(half * TOKENS, TOKENS)

        def tile(columns):
            up = dot(inner[half], rest_columns(pl.ds(FC_AT + columns.start, columns.size)))
            up_out[rows, columns] = up
            act_out[rows, columns] = gelu(up).astype(BF16)

        tiles(UNITS, 512, tile)

    upward(0)
    ride(of_proj)
    links.arrived(inner.at[1], PAIR_AT)
    upward(1)
    of_proj.ready()
    keep = pltpu.make_async_copy(wr, rest_out, local_sems.at[5])
    keep.start()

    def down_tile(half, shards):
        weights = wr[shards, :, PROJ_AT : PROJ_AT + UNITS].reshape(-1, UNITS)
        return dot_nt(act_out[half * TOKENS : (half + 1) * TOKENS, :], weights)

    for start in (0, 4):
        down[:, start * 96 : start * 96 + 384] = down_tile(1, slice(start, start + 4)).astype(BF16)
    links.push(down, down_in, PAIR_AT + 1, peer)
    keep_inner.start()
    keep_up.start()
    own = resid_out[...] + down_tile(0, slice(None))
    links.arrived(down_in, PAIR_AT + 1)
    y_out[...] = (own + down_in[...].astype(F32)).astype(BF16)
    for gather in pieces:
        gather.finish()
    links.finish()
    for copy in (keep, *kept):
        copy.wait()


def shape(dims, kind=BF16):
    return jax.ShapeDtypeStruct(dims, kind)


def forward_block(block, x, seg_keys, seg_queries, vectors, full_q, own_r):
    shards, depth = full_q.shape[:2]
    made = call_remote(
        functools.partial(forward_body, block),
        (
            shape((TOKENS, WIDTH)),
            shape((TOKENS, WIDTH)),
            shape((GROUPS, TOKENS, 256)),
            shape((SPANS, TOKENS, KV_GROUP)),
            shape((GROUPS * GROUP_HEADS, TOKENS, 1), F32),
            shape((TOKENS, WIDTH)),
            shape((TOKENS, WIDTH), F32),
            shape((2, TOKENS, WIDTH)),
            shape((2 * TOKENS, UNITS), F32),
            shape((shards, depth, REST)),
        ),
        20,
        6 + block,
        (x, seg_keys, seg_queries, vectors, full_q.reshape(WIDTH, -1), own_r),
        scratch=[
            pltpu.VMEM((WIDTH, 3 * WIDTH), BF16),
            pltpu.VMEM((shards, depth, REST), BF16),
            pltpu.VMEM((GROUPS, TOKENS, KV_GROUP), BF16),
            pltpu.VMEM((SPANS, TOKENS, KV_GROUP), BF16),
            pltpu.VMEM((GROUPS, TOKENS, 256), BF16),
            pltpu.VMEM((GROUPS, TOKENS, 256), BF16),
            pltpu.VMEM((GROUPS, TOKENS, 256), BF16),
            pltpu.VMEM((GROUPS, TOKENS, 256), BF16),
            pltpu.VMEM((2, TOKENS, WIDTH), BF16),
            pltpu.VMEM((TOKENS, WIDTH), BF16),
            pltpu.VMEM((TOKENS, WIDTH), BF16),
            pltpu.VMEM((TOKENS, WIDTH), BF16),
            pltpu.VMEM((GROUPS * GROUP_HEADS, TOKENS, 1), F32),
            pltpu.VMEM((TOKENS, WIDTH), BF16),
            pltpu.VMEM((TOKENS, WIDTH), F32),
            pltpu.VMEM((2 * TOKENS, UNITS), F32),
            pltpu.VMEM((2 * TOKENS, UNITS), BF16),
            pltpu.VMEM((8, WIDTH), F32),
            *[pltpu.SemaphoreType.DMA((RIDE_COPIES,))] * 6,
        ],
        locals_=14,
        specs=([VMEM] * 4 + [ANY] * 2, (VMEM,) + (ANY,) * 9),
        vmem=60 * 1024 * 1024,
    )
    sent, normed, q_all, kv_all, lse, mixed, resid, inner, up, *weights = made
    inner = inner.reshape(2 * TOKENS, WIDTH)
    return sent, (x, q_all, kv_all, lse, resid, up), (normed, mixed, inner), *weights


BLOCK = 16
HALF = 3 * WIDTH + WIDTH
PART = HALF // 3


def add_rows(dst, terms, rows):
    def step(index, _):
        at = pl.ds(pl.multiple_of(index * BLOCK, BLOCK), BLOCK)
        total = terms[0][at, :].astype(F32)
        for term in terms[1:]:
            total = total + term[at, :].astype(F32)
        dst[at, :] = total.astype(BF16)
        return 0

    lax.fori_loop(0, rows // BLOCK, step, 0)


REDUCE_COPIES = 48
Z_AT, BACK_AT, SHARE_AT = 15, 23, 31
C_Z_AT, C_BACK_AT, C_PAIR_AT, C_AT = 32, 36, 40, 41
QUARTER = PART // GROUPS
RIDE_BUFFERS = (
    (2, DEPTH, HALF), (3, DEPTH, HALF), (2, DEPTH, HALF),
    (SPANS, DEPTH, HALF // SPANS), (GROUPS, DEPTH, HALF // GROUPS), (DEPTH, HALF),
)
TAIL_BUFFERS = (
    (GROUPS, 2, DEPTH, PART), (3, DEPTH, PART), (2, BLOCK, 128),
    (SPANS, DEPTH, 2 * PART // SPANS), (GROUPS, DEPTH, 2 * PART // GROUPS), (DEPTH, HALF),
    (4, DEPTH, PART), (2, DEPTH // 2, PART), (2, DEPTH, PART),
    (GROUPS, SPANS, DEPTH, QUARTER), (SPANS, DEPTH, QUARTER),
    (GROUPS, 2, DEPTH, QUARTER), (3, DEPTH, QUARTER), (DEPTH, QUARTER),
)


class Reduce:
    def __init__(self, core, split, grads, buffers, got, send_sems, recv_sems):
        section, row, col = place()
        self.here = section == core
        self.send_sems, self.recv_sems, self.count = send_sems, recv_sems, 0
        a1, a2, a3, z8, z4, self.res = buffers[:6]
        other = 1 - row
        right, left, far = lax.rem(col + 1, 4), lax.rem(col + 3, 4), lax.rem(col + 2, 4)
        to_right, to_left = {"shard": row * 4 + right}, {"shard": row * 4 + left}
        to_row = {"shard": other * 4 + col}
        context = lax.axis_index("context")
        span = 2 * context + lax.axis_index("tensor")

        def a(a_row, a_col):
            return grads.at[a_row * 4 + a_col, :, pl.ds(0, split)]

        def b(a_row, a_col):
            return grads.at[a_row * 4 + a_col, :, pl.ds(split, PART)]

        def across(source, slots):
            copies = []
            for step in (2, 1, 3):
                target = lax.rem(col + step, 4)
                to = {"shard": row * 4 + target}
                copies += [self.copy(source(r, target), slots.at[col, r], to) for r in range(2)]
            return copies

        def gathered(source, slots, a_row):
            return [source(a_row, col)] + [slots.at[lax.rem(col + step, 4), a_row] for step in (1, 2, 3)]

        if split == HALF:
            a_far_r = self.copy(a(0, far), a1.at[0], to_right)
            a_far_l = self.copy(a(1, far), a1.at[1], to_left)
            a_plain_r = self.copy(a(1, right), a2.at[1], to_right)
            a_plain_l = self.copy(a(0, left), a3.at[0], to_left)
            a_sum_r = self.copy(a1.at[0], a2.at[0], to_right)
            a_sum_l = self.copy(a1.at[1], a3.at[1], to_left)
            a_waits = [a_plain_r, a_plain_l, a_sum_r, a_sum_l]
            self.plain = [a_far_r, a_far_l, *a_waits]
            a_add_r = (a1.at[0], [a1.at[0], a(0, right)])
            a_add_l = (a1.at[1], [a1.at[1], a(1, left)])
            a_add_other = (a2.at[other], [a2.at[other], a3.at[other], a(other, col)])
            a_add_row = (a2.at[row], [a2.at[row], a3.at[row], a(row, col)])
        else:
            a_waits = across(a, a1)
            self.plain = list(a_waits)
            a_add_other = (a2.at[other], gathered(a, a1, other))
            a_add_row = (a2.at[row], gathered(a, a1, row))
        a_row = self.copy(a2.at[other], a2.at[2], to_row)
        self.plain.append(a_row)
        a_total = a2.at[row]
        a_add_total = (a_total, [a_total, a2.at[2]])
        if split < HALF:
            b1, b2, b3, zc, zs, c1, c2, pair = buffers[6:]
            half = DEPTH // 2
            lower, upper = pl.ds(0, half), pl.ds(half, half)
            b_far = self.copy(b(other, far), b1.at[0], to_row)
            b_right = self.copy(b(other, right), b1.at[1], to_row)
            b_left = self.copy(b(other, left), b1.at[2], to_row)
            b_own = self.copy(b(other, col), b1.at[3], to_row)
            b_far_r = self.copy(b1.at[0, lower], b2.at[0], to_right)
            b_far_l = self.copy(b1.at[0, upper], b2.at[1], to_left)
            b_sum_r = self.copy(b1.at[1], b3.at[0], to_right)
            b_sum_l = self.copy(b1.at[2], b3.at[1], to_left)
            self.plain += [b_far, b_right, b_left, b_own, b_far_r, b_far_l, b_sum_r, b_sum_l]
            b_add_far = (b1.at[0], [b1.at[0], b(row, far)])
            b_add_right = (b1.at[1], [b1.at[1], b(row, right)])
            b_add_left = (b1.at[2], [b1.at[2], b(row, left)])
            b_add_lower = (b1.at[1, lower], [b1.at[1, lower], b2.at[0]])
            b_add_upper = (b1.at[2, upper], [b1.at[2, upper], b2.at[1]])
            b_total = b1.at[3]
            b_add_total = (b_total, [b_total, b(row, col), b3.at[0], b3.at[1]])

        count = SPANS if core == 0 else GROUPS
        me, slots = (span, z8) if core == 0 else (context, z4)
        wide = (HALF if split == HALF else 2 * PART) // count
        mine = self.res.at[:, pl.ds(pl.multiple_of(me * wide, 128), wide)]

        def name(t):
            return {"context": t // 2, "tensor": t % 2} if core == 0 else {"context": t}

        pieces, backs, locals_ = [], [], []
        for t in range(count):
            start = t * wide
            src = a_total.at[:, pl.ds(start, wide)] if start < split else b_total.at[:, pl.ds(start - split, wide)]
            away = t != me
            locals_.append((t == me, slots.at[t], src))
            arrival = self.copy(slots.at[t], slots.at[t], name(t), 0, Z_AT + t)
            pieces.append((self.copy(src, slots.at[me], name(t), Z_AT + t, Z_AT + me), arrival, away))
            at = self.res.at[:, pl.ds(start, wide)]
            arrival = self.copy(at, at, name(t), 0, BACK_AT + t)
            backs.append((self.copy(mine, mine, name(t), BACK_AT + t, BACK_AT + me), arrival, away))
        self.pieces, self.backs = pieces, backs
        if split < HALF:
            base = 2 * PART
            quarter = pl.ds(pl.multiple_of(base + context * QUARTER, 128), QUARTER)
            c_mine = self.res.at[:, quarter]
            c_sent, c_backs = [], []
            for t in range(GROUPS):
                to, away = {"context": t}, t != context
                at = pl.ds(base + t * QUARTER, QUARTER)
                c_sent.append(
                    (
                        self.copy(grads.at[:, :, at], zc.at[context], to, C_Z_AT + t, C_Z_AT + context),
                        self.copy(zc.at[t], zc.at[t], to, 0, C_Z_AT + t),
                        away,
                    )
                )
                c_backs.append(
                    (
                        self.copy(c_mine, c_mine, to, C_BACK_AT + t, C_BACK_AT + context),
                        self.copy(self.res.at[:, at], self.res.at[:, at], to, 0, C_BACK_AT + t),
                        away,
                    )
                )

            def c(a_row, a_col):
                return zs.at[a_row * 4 + a_col]

            self.count = C_AT
            c_waits = across(c, c1)
            c_row = self.copy(c2.at[other], c2.at[2], to_row)
            self.plain += [*c_waits, c_row]
            self.backs = backs + c_sent + c_backs
            c_add_other = (c2.at[other], gathered(c, c1, other))
            c_add_row = (c2.at[row], gathered(c, c1, row))
            c_total = c2.at[row]
            c_add_total = (c_total, [c_total, c2.at[2]])
            c_pair = None
            if core == 0:
                peer = {"tensor": 1 - lax.axis_index("tensor")}
                c_pair = self.copy(c_total, pair, peer, C_PAIR_AT, C_PAIR_AT)
                self.plain.append(c_pair)
        self.share = None
        if got is not None:
            self.share = self.copy(self.res, got, {"section": 1 - section}, SHARE_AT, SHARE_AT)

        def add(*sums, rows=DEPTH):
            for dst, terms in sums:
                add_rows(dst, terms, rows)

        def start(*copies):
            for copy in copies:
                copy.start()

        def wait(*copies):
            for copy in copies:
                copy.wait_recv()

        def send_pieces(indices):
            for t in indices:
                pl.when(pieces[t][2])(pieces[t][0].start)
                at_home, dst, src = locals_[t]

                @pl.when(at_home)
                def _(dst=dst, src=src):
                    dst[...] = src[...]

        def s0():
            if split == HALF:
                start(a_far_r, a_far_l)
            else:
                start(*a_waits[:2], b_far, b_right, b_left, b_own, *a_waits[2:])
                for copy, _, away in c_sent:
                    pl.when(away)(copy.start)

        def s1():
            wait(a_far_r)
            add(a_add_r)
            start(a_sum_r)
            wait(a_far_l)
            add(a_add_l)
            start(a_sum_l)
            start(a_plain_r, a_plain_l)

        def s2():
            wait(b_far)
            add(b_add_far)
            start(b_far_r, b_far_l)
            wait(b_right)
            add(b_add_right)
            wait(b_left)
            add(b_add_left)

        def s3():
            wait(*a_waits)
            add(a_add_other)
            start(a_row)
            add(a_add_row)

        def s4():
            wait(b_far_r)
            add(b_add_lower, rows=DEPTH // 2)
            start(b_sum_r)
            wait(b_far_l)
            add(b_add_upper, rows=DEPTH // 2)
            start(b_sum_l)

        def s5():
            wait(a_row)
            add(a_add_total)
            send_pieces([t for t in range(count) if t * wide < split])

        def s6():
            wait(b_own, b_sum_r, b_sum_l)
            add(b_add_total)
            send_pieces([t for t in range(count) if t * wide >= split])

        def s7():
            for _, arrival, away in pieces:
                pl.when(away)(arrival.wait_recv)
            add_rows(mine, [slots.at[t] for t in range(count)], DEPTH)
            for copy, _, away in backs:
                pl.when(away)(copy.start)

        def s8():
            for _, arrival, away in backs:
                pl.when(away)(arrival.wait_recv)

        def s9():
            if self.share is not None:
                self.share.start()

        def k1():
            for _, arrival, away in c_sent:
                pl.when(away)(arrival.wait_recv)
            zc[context] = grads[:, :, quarter]
            for shard in range(SPANS):
                add_rows(zs.at[shard], [zc.at[t, shard] for t in range(GROUPS)], DEPTH)
            start(*c_waits)

        def k3():
            wait(*c_waits)
            add(c_add_other)
            start(c_row)
            add(c_add_row)

        def k4():
            wait(c_row)
            add(c_add_total)
            if c_pair is not None:
                c_pair.start()

        def k5():
            if c_pair is None:
                add_rows(c_mine, [c_total], DEPTH)
            else:
                wait(c_pair)
                add_rows(c_mine, [c_total, pair], DEPTH)
            for copy, _, away in c_backs:
                pl.when(away)(copy.start)

        def k6():
            for _, arrival, away in c_backs:
                pl.when(away)(arrival.wait_recv)

        self.steps = [s0, s1, s3, s5, s7, s8, s9]
        if split < HALF:
            self.steps = [s0, s2, s3, k1, s4, s5, s6, k3, s7, k4, k5, s8, k6, s9]
        self.done = 0

    def copy(self, src, dst, to, send_index=None, recv_index=None):
        if send_index is None:
            send_index = recv_index = self.count
            self.count += 1
        return pltpu.make_async_remote_copy(
            src_ref=src,
            dst_ref=dst,
            send_sem=self.send_sems.at[send_index],
            recv_sem=self.recv_sems.at[recv_index],
            device_id=to,
            device_id_type=MESH,
        )

    def stage(self, count=1):
        for _ in range(count):
            if self.done < len(self.steps):
                pl.when(self.here)(self.steps[self.done])
                self.done += 1

    def finish(self):
        self.stage(len(self.steps))

        @pl.when(self.here)
        def _():
            for copy in self.plain:
                copy.wait_send()
            for copy, _, away in self.pieces + self.backs:
                pl.when(away)(copy.wait_send)
            if self.share is not None:
                self.share.wait_send()

        if self.share is not None:
            pl.when(jnp.logical_not(self.here))(self.share.wait_recv)


def backward_body(last, *refs):
    dy_ref, x_ref, *saved = refs[:7]
    normed_ref, mixed_ref, inner_ref, segk_ref, segq_ref, vectors_ref = refs[7:13]
    wq_ref, wr_ref = refs[13:15]
    refs = refs[15:]
    if last:
        later_ref, vec_ref, first_ref, second_ref = refs[:4]
        mine_out, vec_out, got_out, blocks_out, inputs_out = refs[4:9]
        refs = refs[9:]
    else:
        dx_out, grads, vec_out = refs[:3]
        refs = refs[3:]
    wq, wr, down, down_in, dob, do_all, dqb, dq_all, dkv_sum, dkvb, dkv_all = refs[:11]
    n2, q2, m2, l2, i2, u2, y2, t2, swap_send, swap_recv = refs[11:21]
    fetched = refs[21:26]
    q_ref, kv_ref, lse_ref, resid_ref, up_ref = fetched
    norms_ref, refs = refs[26], refs[27:]
    join_vectors(norms_ref, vectors_ref, 0 if last else 1)
    if last:
        ride_buffers, refs = refs[: len(RIDE_BUFFERS)], refs[len(RIDE_BUFFERS) :]
        ride_sems, refs = refs[:2], refs[2:]
        grads, dx, vec0, vec_got, vec8, vec64 = refs[:6]
        tail_buffers = refs[6 : 6 + len(TAIL_BUFFERS)]
        late_sems = refs[6 + len(TAIL_BUFFERS) : -3]
    send_sems, recv_sems, local_sems = refs[-3:]

    section, row, col = place()
    shard = row * 4 + col
    context, tensor, span, spans = span_peers()
    span_ids = [{"context": c, "tensor": t} for _, c, t in spans]
    to_core = {"section": 1 - section}
    shard_ids = [{"shard": lax.rem(shard + step, 8)} for step in range(1, 8)] if last else []
    greet(span_ids + [to_core] + shard_ids)
    links = Links(send_sems, recv_sems)
    peer = {"tensor": 1 - tensor}
    own, got = pl.ds(0, TOKENS), pl.ds(TOKENS, TOKENS)
    own2, got2 = pl.ds(0, 2 * TOKENS), pl.ds(2 * TOKENS, 2 * TOKENS)
    y2[own] = dy_ref[...]
    links.push(y2.at[own], y2.at[got], PAIR_AT, peer)
    loads = []
    for index, (start, size) in enumerate(((PROJ_AT, UNITS), (FC_AT, UNITS), (OUT_AT, WIDTH))):
        at = pl.ds(start, size)
        loads.append(pltpu.make_async_copy(wr_ref.at[:, at], wr.at[:, at], local_sems.at[index]))
    loads.append(pltpu.make_async_copy(wq_ref, wq, local_sems.at[3]))
    fetch_q, fetch_kv, fetch_lse, fetch_resid, fetch_up = fetches = [
        pltpu.make_async_copy(src, dst, local_sems.at[6 + index])
        for index, (src, dst) in enumerate(zip(saved, fetched))
    ]
    own_fetches = [
        pltpu.make_async_copy(normed_ref, n2.at[own], local_sems.at[11]),
        pltpu.make_async_copy(mixed_ref, m2.at[own], local_sems.at[12]),
        pltpu.make_async_copy(inner_ref, i2.at[own2], local_sems.at[13]),
    ]
    for load in (loads[0], fetch_up, *loads[1:], *fetches[:4], *own_fetches):
        load.start()

    def moved(src, dst, index, sems=(swap_send, swap_recv)):
        return pltpu.make_async_remote_copy(
            src_ref=src,
            dst_ref=dst,
            send_sem=sems[0].at[index],
            recv_sem=sems[1].at[index],
            device_id=to_core,
            device_id_type=MESH,
        )

    to_first = [
        moved(normed_ref, n2.at[got], 0),
        moved(mixed_ref, m2.at[got], 1),
        moved(l2.at[own], l2.at[got], 2),
        moved(q2.at[own], q2.at[got], 3),
    ]
    to_second = [
        moved(inner_ref, i2.at[got2], 4),
        moved(t2.at[own2], t2.at[got2], 5),
        moved(y2.at[own2], y2.at[got2], 6),
        moved(u2.at[own2], u2.at[got2], 7),
    ]

    def send_first(*which):
        @pl.when(section == 1)
        def _():
            for index in which:
                to_first[index].start()

    def send_second(*which):
        @pl.when(section == 0)
        def _():
            for index in which:
                to_second[index].start()

    riding, tail = [], []
    if last:
        riding = [
            Reduce(0, HALF, later_ref, ride_buffers, got_out, *ride_sems),
            Reduce(1, HALF, later_ref, ride_buffers, None, *ride_sems),
        ]
        tail = [
            Reduce(0, PART, grads, tail_buffers, None, *late_sems[0:2]),
            Reduce(1, PART, grads, tail_buffers, got_out, *late_sems[0:2]),
        ]
        out_sems = late_sems[2:4]
        for_second = [
            moved(second_ref, blocks_out.at[0], 0, out_sems),
            moved(dy_ref, inputs_out.at[0], 1, out_sems),
        ]
        for_first = [
            moved(first_ref, blocks_out.at[1], 0, out_sems),
            moved(dx, inputs_out.at[1], 1, out_sems),
        ]
        kept_second = [
            pltpu.make_async_copy(second_ref, blocks_out.at[1], local_sems.at[4]),
            pltpu.make_async_copy(dy_ref, inputs_out.at[1], local_sems.at[5]),
        ]
        kept_first = [
            pltpu.make_async_copy(first_ref, blocks_out.at[0], local_sems.at[4]),
            pltpu.make_async_copy(dx, inputs_out.at[0], local_sems.at[5]),
        ]

    def stage(reductions, count=1):
        for _ in range(count):
            for reduction in reductions:
                reduction.stage()

    stage(riding)
    send_first(0, 1)
    send_second(0)
    if last:

        @pl.when(section == 0)
        def _():
            for copy in for_second:
                copy.start()
            kept_first[0].start()

        @pl.when(section == 1)
        def _():
            for_first[0].start()
            for copy in kept_second:
                copy.start()

    def product(first, second, start):
        size = second.shape[1]
        for top in (0, 4):
            rows = first[:, top * DEPTH : (top + 4) * DEPTH]

            def tile(columns, top=top, rows=rows):
                part = dot_tn(rows, second[:, columns]).astype(BF16)
                grads[top : top + 4, :, pl.ds(start + columns.start, columns.size)] = part.reshape(
                    4, DEPTH, columns.size
                )

            tiles(size, 768, tile)

    loads[0].wait()
    fetch_up.wait()

    def upward(half):
        rows = pl.ds(half * TOKENS, TOKENS)

        def tile(columns):
            grad = dot(y2[rows], wr[:, pl.ds(PROJ_AT + columns.start, columns.size)])
            value, slope = gelu_and_slope(up_ref[rows, columns])
            u2[rows, columns] = (grad * slope).astype(BF16)
            t2[rows, columns] = value.astype(BF16)

        tiles(UNITS, 512, tile)

    def inner_grad(half, columns):
        return dot_nt(u2[half * TOKENS : (half + 1) * TOKENS, :], wr[columns, FC_AT : FC_AT + UNITS])

    def down_peer(columns):
        down[:, columns] = inner_grad(1, columns).astype(BF16)

    upward(0)
    links.arrived(y2.at[got], PAIR_AT)
    send_second(2)
    upward(1)
    send_second(1, 3)
    loads[1].wait()
    tiles(WIDTH, 256, down_peer)
    links.push(down, down_in, PAIR_AT + 1, peer)
    inner_own = inner_grad(0, slice(None))
    stage(riding)

    def feed_products():
        @pl.when(section == 1)
        def _():
            for copy in to_second:
                copy.wait_recv()
            own_fetches[2].wait()
            product(i2, u2, 0)
            product(y2, t2, UNITS)

    if last:
        feed_products()
        tail[1].stage()
    links.arrived(down_in, PAIR_AT + 1)
    inner = inner_own + down_in[...].astype(F32)
    fetch_resid.wait()
    pulled, gain_late, bias_late = norm_pull(resid_ref[...], norms_ref[1:2, :], inner)
    resid_grad = dy_ref[...].astype(F32) + pulled
    l2[own] = resid_grad.astype(BF16)
    send_first(2)
    loads[2].wait()
    for index, part in enumerate(split_groups(dot_nt(l2[own], wr[:, OUT_AT : OUT_AT + WIDTH]))):
        dob[index] = part.astype(BF16)
    for step in range(1, 4):
        group = lax.rem(context + step, 4)
        links.push(dob.at[group], do_all.at[context], O_AT + context, {"context": group})
    do_all[context] = dob[context]

    fetch_q.wait()
    fetch_kv.wait()
    fetch_lse.wait()
    low = lower_lanes(TOKENS)
    for quarter in reversed(range(GROUPS)):
        links.arrived(do_all.at[quarter], O_AT + quarter, quarter == context)
        allowed = allowed_keys(quarter, tensor, segk_ref, segq_ref)
        queries = head_columns(q_ref[quarter].astype(F32) * SCALE, False)
        grads_in = head_columns(do_all[quarter].astype(F32), True)
        outs = []
        count = 2 * (quarter + 1)
        for head in range(GROUP_HEADS):
            rows = head_rows(kv_ref, quarter, head)
            query, grad = queries[head].astype(BF16), grads_in[head].astype(BF16)
            masked = jnp.where(allowed, dot_nt(query, rows), MASKED)
            probs = jnp.exp(masked - lse_ref[quarter * GROUP_HEADS + head])
            prob_grad = dot_nt(grad, rows)
            centre = jnp.sum(probs * prob_grad, -1, keepdims=True)
            score_grad = (probs * (prob_grad - centre)).astype(BF16)
            outs.append(dot(score_grad, rows) * SCALE)
            part = dot_tn(score_grad, query) + dot_tn(probs.astype(BF16), grad)
            part = part.reshape(count, TOKENS, PAIR)
            at = slice(head * PAIR, (head + 1) * PAIR)
            if quarter == GROUPS - 1:
                dkv_sum[0:count, :, at] = part
            else:
                dkv_sum[0:count, :, at] += part
        pair = jnp.where(low, outs[0], swapped(outs[1]))
        last_head = jnp.where(low, outs[2], 0.0)
        dqb[quarter] = jnp.concatenate([pair, last_head], 1).astype(BF16)
        links.push(dqb.at[quarter], dq_all.at[context], Q_AT + context, {"context": quarter}, quarter == context)
        for index in (2 * quarter, 2 * quarter + 1):
            dkvb[index] = dkv_sum[index].astype(BF16)
            links.push(
                dkvb.at[index], dkv_all.at[span], KV_AT + span,
                {"context": quarter, "tensor": index - 2 * quarter}, index == span,
            )
    dq_all[context] = dqb[context]
    dkv_all[span] = dkvb[span]
    for index in range(GROUPS):
        links.arrived(dq_all.at[index], Q_AT + index, index == context)
    joined = join_groups([dq_all[index].astype(F32) for index in range(GROUPS)])
    q2[own, :WIDTH] = joined.astype(BF16)
    for index in range(SPANS):
        links.arrived(dkv_all.at[index], KV_AT + index, index == span)
    for group in range(GROUPS):
        total = dkv_all[2 * group].astype(F32) + dkv_all[2 * group + 1].astype(F32)
        at = WIDTH + group * KV_GROUP
        q2[own, at : at + KV_GROUP] = total.astype(BF16)
    send_first(3)
    loads[3].wait()
    normed_grad = dot_nt(q2[own], wq[...])
    pulled, gain_early, bias_early = norm_pull(x_ref[...].astype(F32), norms_ref[0:1, :], normed_grad)
    dx_low = (resid_grad + pulled).astype(BF16)
    vec_here = vec0 if last else vec_out
    for index, vector in enumerate((gain_early, gain_late, bias_early, bias_late)):
        vec_here[index : index + 1, :] = vector
    vec_here[4:8, :] = jnp.zeros((4, WIDTH), F32)
    if last:
        dx[...] = dx_low
        vec_first = moved(vec0, vec_got, 2, out_sems)
        vec_second = moved(vec_ref, vec_got, 2, out_sems)

        @pl.when(section == 0)
        def _():
            kept_first[1].start()
            vec_second.start()

        @pl.when(section == 1)
        def _():
            for_first[1].start()
            vec_first.start()
    else:
        dx_out[...] = dx_low
    stage(riding)

    for fetch in own_fetches[:2]:
        fetch.wait()
    pl.when(section == 0)(own_fetches[2].wait)

    @pl.when(section == 0)
    def _():
        for copy in to_first:
            copy.wait_recv()
        product(n2, q2, 0)
        product(m2, l2, 3 * WIDTH)

    if not last:
        feed_products()

    if last:
        tail[0].stage()
        vec_first.wait_recv()
        vec8[shard] = jnp.where(section == 0, vec0[...], vec_ref[...]) + vec_got[...]
        sems = late_sems[4:6]
        sums = []

        def spread(buffer, me, ids, sources, base):
            for index, target in enumerate(ids):
                copy = pltpu.make_async_remote_copy(
                    src_ref=buffer.at[me],
                    dst_ref=buffer.at[me],
                    send_sem=sems[0].at[base + index],
                    recv_sem=sems[1].at[base + index],
                    device_id=target,
                    device_id_type=MESH,
                )
                copy.start()
                sums.append(copy)

        spread(vec8, shard, shard_ids, None, 0)
        stage(tail)
        stage(riding)
        stage(tail)
        for copy in sums[:7]:
            copy.wait_recv()
        vec64[span] = jnp.sum(vec8[...], 0)
        spread(vec64, span, span_ids, None, 7)
        stage(tail, 2)
        stage(riding)
        stage(tail, 5)
        stage(riding, 2)
        stage(tail, 16)
        for copy in sums[7:]:
            copy.wait_recv()
        vec_out[...] = jnp.sum(vec64[...], 0)

        @pl.when(section == 0)
        def _():
            mine_out[...] = tail[0].res[...]

        @pl.when(section == 1)
        def _():
            mine_out[...] = riding[1].res[...]

        for reduction in riding + tail:
            reduction.finish()
        for copy in sums:
            copy.wait_send()
        for_second[0].wait_recv()
        for_second[1].wait_recv()

        @pl.when(section == 0)
        def _():
            for copy in for_second + [vec_second]:
                copy.wait_send()

        @pl.when(section == 1)
        def _():
            for copy in for_first + [vec_first]:
                copy.wait_send()

        for copy in kept_first:
            copy.wait()

    @pl.when(section == 1)
    def _():
        for copy in to_first:
            copy.wait_send()

    @pl.when(section == 0)
    def _():
        for copy in to_second:
            copy.wait_send()

    links.finish()


def backward_block(last, args, weights, extra=()):
    outputs, scratch = (
        (
            shape((DEPTH, HALF)),
            shape((8, WIDTH), F32),
            shape((DEPTH, HALF)),
            shape((2, TOKENS, WIDTH)),
            shape((2, TOKENS, WIDTH)),
        ),
        [
            *[pltpu.VMEM(dims, BF16) for dims in RIDE_BUFFERS],
            *[pltpu.SemaphoreType.DMA((REDUCE_COPIES,))] * 2,
            pltpu.VMEM((SPANS, DEPTH, HALF), BF16),
            pltpu.VMEM((TOKENS, WIDTH), BF16),
            pltpu.VMEM((8, WIDTH), F32),
            pltpu.VMEM((8, WIDTH), F32),
            pltpu.VMEM((SPANS, 8, WIDTH), F32),
            pltpu.VMEM((SPANS, 8, WIDTH), F32),
            *[pltpu.VMEM(dims, BF16) for dims in TAIL_BUFFERS],
            *[pltpu.SemaphoreType.DMA((REDUCE_COPIES,))] * 2,
            *[pltpu.SemaphoreType.DMA((4,))] * 2,
            *[pltpu.SemaphoreType.DMA((14,))] * 2,
        ],
    ) if last else (
        (shape((TOKENS, WIDTH)), shape((SPANS, DEPTH, HALF)), shape((8, WIDTH), F32)),
        [],
    )
    out_specs = (VMEM, VMEM, ANY, ANY, ANY) if last else (VMEM,) * 3
    return call_remote(
        functools.partial(backward_body, last),
        outputs,
        20,
        9 if last else 8,
        (*args, *weights, *extra),
        scratch=[
            pltpu.VMEM((WIDTH, 3 * WIDTH), BF16),
            pltpu.VMEM((WIDTH, REST), BF16),
            pltpu.VMEM((TOKENS, WIDTH), BF16),
            pltpu.VMEM((TOKENS, WIDTH), BF16),
            *[pltpu.VMEM((GROUPS, TOKENS, 256), BF16)] * 4,
            pltpu.VMEM((SPANS, TOKENS, KV_GROUP), F32),
            pltpu.VMEM((SPANS, TOKENS, KV_GROUP), BF16),
            pltpu.VMEM((SPANS, TOKENS, KV_GROUP), BF16),
            pltpu.VMEM((2 * TOKENS, WIDTH), BF16),
            pltpu.VMEM((2 * TOKENS, 3 * WIDTH), BF16),
            pltpu.VMEM((2 * TOKENS, WIDTH), BF16),
            pltpu.VMEM((2 * TOKENS, WIDTH), BF16),
            pltpu.VMEM((4 * TOKENS, WIDTH), BF16),
            pltpu.VMEM((4 * TOKENS, UNITS), BF16),
            pltpu.VMEM((4 * TOKENS, WIDTH), BF16),
            pltpu.VMEM((4 * TOKENS, UNITS), BF16),
            *[pltpu.SemaphoreType.DMA((8,))] * 2,
            pltpu.VMEM((GROUPS, TOKENS, 256), BF16),
            pltpu.VMEM((SPANS, TOKENS, KV_GROUP), BF16),
            pltpu.VMEM((GROUPS * GROUP_HEADS, TOKENS, 1), F32),
            pltpu.VMEM((TOKENS, WIDTH), F32),
            pltpu.VMEM((2 * TOKENS, UNITS), F32),
            pltpu.VMEM((8, WIDTH), F32),
            *scratch,
        ],
        locals_=14,
        specs=([VMEM] * 2 + [ANY] * 8 + [VMEM] * 3 + [ANY] * 2 + [VMEM] * len(extra), out_specs),
        vmem=60 * 1024 * 1024,
    )


def per_device(
    block_input, cotangent, segment_ids, w_qkv, w_out, w_fc, w_proj, norm_gains, norm_biases
):
    section = lax.axis_index("section")
    tensor = lax.axis_index("tensor")
    tokens, width = block_input.shape[2:]
    units = w_fc.shape[2]
    depth = w_qkv.shape[1]
    heads = width // HEAD_DIM

    pairs = w_qkv[0][:, width:].reshape(depth, 2, heads, HEAD_DIM).transpose(0, 2, 1, 3)
    own_q = jnp.concatenate([w_qkv[0][:, :width], pairs.reshape(depth, 2 * width)], 1)
    own_r = jnp.concatenate([w_out[0], w_fc[0], w_proj[0].T], 1)
    vectors = jnp.concatenate([norm_gains[0], norm_biases[0]], 0)
    vectors = jnp.pad(vectors, ((0, 12), (0, 128 - depth)))
    first_q, second_q, vectors = gather_first(own_q, vectors)

    def mine(stacked):
        return lax.dynamic_index_in_dim(stacked, section, 0, keepdims=False)

    seg_keys = mine(segment_ids)
    seg_queries = lax.dynamic_index_in_dim(
        seg_keys.reshape(4, 2, tokens), tensor, 1, keepdims=False
    ).reshape(-1, 1)

    entry = mine(block_input)[0]
    first, kept_first, ops_first, rest_first = forward_block(
        0, entry, seg_keys, seg_queries, vectors, first_q, own_r
    )
    second, kept_second, ops_second, rest_second = forward_block(
        1, first, seg_keys, seg_queries, vectors, second_q, own_r
    )

    def arguments(block, incoming, kept, operands):
        return (incoming, *kept, *operands, seg_keys, seg_queries, vectors)

    def flat(*weights):
        return tuple(weight.reshape(width, -1) for weight in weights)

    grad_second, grads_second, vectors_second = backward_block(
        False, arguments(1, mine(cotangent)[0], kept_second, ops_second), flat(second_q, rest_second)
    )
    own_half, vector_grads, other_half, block_outputs, input_grads = backward_block(
        True,
        arguments(0, grad_second, kept_first, ops_first),
        flat(first_q, rest_first),
        (grads_second, vectors_second, first, second),
    )
    out_a = jnp.where(section == 0, own_half, other_half).astype(F32)
    out_b = jnp.where(section == 0, other_half, own_half).astype(F32)
    out_n = lax.dynamic_slice_in_dim(vector_grads, lax.axis_index("shard") * depth, depth, 1)
    pairs = out_a[:, width : 3 * width].reshape(depth, heads, 2, HEAD_DIM).transpose(0, 2, 1, 3)
    out_qkv = jnp.concatenate([out_a[:, :width], pairs.reshape(depth, 2 * width)], 1)
    return (
        block_outputs[None, :, None],
        input_grads[None, :, None],
        out_qkv[None],
        out_a[None, :, 3 * width :],
        out_b[None, :, :units],
        out_b[:, units:].T[None],
        out_n[None, :2],
        out_n[None, 2],
        out_n[None, 3],
    )


def solution(mesh):
    in_specs = (
        P(None, "shard", ("context", "tensor"), None),
        P(None, "shard", ("context", "tensor"), None),
        P(None, "shard", None),
        P("section", "shard", None),
        P("section", "shard", None),
        P("section", "shard", "tensor"),
        P("section", "tensor", "shard"),
        P("section", None, "shard"),
        P("section", None, "shard"),
    )
    out_specs = (
        P("section", None, "shard", ("context", "tensor"), None),
        P("section", None, "shard", ("context", "tensor"), None),
        P("section", "shard", None),
        P("section", "shard", None),
        P("section", "shard", "tensor"),
        P("section", "tensor", "shard"),
        P("section", None, "shard"),
        P("section", "shard"),
        P("section", "shard"),
    )
    return jax.shard_map(
        per_device, mesh=mesh, in_specs=in_specs, out_specs=out_specs, check_vma=False
    )
```
